128 devices in a mesh: seq: 16 (over x, y_hi, core), tp: 8 (over y_lo, z).
Axes of the slice: x: 4, y: 4 (y_hi: 2, y_lo: 2; y = y_hi * 2 + y_lo), z: 4, core: 2. Of those that a mesh axis runs over, the one named last changes fastest.
Arguments:
- hidden_in: bfloat16 [4096, 4096], P('seq'), may hold values from -16 to 16
- temporal_weight_stack: bfloat16 [4096, 4, 2048], P(None, None, 'tp'), may hold values from -0.5 to 0.5
- depth_in: bfloat16 [4096, 512], replicated, may hold values from -0.09375 to 0.09375
- depth_stack: bfloat16 [4096, 512], replicated, may hold values from -6 to 6
- audio_codes: int32 [4096, 8], P(('seq', 'tp')), may hold values from 0 to 1023
Outputs:
- grad_temporal: float32 [4096, 4, 2048], P('seq', None, 'tp')
- grad_win: float32 [4096, 512], P(('seq', 'tp'))
- grad_depth: float32 [4096, 512], P(('seq', 'tp'))
The draws below stay inside these ranges and needn't reach their ends.
All inputs are finite; a program needn't handle non-finite values.
Results may differ from the reference program's by a relative error of at most 0.033.
Values may be sent and summed in bfloat16 or wider, within the bound.
A program may use at most 192 MiB of HBM per device.

```python
import math
import jax
import jax.numpy as jnp
from jax import lax

D = 4096
HEADS = 16
HD = 128
DD = 512
DHD = 64
VOCAB = 1024
CB = 8
FR_DEV = 256
FRAMES = 4096
N_SEQ = 16


def draw_hidden_in(key, part):
    key = jax.random.fold_in(key, 11)
    keys = jax.random.split(key, 3)
    columns = jnp.exp(jax.random.uniform(keys[1], (1, D), jnp.float32, math.log(0.3), math.log(3.0)))
    row_scales = jnp.exp(jax.random.uniform(keys[2], (FRAMES, 1), jnp.float32, math.log(0.4), math.log(4.0)))
    values = jax.random.normal(keys[0], (FRAMES, D), jnp.float32) * columns * row_scales
    return jnp.clip(values, -16.0, 16.0).astype(jnp.bfloat16)


def draw_temporal_weight_stack(key, part):
    key = jax.random.fold_in(key, 23)
    keys = jax.random.split(key, 1)
    inner_all = HEADS * HD
    base = jax.random.normal(keys[0], (D, 4, inner_all), jnp.float32)
    scaling = jnp.array([1.0, 1.0, 1.0, 0.0], jnp.float32) / math.sqrt(D) + jnp.array([0.0, 0.0, 0.0, 0.1], jnp.float32)
    values = base * scaling[None, :, None]
    return jnp.clip(values, -0.5, 0.5).astype(jnp.bfloat16)


def draw_depth_stack(key, part):
    key = jax.random.fold_in(key, 37)
    keys = jax.random.split(key, 1)
    row_total = 4 * DD + 2 * VOCAB
    base = jax.random.normal(keys[0], (row_total, DD), jnp.float32)
    index_rows = jnp.arange(row_total)
    scaling = jnp.where(index_rows < 4 * DD, 1.0 / math.sqrt(DD), jnp.where(index_rows < 4 * DD + VOCAB, 3.0 / math.sqrt(DD), 1.0))
    values = base * scaling[:, None]
    return jnp.clip(values, -6.0, 6.0).astype(jnp.bfloat16)


def touch_ends(result, rng, low, top_value):
    index_at = [jax.random.randint(jax.random.fold_in(rng, axis), (), 0, length) for axis, length in enumerate(result.shape)]
    widest = result.shape.index(max(result.shape))
    beside = index_at[:widest] + [(index_at[widest] + 1) % result.shape[widest]] + index_at[widest + 1:]
    return result.at[tuple(index_at)].set(low).at[tuple(beside)].set(top_value)


def normal_values(stream_key, extent, scale, most, held_as=jnp.bfloat16):
    entries = jax.random.normal(stream_key, extent, jnp.float32) * scale
    return jnp.minimum(jnp.maximum(entries, -most), most).astype(held_as)


def setup_inputs(seed: int = 0) -> dict:
    seeds = jax.random.split(jax.random.key(seed), 6)
    hidden_in = draw_hidden_in(jax.random.fold_in(seeds[5], 71), 0)
    temporal_weight_stack = draw_temporal_weight_stack(jax.random.fold_in(seeds[5], 71), 0)
    depth_in = normal_values(seeds[2], (D, DD), D ** -0.5, 0.09375)
    depth_stack = draw_depth_stack(jax.random.fold_in(seeds[5], 71), 0)
    audio_codes = touch_ends(jax.random.randint(seeds[4], (FRAMES, CB), 0, VOCAB), jax.random.fold_in(seeds[4], 1), 0, VOCAB - 1).astype(jnp.int32)
    return dict(hidden_in=hidden_in, temporal_weight_stack=temporal_weight_stack, depth_in=depth_in, depth_stack=depth_stack, audio_codes=audio_codes)


EPSILON = 1e-05
MASKED = -1e+30
ROPE_BASE = 10000.0
FULL_PRECISION = lax.Precision.HIGHEST

def rms_scale(values):
    return lax.rsqrt(lax.optimization_barrier(jnp.mean(values * values, axis=-1, keepdims=True)) + EPSILON)

def norm_back(values, gradient):
    scaling = rms_scale(values)
    inner_mean = lax.optimization_barrier(jnp.mean(gradient * values, axis=-1, keepdims=True))
    return scaling * (gradient - values * (scaling * scaling) * inner_mean)

def rotate(values, positions, orientation):
    half_width = values.shape[-1] // 2
    frequency = ROPE_BASE ** (-jnp.arange(half_width).astype(jnp.float32) / half_width)
    angles = positions[:, None] * frequency[None, :]
    cosine = jnp.cos(angles)[:, None, :]
    sine = orientation * jnp.sin(angles)[:, None, :]
    lower_half = values[..., :half_width]
    upper_half = values[..., half_width:]
    return jnp.concatenate([lower_half * cosine - upper_half * sine, upper_half * cosine + lower_half * sine], axis=-1)

def masked_softmax(scores, allowed):
    scores = jnp.where(allowed, scores, MASKED)
    row_top = lax.optimization_barrier(jnp.max(scores, axis=-1, keepdims=True))
    weights = jnp.where(allowed, jnp.exp(scores - row_top), 0.0)
    return weights / lax.optimization_barrier(jnp.sum(weights, axis=-1, keepdims=True))

def softmax_back(probs, prob_grad):
    return probs * (prob_grad - lax.optimization_barrier(jnp.sum(probs * prob_grad, axis=-1, keepdims=True)))

def rounded_up(values):
    return lax.optimization_barrier(values.astype(jnp.bfloat16)).astype(jnp.float32)

def depth_pass(latent, depth_stack, audio_codes):
    frame_count, book_count = audio_codes.shape
    depth_width = latent.shape[1]
    head_count = depth_width // DHD
    token_count = frame_count * book_count
    qkv_rows = depth_stack[:3 * depth_width]
    out_rows = depth_stack[3 * depth_width:4 * depth_width]
    head_rows = depth_stack[4 * depth_width:4 * depth_width + VOCAB]
    embed_rows = depth_stack[4 * depth_width + VOCAB:]
    earlier = audio_codes[:, :-1]
    embedded = embed_rows[earlier].astype(jnp.float32)
    opening = jnp.zeros((frame_count, 1, depth_width), jnp.float32)
    stream = latent[:, None, :] + jnp.concatenate([opening, embedded], axis=1)
    stream_flat = stream.reshape(token_count, depth_width)
    stream_norm = (stream_flat * rms_scale(stream_flat)).astype(jnp.bfloat16)
    depth_proj = jnp.dot(stream_norm, qkv_rows.T, preferred_element_type=jnp.float32).astype(jnp.bfloat16)
    split_narrow = depth_proj.reshape(frame_count, book_count, 3, head_count, DHD)
    depth_split = split_narrow.astype(jnp.float32)
    queries = depth_split[:, :, 0]
    key_vals = depth_split[:, :, 1]
    value_vals = depth_split[:, :, 2]
    depth_scale = 1.0 / math.sqrt(DHD)
    causal = jnp.arange(book_count)[None, :] <= jnp.arange(book_count)[:, None]
    scores = jnp.einsum('fqhe,fkhe->fhqk', split_narrow[:, :, 0], split_narrow[:, :, 1], preferred_element_type=jnp.float32) * depth_scale
    depth_probs = masked_softmax(scores, causal)
    round_narrow = depth_probs.astype(jnp.bfloat16)
    depth_round = round_narrow.astype(jnp.float32)
    depth_mixed = jnp.einsum('fhqk,fkhe->fqhe', round_narrow, split_narrow[:, :, 2], preferred_element_type=jnp.float32)
    depth_mixed = depth_mixed.astype(jnp.bfloat16).reshape(token_count, depth_width)
    resid = stream_flat + jnp.dot(depth_mixed, out_rows.T, preferred_element_type=jnp.float32)
    resid_norm = (resid * rms_scale(resid)).astype(jnp.bfloat16)
    logits = jnp.dot(resid_norm, head_rows.T, preferred_element_type=jnp.float32)
    targets = audio_codes.reshape(token_count)
    target_hot = (targets[:, None] == jnp.arange(VOCAB)[None, :]).astype(jnp.float32)
    logit_probs = masked_softmax(logits, jnp.ones_like(logits, dtype=bool))
    loss_scale = 1.0 / math.sqrt(FRAMES * CB)
    logit_grad = ((logit_probs - target_hot) * loss_scale).astype(jnp.bfloat16)
    head_grad = jnp.dot(logit_grad.T, resid_norm, preferred_element_type=jnp.float32)
    resid_norm_grad = jnp.dot(logit_grad, head_rows, preferred_element_type=jnp.float32)
    resid_grad = norm_back(resid, resid_norm_grad)
    resid_round = resid_grad.astype(jnp.bfloat16)
    out_grad = jnp.dot(resid_round.T, depth_mixed, preferred_element_type=jnp.float32)
    mixed_grad = jnp.dot(resid_round, out_rows, preferred_element_type=jnp.float32)
    mixed_grad = mixed_grad.reshape(frame_count, book_count, head_count, DHD)
    value_grad = jnp.einsum('fhqk,fqhe->fkhe', depth_round, mixed_grad, precision=FULL_PRECISION)
    prob_grad = jnp.einsum('fqhe,fkhe->fhqk', mixed_grad, value_vals, precision=FULL_PRECISION)
    score_grad = softmax_back(depth_probs, prob_grad) * depth_scale
    query_grad = jnp.einsum('fhqk,fkhe->fqhe', score_grad, key_vals, precision=FULL_PRECISION)
    key_grad = jnp.einsum('fhqk,fqhe->fkhe', score_grad, queries, precision=FULL_PRECISION)
    proj_grad = jnp.stack([query_grad, key_grad, value_grad], axis=2)
    proj_grad = proj_grad.reshape(token_count, 3 * depth_width).astype(jnp.bfloat16)
    qkv_grad = jnp.dot(proj_grad.T, stream_norm, preferred_element_type=jnp.float32)
    stream_norm_grad = jnp.dot(proj_grad, qkv_rows, preferred_element_type=jnp.float32)
    stream_grad = resid_grad + norm_back(stream_flat, stream_norm_grad)
    stream_grid = stream_grad.reshape(frame_count, book_count, depth_width)
    embed_terms = rounded_up(stream_grid[:, 1:]).reshape(-1, depth_width)
    embed_grad = jax.ops.segment_sum(embed_terms, earlier.reshape(-1).astype(jnp.int32), num_segments=VOCAB)
    latent_grad = lax.optimization_barrier(jnp.sum(stream_grid, axis=1)).astype(jnp.bfloat16)
    grad_depth = jnp.concatenate([qkv_grad, out_grad, head_grad, embed_grad], axis=0)
    return (grad_depth, latent_grad)

def block_sum(left, right, frames):
    leftward_blocks = left.reshape(N_SEQ, FR_DEV, frames).astype(jnp.float32)
    rightward_blocks = right.reshape(N_SEQ, FR_DEV, right.shape[-1]).astype(jnp.float32)
    partial_results = jnp.einsum('ghi,ghl->gil', leftward_blocks, rightward_blocks, precision=FULL_PRECISION)
    return lax.optimization_barrier(jnp.sum(rounded_up(partial_results), axis=0))

def reference(hidden_in, temporal_weight_stack, depth_in, depth_stack, audio_codes):
    frames = hidden_in.shape[0]
    model_width = hidden_in.shape[1]
    inner_all = temporal_weight_stack.shape[2]
    head_count = inner_all // HD
    att_scale = 1.0 / math.sqrt(HD)
    hidden_full = hidden_in.astype(jnp.float32)
    rms_normalized = (hidden_full * rms_scale(hidden_full)).astype(jnp.bfloat16)
    projected = jnp.dot(rms_normalized, temporal_weight_stack[:, :3, :].reshape(model_width, 3 * inner_all), preferred_element_type=jnp.float32)
    projected = projected.reshape(frames, 3, inner_all)
    positions = jnp.arange(frames).astype(jnp.float32)
    query_rows = rotate(projected[:, 0].reshape(frames, head_count, HD), positions, 1.0).astype(jnp.bfloat16)
    key_rows = rotate(projected[:, 1].reshape(frames, head_count, HD), positions, 1.0).astype(jnp.bfloat16)
    value_rows = projected[:, 2].reshape(frames, head_count, HD).astype(jnp.bfloat16)
    allowed = jnp.arange(frames)[None, :] <= jnp.arange(frames)[:, None]
    by_head = (query_rows.transpose(1, 0, 2), key_rows.transpose(1, 0, 2), value_rows.transpose(1, 0, 2))

    def head_forward(operands):
        query_head, key_head, value_head = operands
        scores = jnp.dot(query_head, key_head.T, preferred_element_type=jnp.float32) * att_scale
        attn_round = masked_softmax(scores, allowed).astype(jnp.bfloat16)
        return jnp.dot(attn_round, value_head, preferred_element_type=jnp.float32).astype(jnp.bfloat16)
    attended = lax.map(head_forward, by_head).transpose(1, 0, 2).reshape(frames, inner_all)
    out_w = temporal_weight_stack[:, 3, :]
    branch = jnp.dot(attended, out_w.T, preferred_element_type=jnp.float32)
    merged = hidden_full + branch
    merged_norm = (merged * rms_scale(merged)).astype(jnp.bfloat16)
    latent = jnp.dot(merged_norm, depth_in, preferred_element_type=jnp.float32)
    grad_depth, latent_grad = depth_pass(latent, depth_stack, audio_codes)
    grad_win = jnp.dot(merged_norm.T, latent_grad, preferred_element_type=jnp.float32)
    merged_norm_grad = jnp.dot(latent_grad, depth_in.T, preferred_element_type=jnp.float32)
    merged_grad = norm_back(merged, merged_norm_grad).astype(jnp.bfloat16)
    attended_grad = jnp.dot(merged_grad, out_w, preferred_element_type=jnp.float32).astype(jnp.bfloat16)
    grad_heads = attended_grad.reshape(frames, head_count, HD).transpose(1, 0, 2)

    def head_backward(operands):
        query_head, key_head, value_head, grad_head = operands
        scores = jnp.dot(query_head, key_head.T, preferred_element_type=jnp.float32) * att_scale
        attn_probs = masked_softmax(scores, allowed)
        attn_round = attn_probs.astype(jnp.bfloat16)
        prob_temporal = jnp.dot(grad_head, value_head.T, preferred_element_type=jnp.float32)
        score_temporal = (softmax_back(attn_probs, prob_temporal) * att_scale).astype(jnp.bfloat16)
        query_temporal = jnp.dot(score_temporal, key_head, preferred_element_type=jnp.float32)
        key_temporal = block_sum(score_temporal, query_head, frames)
        value_temporal = block_sum(attn_round, grad_head, frames)
        return (query_temporal, key_temporal, value_temporal)
    query_back, key_back, value_back = lax.map(head_backward, by_head + (grad_heads,))
    query_back = rotate(query_back.transpose(1, 0, 2), positions, -1.0)
    key_back = rotate(key_back.transpose(1, 0, 2), positions, -1.0)
    value_back = value_back.transpose(1, 0, 2)
    temporal_projection = jnp.stack([query_back.reshape(frames, inner_all), key_back.reshape(frames, inner_all), value_back.reshape(frames, inner_all)], axis=1).astype(jnp.bfloat16)

    def block_grads(running, blocks):
        normed_block, proj_block, merged_block, attended_block = blocks
        term_in = jnp.dot(normed_block.T, proj_block.reshape(FR_DEV, 3 * inner_all), preferred_element_type=jnp.float32)
        term_out = jnp.dot(merged_block.T, attended_block, preferred_element_type=jnp.float32)
        term_all = jnp.concatenate([term_in.reshape(model_width, 3, inner_all), term_out[:, None, :]], axis=1)
        return (running + rounded_up(term_all), None)
    blocks = (rms_normalized.reshape(N_SEQ, FR_DEV, model_width), temporal_projection.reshape(N_SEQ, FR_DEV, 3, inner_all), merged_grad.reshape(N_SEQ, FR_DEV, model_width), attended.reshape(N_SEQ, FR_DEV, inner_all))
    grad_temporal, _ = lax.scan(block_grads, jnp.zeros((model_width, 4, inner_all), jnp.float32), blocks)
    return (grad_temporal, grad_win, grad_depth)
```

```python
import math

import jax
import jax.numpy as jnp
from jax import lax
from jax.sharding import PartitionSpec as P

HD = 128
DHD = 64
VOCAB = 1024


EPSILON = 1e-05
MASKED = -1e30
ROPE_BASE = 10000.0
FULL_PRECISION = lax.Precision.HIGHEST
CONTRACT_ROWS = (((0,), (0,)), ((), ()))
CONTRACT_COLS = (((1,), (1,)), ((), ()))


def rms_scale(values):
    return lax.rsqrt(jnp.mean(values * values, axis=-1, keepdims=True) + EPSILON)


def norm_back(values, gradient):
    scaling = rms_scale(values)
    inner_mean = jnp.mean(gradient * values, axis=-1, keepdims=True)
    return scaling * (gradient - values * (scaling * scaling) * inner_mean)


def rotate(values, positions, orientation):
    half_width = values.shape[-1] // 2
    frequency = ROPE_BASE ** (-jnp.arange(half_width).astype(jnp.float32) / half_width)
    angles = positions[:, None] * frequency[None, :]
    cosine = jnp.cos(angles)[:, None, :]
    sine = orientation * jnp.sin(angles)[:, None, :]
    lower_half = values[..., :half_width]
    upper_half = values[..., half_width:]
    return jnp.concatenate(
        [lower_half * cosine - upper_half * sine, upper_half * cosine + lower_half * sine], axis=-1
    )


def masked_softmax(scores, allowed):
    scores = jnp.where(allowed, scores, MASKED)
    row_top = jnp.max(scores, axis=-1, keepdims=True)
    weights = jnp.where(allowed, jnp.exp(scores - row_top), 0.0)
    return weights / jnp.sum(weights, axis=-1, keepdims=True)


def softmax_back(probs, prob_grad):
    return probs * (prob_grad - jnp.sum(probs * prob_grad, axis=-1, keepdims=True))


def frame_sum(term_all):
    return lax.psum_scatter(
        term_all.astype(jnp.bfloat16), "seq", scatter_dimension=0, tiled=True
    ).astype(jnp.float32)


def depth_pass(latent, depth_stack, audio_codes, loss_scale):
    frame_count, book_count = audio_codes.shape
    depth_width = latent.shape[1]
    head_count = depth_width // DHD
    token_count = frame_count * book_count
    qkv_rows = depth_stack[: 3 * depth_width]
    out_rows = depth_stack[3 * depth_width : 4 * depth_width]
    head_rows = depth_stack[4 * depth_width : 4 * depth_width + VOCAB]
    embed_rows = depth_stack[4 * depth_width + VOCAB :]
    earlier = audio_codes[:, :-1]
    one_hot = (earlier[:, :, None] == jnp.arange(VOCAB)[None, None, :]).astype(jnp.bfloat16)
    embedded = jnp.einsum("fkv,vd->fkd", one_hot, embed_rows, preferred_element_type=jnp.float32)
    opening = jnp.zeros((frame_count, 1, depth_width), jnp.float32)
    stream = latent[:, None, :] + jnp.concatenate([opening, embedded], axis=1)
    stream_flat = stream.reshape(token_count, depth_width)
    stream_norm = (stream_flat * rms_scale(stream_flat)).astype(jnp.bfloat16)
    depth_proj = lax.dot_general(
        stream_norm, qkv_rows, CONTRACT_COLS, preferred_element_type=jnp.float32
    ).astype(jnp.bfloat16)
    split_narrow = depth_proj.reshape(frame_count, book_count, 3, head_count, DHD)
    depth_split = split_narrow.astype(jnp.float32)
    queries = depth_split[:, :, 0]
    key_vals = depth_split[:, :, 1]
    value_vals = depth_split[:, :, 2]
    depth_scale = 1.0 / math.sqrt(DHD)
    causal = jnp.arange(book_count)[None, :] <= jnp.arange(book_count)[:, None]
    scores = (
        jnp.einsum(
            "fqhe,fkhe->fhqk",
            split_narrow[:, :, 0],
            split_narrow[:, :, 1],
            preferred_element_type=jnp.float32,
        )
        * depth_scale
    )
    depth_probs = masked_softmax(scores, causal)
    round_narrow = depth_probs.astype(jnp.bfloat16)
    depth_round = round_narrow.astype(jnp.float32)
    depth_mixed = jnp.einsum(
        "fhqk,fkhe->fqhe", round_narrow, split_narrow[:, :, 2], preferred_element_type=jnp.float32
    )
    depth_mixed = depth_mixed.astype(jnp.bfloat16).reshape(token_count, depth_width)
    resid = stream_flat + lax.dot_general(
        depth_mixed, out_rows, CONTRACT_COLS, preferred_element_type=jnp.float32
    )
    resid_norm = (resid * rms_scale(resid)).astype(jnp.bfloat16)
    logits = lax.dot_general(
        resid_norm, head_rows, CONTRACT_COLS, preferred_element_type=jnp.float32
    )
    targets = audio_codes.reshape(token_count)
    target_hot = (targets[:, None] == jnp.arange(VOCAB)[None, :]).astype(jnp.float32)
    logit_probs = masked_softmax(logits, jnp.ones_like(logits, dtype=bool))
    logit_grad = ((logit_probs - target_hot) * loss_scale).astype(jnp.bfloat16)
    head_grad = lax.dot_general(
        logit_grad, resid_norm, CONTRACT_ROWS, preferred_element_type=jnp.float32
    )
    resid_norm_grad = jnp.dot(logit_grad, head_rows, preferred_element_type=jnp.float32)
    resid_grad = norm_back(resid, resid_norm_grad)
    resid_round = resid_grad.astype(jnp.bfloat16)
    out_grad = lax.dot_general(
        resid_round, depth_mixed, CONTRACT_ROWS, preferred_element_type=jnp.float32
    )
    mixed_grad = jnp.dot(resid_round, out_rows, preferred_element_type=jnp.float32)
    mixed_grad = mixed_grad.reshape(frame_count, book_count, head_count, DHD)
    value_grad = jnp.einsum("fhqk,fqhe->fkhe", depth_round, mixed_grad, precision=FULL_PRECISION)
    prob_grad = jnp.einsum("fqhe,fkhe->fhqk", mixed_grad, value_vals, precision=FULL_PRECISION)
    score_grad = softmax_back(depth_probs, prob_grad) * depth_scale
    query_grad = jnp.einsum("fhqk,fkhe->fqhe", score_grad, key_vals, precision=FULL_PRECISION)
    key_grad = jnp.einsum("fhqk,fqhe->fkhe", score_grad, queries, precision=FULL_PRECISION)
    proj_grad = jnp.stack([query_grad, key_grad, value_grad], axis=2)
    proj_grad = proj_grad.reshape(token_count, 3 * depth_width).astype(jnp.bfloat16)
    qkv_grad = lax.dot_general(
        proj_grad, stream_norm, CONTRACT_ROWS, preferred_element_type=jnp.float32
    )
    stream_norm_grad = jnp.dot(proj_grad, qkv_rows, preferred_element_type=jnp.float32)
    stream_grad = resid_grad + norm_back(stream_flat, stream_norm_grad)
    stream_grid = stream_grad.reshape(frame_count, book_count, depth_width)
    embed_grad = jnp.einsum(
        "fkv,fkd->vd",
        one_hot,
        stream_grid[:, 1:].astype(jnp.bfloat16),
        preferred_element_type=jnp.float32,
    )
    latent_grad = jnp.sum(stream_grid, axis=1).astype(jnp.bfloat16)
    grad_depth = jnp.concatenate([qkv_grad, out_grad, head_grad, embed_grad], axis=0)
    return (grad_depth, latent_grad)


def per_device(hidden_in, temporal_weight_stack, depth_in, depth_stack, audio_codes):
    frames_dev = hidden_in.shape[0]
    inner_dev = temporal_weight_stack.shape[2]
    head_count = inner_dev // HD
    depth_frames = audio_codes.shape[0]
    book_count = audio_codes.shape[1]
    depth_width = depth_in.shape[1]
    seq_count = lax.axis_size("seq")
    tp_count = lax.axis_size("tp")
    device_count = seq_count * tp_count
    seq_index = lax.axis_index("seq")
    tp_index = lax.axis_index("tp")
    total_frames = frames_dev * seq_count
    att_scale = 1.0 / math.sqrt(HD)
    hidden_full = hidden_in.astype(jnp.float32)
    rms_normalized = (hidden_full * rms_scale(hidden_full)).astype(jnp.bfloat16)
    projected = jnp.einsum(
        "wo,obu->wbu",
        rms_normalized,
        temporal_weight_stack[:, :3, :],
        preferred_element_type=jnp.float32,
    )
    query_pos = seq_index * frames_dev + jnp.arange(frames_dev)
    positions = query_pos.astype(jnp.float32)
    query_rows = rotate(projected[:, 0].reshape(frames_dev, head_count, HD), positions, 1.0).astype(
        jnp.bfloat16
    )
    key_rows = rotate(projected[:, 1].reshape(frames_dev, head_count, HD), positions, 1.0).astype(
        jnp.bfloat16
    )
    value_rows = projected[:, 2].astype(jnp.bfloat16)
    local_pairs = jnp.stack([key_rows.reshape(frames_dev, inner_dev), value_rows], axis=1)
    all_pairs = lax.all_gather(local_pairs, "seq", axis=0, tiled=True)
    keys_all = all_pairs[:, 0].reshape(total_frames, head_count, HD)
    values_all = all_pairs[:, 1].reshape(total_frames, head_count, HD)
    allowed = (jnp.arange(total_frames)[None, :] <= query_pos[:, None])[None]
    scores = (
        jnp.einsum("qhe,khe->hqk", query_rows, keys_all, preferred_element_type=jnp.float32)
        * att_scale
    )
    attn_probs = masked_softmax(scores, allowed)
    attn_round = attn_probs.astype(jnp.bfloat16)
    attended = jnp.einsum(
        "hqk,khe->qhe", attn_round, values_all, preferred_element_type=jnp.float32
    )
    attended = attended.astype(jnp.bfloat16).reshape(frames_dev, inner_dev)
    out_w = temporal_weight_stack[:, 3, :]
    branch = lax.psum_scatter(
        lax.dot_general(attended, out_w, CONTRACT_COLS, preferred_element_type=jnp.float32).astype(
            jnp.bfloat16
        ),
        "tp",
        scatter_dimension=0,
        tiled=True,
    ).astype(jnp.float32)
    own_hidden = lax.dynamic_slice_in_dim(hidden_full, tp_index * depth_frames, depth_frames, 0)
    merged = own_hidden + branch
    merged_norm = (merged * rms_scale(merged)).astype(jnp.bfloat16)
    latent = jnp.dot(merged_norm, depth_in, preferred_element_type=jnp.float32)
    loss_scale = 1.0 / math.sqrt(total_frames * book_count)
    grad_depth, latent_grad = depth_pass(latent, depth_stack, audio_codes, loss_scale)
    grad_win = lax.dot_general(
        merged_norm, latent_grad, CONTRACT_ROWS, preferred_element_type=jnp.float32
    )
    blocks = jnp.concatenate(
        [
            grad_win.reshape(seq_count, tp_count, -1, depth_width),
            grad_depth.reshape(seq_count, tp_count, -1, depth_width),
        ],
        axis=2,
    ).astype(jnp.bfloat16)
    blocks = blocks.transpose(1, 0, 2, 3)
    share = lax.psum_scatter(blocks, "tp", scatter_dimension=0, tiled=True)[0]
    share = lax.psum_scatter(share, "seq", scatter_dimension=0, tiled=True)[0]
    share = share.astype(jnp.float32)
    depth_rows = depth_stack.shape[0] // device_count
    depth_share = share[share.shape[0] - depth_rows :]
    win_share = share[: share.shape[0] - depth_rows]
    merged_norm_grad = lax.dot_general(
        latent_grad, depth_in, CONTRACT_COLS, preferred_element_type=jnp.float32
    )
    merged_grad = norm_back(merged, merged_norm_grad).astype(jnp.bfloat16)
    shard_rows = lax.all_gather(merged_grad, "tp", axis=0, tiled=True)
    update = jnp.dot(shard_rows, out_w, preferred_element_type=jnp.float32)
    attended_grad = update
    out_w_grad = lax.dot_general(
        shard_rows, attended, CONTRACT_ROWS, preferred_element_type=jnp.float32
    )
    attended_grad, out_w_grad = (attended_grad, out_w_grad)
    attended_round = attended_grad.astype(jnp.bfloat16).reshape(frames_dev, head_count, HD)
    prob_temporal = jnp.einsum(
        "qhe,khe->hqk", attended_round, values_all, preferred_element_type=jnp.float32
    )
    score_temporal = (softmax_back(attn_probs, prob_temporal) * att_scale).astype(jnp.bfloat16)
    query_temporal = jnp.einsum(
        "hqk,khe->qhe", score_temporal, keys_all, preferred_element_type=jnp.float32
    )
    key_partial = jnp.einsum(
        "hqk,qhe->khe", score_temporal, query_rows, preferred_element_type=jnp.float32
    )
    value_partial = jnp.einsum(
        "hqk,qhe->khe", attn_round, attended_round, preferred_element_type=jnp.float32
    )
    key_term = jnp.stack(
        [
            key_partial.reshape(total_frames, inner_dev),
            value_partial.reshape(total_frames, inner_dev),
        ],
        axis=1,
    )
    key_share = frame_sum(key_term)
    query_back = rotate(query_temporal, positions, -1.0).reshape(frames_dev, inner_dev)
    key_back = rotate(key_share[:, 0].reshape(frames_dev, head_count, HD), positions, -1.0).reshape(
        frames_dev, inner_dev
    )
    temporal_projection = jnp.stack([query_back, key_back, key_share[:, 1]], axis=1).astype(
        jnp.bfloat16
    )
    incoming_gradient = jnp.einsum(
        "jn,jws->nws", rms_normalized, temporal_projection, preferred_element_type=jnp.float32
    )
    weight_term = jnp.concatenate([incoming_gradient, out_w_grad[:, None, :]], axis=1)
    weight_share = frame_sum(weight_term)
    return (weight_share, win_share, depth_share)


def solution(mesh):
    in_specs = (P("seq", None), P(None, None, "tp"), P(), P(), P(("seq", "tp"), None))
    out_specs = (P("seq", None, "tp"), P(("seq", "tp"), None), P(("seq", "tp"), None))
    return jax.shard_map(
        per_device, mesh=mesh, in_specs=in_specs, out_specs=out_specs, check_vma=False
    )
```

```python
import functools
import math

import jax
import jax.numpy as jnp
from jax import lax
from jax.experimental import pallas as pl
from jax.experimental.pallas import tpu as pltpu
from jax.sharding import PartitionSpec as P

HD = 128
DHD = 64
VOCAB = 1024
CHIPS = 8
TP = 8
FR = 256
FR2 = 512
DD = 512
NS = 512

EPSILON = 1e-05
MASKED = -1e30
ROPE_BASE = 10000.0
MIB = 2**20
MESH = pl.DeviceIdType.MESH
F32 = jnp.float32
BF16 = jnp.bfloat16
ANY = pl.BlockSpec(memory_space=pl.ANY)
VMEM = pl.BlockSpec(memory_space=pltpu.VMEM)
TP_ORDER = (4, 1, 3, 5, 7, 2, 6)
CHIP_ORDER = (2, 6, 1, 4, 3, 7, 5)


def dot_nn(left, right):
    return jnp.dot(left, right, preferred_element_type=F32)


def dot_nt(left, right):
    return lax.dot_general(left, right, (((1,), (1,)), ((), ())), preferred_element_type=F32)


def dot_tn(left, right):
    return lax.dot_general(left, right, (((0,), (0,)), ((), ())), preferred_element_type=F32)


def rms_scale(values):
    return lax.rsqrt(jnp.mean(values * values, axis=-1, keepdims=True) + EPSILON)


def norm_back(values, scaling, gradient):
    inner_mean = jnp.mean(gradient * values, axis=-1, keepdims=True)
    return scaling * (gradient - values * (scaling * scaling) * inner_mean)


def angle_tables(first, count):
    half_width = HD // 2
    frequency = ROPE_BASE ** (-jnp.arange(half_width).astype(F32) / half_width)
    positions = (first + jnp.arange(count)).astype(F32)
    angles = positions[:, None] * frequency[None, :]
    return jnp.cos(angles), jnp.sin(angles)


def rotate(values, cosine, sine):
    half_width = HD // 2
    lower_half = values[..., :half_width]
    upper_half = values[..., half_width:]
    cosine = cosine[:, None, :]
    sine = sine[:, None, :]
    return jnp.concatenate(
        [lower_half * cosine - upper_half * sine, upper_half * cosine + lower_half * sine], axis=-1
    )


def place():
    seq = lax.axis_index("seq")
    tp = lax.axis_index("tp")
    return seq, seq // 2, seq % 2, tp


def run_exchange(peers, jobs, locals_, send_sems, recv_sems):
    barrier = pltpu.get_barrier_semaphore()
    for peer in peers:
        pl.semaphore_signal(barrier, inc=1, device_id=peer, device_id_type=MESH)
    pl.semaphore_wait(barrier, len(peers))
    copies = []
    for number, (source, target, device) in enumerate(jobs):
        copy = pltpu.make_async_remote_copy(
            src_ref=source,
            dst_ref=target,
            send_sem=send_sems.at[number],
            recv_sem=recv_sems.at[number],
            device_id=device,
            device_id_type=MESH,
        )
        copy.start()
        copies.append(copy)
    for source, bounce, target, sem in locals_:
        copy = pltpu.make_async_copy(source, bounce, sem)
        copy.start()
        copy.wait()
        copy = pltpu.make_async_copy(bounce, target, sem)
        copy.start()
        copy.wait()
    for copy in copies:
        copy.wait()


def exchange(kernel, name, collective_id, ins, outs, copies, bounces):
    return pl.pallas_call(
        kernel,
        name=name,
        out_shape=outs,
        in_specs=[ANY] * len(ins),
        out_specs=[ANY] * len(outs),
        scratch_shapes=[
            pltpu.SemaphoreType.DMA((copies,)),
            pltpu.SemaphoreType.DMA((copies,)),
            pltpu.SemaphoreType.DMA,
        ]
        + [pltpu.VMEM(shape, dtype) for shape, dtype in bounces],
        compiler_params=pltpu.CompilerParams(
            collective_id=collective_id, has_side_effects=True, vmem_limit_bytes=16 * MIB
        ),
    )(*ins)


def tp_peers(seq, tp, order=TP_ORDER):
    return [(seq, lax.rem(tp + hop, TP)) for hop in order]


def chip_peers(chip, core, tp, order=CHIP_ORDER):
    return [(lax.rem(chip + hop, CHIPS) * 2 + core, tp) for hop in order]


def keys_kernel(
    kv, query, normed, out_w, kv_all, query_two, normed_other, w_all,
    send_sems, recv_sems, sem, kv_bounce, query_bounce, w_bounce,
):
    seq, chip, core, tp = place()
    partner = (chip * 2 + 1 - core, tp)
    peers = [partner]
    jobs = [(query.at[1 - core], query_two.at[core], partner)]
    jobs.append((kv.at[1 - core], kv_all.at[seq], partner))
    for other in chip_peers(chip, core, tp):
        peers.append(other)
        jobs.append((kv.at[core], kv_all.at[seq], other))
    for other in chip_peers(chip, 1 - core, tp):
        peers.append(other)
        jobs.append((kv.at[1 - core], kv_all.at[seq], other))
    for other in tp_peers(seq, tp):
        peers.append(other)
        jobs.append((out_w.at[other[1]], w_all.at[tp], other))
    jobs.append((normed, normed_other, partner))
    run_exchange(
        peers,
        jobs,
        [
            (kv.at[core], kv_bounce, kv_all.at[seq], sem),
            (query.at[core], query_bounce, query_two.at[core], sem),
            (out_w.at[tp], w_bounce, w_all.at[tp], sem),
        ],
        send_sems,
        recv_sems,
    )


def exchange_keys(kv, query, normed, out_w):
    return exchange(
        keys_kernel,
        "exchange_keys",
        1,
        (kv, query, normed, out_w),
        [
            jax.ShapeDtypeStruct((2 * CHIPS, FR, 2 * HD), BF16),
            jax.ShapeDtypeStruct((2, FR, HD), BF16),
            jax.ShapeDtypeStruct(normed.shape, BF16),
            jax.ShapeDtypeStruct(out_w.shape, BF16),
        ],
        24,
        [((FR, 2 * HD), BF16), ((FR, HD), BF16), (out_w.shape[1:], BF16)],
    )


def attended_kernel(source, target, send_sems, recv_sems, sem, bounce):
    seq, chip, core, tp = place()
    slot = tp * 2 + core
    partner_seq = chip * 2 + 1 - core
    peers = [(partner_seq, tp)] + tp_peers(seq, tp) + tp_peers(partner_seq, tp)
    own = pl.ds(core * FR, FR)
    other = pl.ds((1 - core) * FR, FR)
    rows = [other] + [own] * (TP - 1) + [other] * (TP - 1)
    jobs = [(source.at[part], target.at[slot], peer) for part, peer in zip(rows, peers)]
    run_exchange(
        peers, jobs, [(source.at[own], bounce, target.at[slot], sem)], send_sems, recv_sems
    )


def exchange_attended(attended):
    return exchange(
        attended_kernel,
        "exchange_attended",
        2,
        (attended,),
        [jax.ShapeDtypeStruct((2 * TP, FR, HD), BF16)],
        15,
        [((FR, HD), BF16)],
    )[0]


def scatter_kernel(source, target, send_sems, recv_sems, sem, bounce):
    seq, chip, core, tp = place()
    peers = tp_peers(seq, tp)
    jobs = [(source.at[peer[1]], target.at[tp], peer) for peer in peers]
    run_exchange(
        peers, jobs, [(source.at[tp], bounce, target.at[tp], sem)], send_sems, recv_sems
    )


def gather_kernel(source, target, send_sems, recv_sems, sem, bounce):
    seq, chip, core, tp = place()
    peers = tp_peers(seq, tp)
    jobs = [(source, target.at[tp], peer) for peer in peers]
    run_exchange(peers, jobs, [(source, bounce, target.at[tp], sem)], send_sems, recv_sems)


def exchange_latent(parts):
    return exchange(
        scatter_kernel,
        "exchange_latent",
        3,
        (parts,),
        [jax.ShapeDtypeStruct(parts.shape, parts.dtype)],
        7,
        [(parts.shape[1:], parts.dtype)],
    )[0]


def exchange_message(message):
    return exchange(
        gather_kernel,
        "exchange_message",
        4,
        (message,),
        [jax.ShapeDtypeStruct((TP,) + message.shape, message.dtype)],
        7,
        [(message.shape, message.dtype)],
    )[0]


def cotangent_kernel(source, target, send_sems, recv_sems, sem, bounce):
    seq, chip, core, tp = place()
    partner_seq = chip * 2 + 1 - core
    peers = [(partner_seq, tp)] + tp_peers(seq, tp) + tp_peers(partner_seq, tp)
    heads = [1 - core] + [core] * (TP - 1) + [1 - core] * (TP - 1)
    jobs = [
        (source.at[peer[1] * 2 + head], target.at[core, tp], peer)
        for head, peer in zip(heads, peers)
    ]
    run_exchange(
        peers,
        jobs,
        [(source.at[tp * 2 + core], bounce, target.at[core, tp], sem)],
        send_sems,
        recv_sems,
    )


def exchange_cotangent(parts):
    return exchange(
        cotangent_kernel,
        "exchange_cotangent",
        5,
        (parts,),
        [jax.ShapeDtypeStruct((2, TP, FR, HD), BF16)],
        15,
        [((FR, HD), BF16)],
    )[0]


def key_grads_kernel(source, target, send_sems, recv_sems, sem, bounce):
    seq, chip, core, tp = place()
    peers = chip_peers(chip, core, tp)
    jobs = [(source.at[peer[0] // 2], target.at[chip], peer) for peer in peers]
    run_exchange(
        peers, jobs, [(source.at[chip], bounce, target.at[chip], sem)], send_sems, recv_sems
    )


def exchange_key_grads(parts):
    return exchange(
        key_grads_kernel,
        "exchange_key_grads",
        6,
        (parts,),
        [jax.ShapeDtypeStruct(parts.shape, parts.dtype)],
        7,
        [(parts.shape[1:], parts.dtype)],
    )[0]


def weights_kernel(source, target, send_sems, recv_sems, sem, bounce):
    seq, chip, core, tp = place()
    partner = (chip * 2 + 1 - core, tp)
    peers = [partner] + chip_peers(chip, core, tp) + chip_peers(chip, 1 - core, tp)
    jobs = [(source.at[peer[0]], target.at[core, chip], peer) for peer in peers]
    run_exchange(
        peers, jobs, [(source.at[seq], bounce, target.at[core, chip], sem)], send_sems, recv_sems
    )


def exchange_weights(parts):
    return exchange(
        weights_kernel,
        "exchange_weights",
        7,
        (parts,),
        [jax.ShapeDtypeStruct((2, CHIPS) + parts.shape[1:], parts.dtype)],
        15,
        [(parts.shape[1:], parts.dtype)],
    )[0]


def compute(kernel, name, ins, outs, scratch=(), limit=48):
    return pl.pallas_call(
        kernel,
        name=name,
        out_shape=outs,
        in_specs=[VMEM] * len(ins),
        out_specs=[VMEM] * len(outs),
        scratch_shapes=list(scratch),
        compiler_params=pltpu.CompilerParams(vmem_limit_bytes=limit * MIB),
    )(*ins)


def attend_kernel(kv_ref, query_ref, out_ref, prob_ref, out_t_ref, inverse_ref, score_ref):
    chip = lax.axis_index("seq") // 2
    blocks = 2 * chip + 2
    query = query_ref[...].reshape(FR2, HD)
    key_at = lax.broadcasted_iota(jnp.int32, (FR, FR2), 0)
    query_at = lax.broadcasted_iota(jnp.int32, (FR, FR2), 1) + chip * FR2

    def scores(block, top):
        score = dot_nt(kv_ref[block][:, :HD], query) * (1.0 / math.sqrt(HD))
        score = jnp.where(key_at + block * FR <= query_at, score, MASKED)
        score_ref[block] = score
        return jnp.maximum(top, jnp.max(score, axis=0, keepdims=True))

    top = lax.fori_loop(0, blocks, scores, jnp.full((1, FR2), MASKED, F32))

    def weigh(block, carry):
        total, mixed = carry
        prob = jnp.exp(score_ref[block] - top)
        total = total + jnp.sum(prob, axis=0, keepdims=True)
        prob = prob.astype(BF16)
        prob_ref[block] = prob
        return total, mixed + dot_tn(kv_ref[block][:, HD:], prob)

    total, mixed = lax.fori_loop(
        0, blocks, weigh, (jnp.zeros((1, FR2), F32), jnp.zeros((HD, FR2), F32))
    )
    inverse = 1.0 / total
    mixed = mixed * inverse
    out_t_ref[...] = mixed
    inverse_ref[...] = inverse
    out_ref[...] = mixed.T.astype(BF16)


def attend(kv_all, query_two):
    return compute(
        attend_kernel,
        "attend",
        (kv_all, query_two),
        [
            jax.ShapeDtypeStruct((FR2, HD), BF16),
            jax.ShapeDtypeStruct((2 * CHIPS, FR, FR2), BF16),
            jax.ShapeDtypeStruct((HD, FR2), F32),
            jax.ShapeDtypeStruct((1, FR2), F32),
        ],
        [pltpu.VMEM((2 * CHIPS, FR, FR2), F32)],
    )


def merge_kernel(att_ref, w_ref, hidden_ref, depth_in_ref, merged_ref, part_ref):
    merged = hidden_ref[...].astype(F32)
    for tp in range(TP):
        pair = jnp.concatenate([att_ref[2 * tp], att_ref[2 * tp + 1]], axis=1)
        merged = merged + dot_nt(pair, w_ref[tp])
    merged_ref[...] = merged
    squares = jnp.sum(merged * merged, axis=-1, keepdims=True)
    latent = dot_nn(merged.astype(BF16), depth_in_ref[...])
    part_ref[:, :, :DD] = latent.reshape(TP, FR // TP, DD)
    part_ref[:, :, DD:] = jnp.broadcast_to(squares, (FR, HD)).reshape(TP, FR // TP, HD)


def merge(att_all, w_all, hidden_slice, depth_in_slice):
    return compute(
        merge_kernel,
        "merge",
        (att_all, w_all, hidden_slice, depth_in_slice),
        [
            jax.ShapeDtypeStruct((FR, NS), F32),
            jax.ShapeDtypeStruct((TP, FR // TP, DD + HD), F32),
        ],
    )


def depth_kernel(width, loss_scale, part_ref, stack_ref, before_ref, code_ref, message_ref, grad_ref, prob_ref):
    frames = part_ref.shape[1]
    books = before_ref.shape[0] // frames
    tokens = frames * books
    qkv_rows = stack_ref[: 3 * DD]
    out_rows = stack_ref[3 * DD : 4 * DD]
    head_rows = stack_ref[4 * DD : 4 * DD + VOCAB]
    embed_rows = stack_ref[4 * DD + VOCAB :]
    total = jnp.sum(part_ref[...], axis=0)
    raw = total[:, :DD]
    scale_in = lax.rsqrt(total[:, DD : DD + 1] * (1.0 / width) + EPSILON)
    latent = raw * scale_in
    latent = jnp.broadcast_to(latent[:, None, :], (frames, books, DD)).reshape(tokens, DD)
    vocab_at = lax.broadcasted_iota(jnp.int32, (tokens, VOCAB), 1)
    hot = jnp.where(before_ref[...] == vocab_at, 1.0, 0.0).astype(BF16)
    stream = latent + dot_nn(hot, embed_rows)
    stream_scale = rms_scale(stream)
    stream_norm = (stream * stream_scale).astype(BF16)
    proj = dot_nt(stream_norm, qkv_rows).astype(BF16)
    row_at = lax.broadcasted_iota(jnp.int32, (tokens, tokens), 0)
    col_at = lax.broadcasted_iota(jnp.int32, (tokens, tokens), 1)
    allowed = (row_at // books == col_at // books) & (col_at <= row_at)
    depth_scale = 1.0 / math.sqrt(DHD)
    mixed = []
    for head in range(DD // DHD):
        low = head * DHD
        queries = proj[:, low : low + DHD]
        keys = proj[:, DD + low : DD + low + DHD]
        values = proj[:, 2 * DD + low : 2 * DD + low + DHD]
        scores = jnp.where(allowed, dot_nt(queries, keys) * depth_scale, MASKED)
        weights = jnp.exp(scores - jnp.max(scores, axis=-1, keepdims=True))
        probs = weights / jnp.sum(weights, axis=-1, keepdims=True)
        prob_ref[head] = probs
        mixed.append(dot_nn(probs.astype(BF16), values))
    mixed = jnp.concatenate(mixed, axis=1).astype(BF16)
    resid = stream + dot_nt(mixed, out_rows)
    resid_scale = rms_scale(resid)
    resid_norm = (resid * resid_scale).astype(BF16)
    logits = dot_nt(resid_norm, head_rows)
    weights = jnp.exp(logits - jnp.max(logits, axis=-1, keepdims=True))
    logit_probs = weights / jnp.sum(weights, axis=-1, keepdims=True)
    target = jnp.where(code_ref[...] == vocab_at, 1.0, 0.0)
    logit_grad = ((logit_probs - target) * loss_scale).astype(BF16)
    grad_ref[4 * DD : 4 * DD + VOCAB] = dot_tn(logit_grad, resid_norm).astype(BF16)
    resid_grad = norm_back(resid, resid_scale, dot_nn(logit_grad, head_rows))
    resid_round = resid_grad.astype(BF16)
    grad_ref[3 * DD : 4 * DD] = dot_tn(resid_round, mixed).astype(BF16)
    mixed_grad = dot_nn(resid_round, out_rows).astype(BF16)
    query_grad, key_grad, value_grad = [], [], []
    for head in range(DD // DHD):
        low = head * DHD
        queries = proj[:, low : low + DHD]
        keys = proj[:, DD + low : DD + low + DHD]
        values = proj[:, 2 * DD + low : 2 * DD + low + DHD]
        probs = prob_ref[head]
        mix_grad = mixed_grad[:, low : low + DHD]
        value_grad.append(dot_tn(probs.astype(BF16), mix_grad))
        prob_grad = dot_nt(mix_grad, values)
        inner = jnp.sum(probs * prob_grad, axis=-1, keepdims=True)
        score_grad = (probs * (prob_grad - inner) * depth_scale).astype(BF16)
        query_grad.append(dot_nn(score_grad, keys))
        key_grad.append(dot_tn(score_grad, queries))
    proj_grad = jnp.concatenate(query_grad + key_grad + value_grad, axis=1).astype(BF16)
    grad_ref[: 3 * DD] = dot_tn(proj_grad, stream_norm).astype(BF16)
    stream_grad = resid_grad + norm_back(stream, stream_scale, dot_nn(proj_grad, qkv_rows))
    grad_ref[4 * DD + VOCAB :] = dot_tn(hot, stream_grad.astype(BF16)).astype(BF16)
    latent_grad = jnp.sum(stream_grad.reshape(frames, books, DD), axis=1)
    latent_grad = latent_grad.astype(BF16).astype(F32)
    inner = jnp.sum(latent_grad * raw, axis=-1, keepdims=True) * (1.0 / width)
    pull = scale_in * scale_in * scale_in * inner
    coarse = pull.astype(BF16)
    fine = (pull - coarse.astype(F32)).astype(BF16)
    message_ref[:, :DD] = (latent_grad * scale_in).astype(BF16)
    message_ref[:, DD : DD + HD] = jnp.broadcast_to(coarse, (frames, HD))
    message_ref[:, DD + HD :] = jnp.broadcast_to(fine, (frames, HD))


def depth(parts, stack, before, codes, width, loss_scale):
    tokens = before.shape[0]
    return compute(
        functools.partial(depth_kernel, width, loss_scale),
        "depth",
        (parts, stack, before, codes),
        [
            jax.ShapeDtypeStruct((parts.shape[1], DD + 2 * HD), BF16),
            jax.ShapeDtypeStruct(stack.shape, BF16),
        ],
        [pltpu.VMEM((DD // DHD, tokens, tokens), F32)],
    )


def unmerge_kernel(message_ref, merged_ref, depth_in_ref, w_ref, merged_grad_ref, part_ref):
    message = message_ref[...].reshape(FR, DD + 2 * HD)
    pull = message[:, DD : DD + 1].astype(F32) + message[:, DD + HD : DD + HD + 1].astype(F32)
    gradient = dot_nt(message[:, :DD], depth_in_ref[...]) - merged_ref[...] * pull
    gradient = gradient.astype(BF16)
    merged_grad_ref[...] = gradient
    for tp in range(TP):
        pair = dot_nn(gradient, w_ref[tp]).astype(BF16)
        part_ref[2 * tp] = pair[:, :HD]
        part_ref[2 * tp + 1] = pair[:, HD:]


def unmerge(messages, merged, depth_in_slice, w_all):
    return compute(
        unmerge_kernel,
        "unmerge",
        (messages, merged, depth_in_slice, w_all),
        [
            jax.ShapeDtypeStruct((FR, NS), BF16),
            jax.ShapeDtypeStruct((2 * TP, FR, HD), BF16),
        ],
    )


def side_kernel(messages_ref, merged_ref, merged_grad_ref, att_ref, win_ref, out_ref):
    message = messages_ref[...].reshape(FR, DD + 2 * HD)
    win_ref[...] = dot_tn(merged_ref[...].astype(BF16), message[:, :DD]).astype(BF16)
    gradient = merged_grad_ref[...]
    for tp in range(TP):
        pair = jnp.concatenate([att_ref[2 * tp], att_ref[2 * tp + 1]], axis=1)
        out_ref[:, tp] = dot_tn(gradient, pair).astype(BF16)


def side_grads(messages, merged, merged_grad, att_all):
    return compute(
        side_kernel,
        "side_grads",
        (messages, merged, merged_grad, att_all),
        [
            jax.ShapeDtypeStruct((NS, DD), BF16),
            jax.ShapeDtypeStruct((NS, TP, 2 * HD), BF16),
        ],
    )


def attend_back_kernel(
    prob_ref, kv_ref, query_ref, part_ref, out_t_ref, inverse_ref, cos_ref, sin_ref, grad_ref, query_grad_ref
):
    chip = lax.axis_index("seq") // 2
    blocks = 2 * chip + 2
    grad_ref[...] = jnp.zeros_like(grad_ref)
    query = query_ref[...].reshape(FR2, HD)
    gradient = jnp.sum(part_ref[...].astype(F32), axis=1).reshape(FR2, HD)
    gradient = gradient.astype(BF16).astype(F32)
    gradient_t = (gradient.T * inverse_ref[...]).astype(BF16)
    wide_t = gradient_t.astype(F32)
    inner = jnp.sum(wide_t * out_t_ref[...], axis=0, keepdims=True)
    gradient = wide_t.T.astype(BF16)
    scale = 1.0 / math.sqrt(HD)

    def step(block, query_grad):
        prob = prob_ref[block]
        score_grad = prob.astype(F32) * (dot_nn(kv_ref[block, :, HD:], gradient_t) - inner)
        score_grad = score_grad.astype(BF16)
        grad_ref[block, :, :HD] = (dot_nn(score_grad, query) * scale).astype(BF16)
        grad_ref[block, :, HD:] = dot_nn(prob, gradient).astype(BF16)
        return query_grad + dot_tn(kv_ref[block, :, :HD], score_grad)

    query_grad = lax.fori_loop(0, blocks, step, jnp.zeros((HD, FR2), F32)) * scale

    query_grad = query_grad.T
    lower, upper = query_grad[:, : HD // 2], query_grad[:, HD // 2 :]
    cosine, sine = cos_ref[...], sin_ref[...]
    query_grad_ref[...] = jnp.concatenate(
        [lower * cosine + upper * sine, upper * cosine - lower * sine], axis=1
    ).astype(BF16)


def attend_back(probs, kv_all, query_two, parts, out_t, inverse, cosine, sine):
    return compute(
        attend_back_kernel,
        "attend_back",
        (probs, kv_all, query_two, parts, out_t, inverse, cosine, sine),
        [
            jax.ShapeDtypeStruct((2 * CHIPS, FR, 2 * HD), BF16),
            jax.ShapeDtypeStruct((FR2, HD), BF16),
        ],
    )


def weight_kernel(part_ref, query_grad_ref, cos_ref, sin_ref, normed_ref, other_ref, out_ref):
    core = lax.axis_index("seq") % 2
    total = jnp.sum(part_ref[...].astype(F32), axis=0)
    lower, upper = total[:, : HD // 2], total[:, HD // 2 : HD]
    cosine, sine = cos_ref[...], sin_ref[...]
    proj = jnp.concatenate(
        [
            query_grad_ref[...].astype(F32),
            lower * cosine + upper * sine,
            upper * cosine - lower * sine,
            total[:, HD:],
        ],
        axis=1,
    )
    proj_t = proj.T
    first, second = proj_t[:, :FR], proj_t[:, FR:]
    own = jnp.where(core == 0, first, second).astype(BF16)
    other = jnp.where(core == 0, second, first).astype(BF16)
    for piece in range(2 * CHIPS):
        low = piece * FR
        term = dot_nn(own, normed_ref[:, low : low + FR])
        term = term + dot_nn(other, other_ref[:, low : low + FR])
        out_ref[piece] = term.astype(BF16)


def weight_terms(parts, query_grad, cosine, sine, normed, normed_other):
    return compute(
        weight_kernel,
        "weight_terms",
        (parts, query_grad, cosine, sine, normed, normed_other),
        [jax.ShapeDtypeStruct((2 * CHIPS, 3 * HD, FR), BF16)],
    )[0]


def weight_sum_kernel(part_ref, out_ref):
    for head in range(2):
        total = jnp.sum(part_ref[head].astype(F32), axis=0).T
        for kind in range(3):
            out_ref[kind, :, head * HD : (head + 1) * HD] = total[:, kind * HD : (kind + 1) * HD]


def weight_sum(parts):
    return compute(
        weight_sum_kernel,
        "weight_sum",
        (parts,),
        [jax.ShapeDtypeStruct((3, FR, 2 * HD), F32)],
    )[0]


def per_device(hidden_in, temporal_weight_stack, depth_in, depth_stack, audio_codes):
    seq_index = lax.axis_index("seq")
    tp_index = lax.axis_index("tp")
    chip = seq_index // 2
    width = hidden_in.shape[1]
    depth_frames, book_count = audio_codes.shape
    seq_count = 2 * CHIPS
    total_frames = FR * seq_count
    loss_scale = 1.0 / math.sqrt(total_frames * book_count)

    hidden_full = hidden_in.astype(F32)
    normed = (hidden_full * rms_scale(hidden_full)).astype(BF16)
    projected = jnp.einsum(
        "wo,obu->wbu", normed, temporal_weight_stack[:, :3, :], preferred_element_type=F32
    )
    cosine, sine = angle_tables(seq_index * FR, FR)
    query = rotate(projected[:, 0].reshape(FR, 2, HD), cosine, sine).astype(BF16)
    key = rotate(projected[:, 1].reshape(FR, 2, HD), cosine, sine).astype(BF16)
    value = projected[:, 2].reshape(FR, 2, HD).astype(BF16)
    kv = jnp.concatenate([key, value], axis=-1).transpose(1, 0, 2)
    query = query.transpose(1, 0, 2)
    out_w = temporal_weight_stack[:, 3, :].reshape(seq_count, TP, -1, 2 * HD)
    out_w = out_w.transpose(1, 0, 2, 3).reshape(TP, NS, 2 * HD)
    kv_all, query_two, normed_other, w_all = exchange_keys(kv, query, normed, out_w)

    hidden_slice = lax.dynamic_index_in_dim(
        hidden_in.reshape(FR, seq_count, TP, -1), tp_index, 2, keepdims=False
    ).reshape(FR, NS)
    depth_in_slice = lax.dynamic_index_in_dim(
        depth_in.reshape(seq_count, TP, -1, DD), tp_index, 1, keepdims=False
    ).reshape(NS, DD)
    attended, probs, out_t, inverse = attend(kv_all, query_two)
    att_all = exchange_attended(attended)
    merged, latent_parts = merge(att_all, w_all, hidden_slice, depth_in_slice)
    latent_parts = exchange_latent(latent_parts)
    before = jnp.concatenate(
        [jnp.full((depth_frames, 1), -1, jnp.int32), audio_codes[:, :-1]], axis=1
    ).reshape(-1, 1)
    message, grad_depth = depth(
        latent_parts, depth_stack, before, audio_codes.reshape(-1, 1), width, loss_scale
    )
    messages = exchange_message(message)
    merged_grad, cotangent_parts = unmerge(messages, merged, depth_in_slice, w_all)
    cotangent_parts = exchange_cotangent(cotangent_parts)

    grad_depth = grad_depth.reshape(seq_count, TP, -1, DD).transpose(1, 0, 2, 3)
    grad_depth = lax.psum_scatter(grad_depth, "tp", scatter_dimension=0, tiled=True)[0]
    grad_depth = lax.psum_scatter(grad_depth, "seq", scatter_dimension=0, tiled=True)[0]
    grad_win, grad_out = side_grads(messages, merged, merged_grad, att_all)
    grad_win = lax.psum_scatter(grad_win, "seq", scatter_dimension=0, tiled=True)
    grad_out = lax.psum_scatter(grad_out, "seq", scatter_dimension=0, tiled=True)
    grad_out = lax.all_to_all(grad_out, "tp", 1, 0, tiled=True).reshape(FR, 1, 2 * HD)

    cosine, sine = angle_tables(chip * FR2, FR2)
    key_parts, query_grad = attend_back(
        probs, kv_all, query_two, cotangent_parts, out_t, inverse, cosine, sine
    )
    key_parts = exchange_key_grads(key_parts.reshape(CHIPS, FR2, 2 * HD))
    parts = weight_terms(key_parts, query_grad, cosine, sine, normed, normed_other)
    grad_in = weight_sum(exchange_weights(parts))
    grad_temporal = jnp.concatenate([grad_in.transpose(1, 0, 2), grad_out.astype(F32)], axis=1)
    return grad_temporal, grad_win.astype(F32), grad_depth.astype(F32)


def solution(mesh):
    in_specs = (P("seq", None), P(None, None, "tp"), P(), P(), P(("seq", "tp"), None))
    out_specs = (P("seq", None, "tp"), P(("seq", "tp"), None), P(("seq", "tp"), None))
    return jax.shard_map(
        per_device, mesh=mesh, in_specs=in_specs, out_specs=out_specs, check_vma=False
    )
```

```python
import functools
import math

import jax
import jax.numpy as jnp
from jax import lax
from jax.experimental import pallas as pl
from jax.experimental.pallas import tpu as pltpu
from jax.sharding import PartitionSpec as P

HD = 128
DHD = 64
VOCAB = 1024
CHIPS = 8
TP = 8
FR = 256
FR2 = 512
DD = 512
NS = 512

EPSILON = 1e-05
MASKED = -1e30
ROPE_BASE = 10000.0
MIB = 2**20
MESH = pl.DeviceIdType.MESH
F32 = jnp.float32
BF16 = jnp.bfloat16
ANY = pl.BlockSpec(memory_space=pl.ANY)
VMEM = pl.BlockSpec(memory_space=pltpu.VMEM)
TP_ORDER = (4, 1, 3, 5, 7, 2, 6)
CHIP_ORDER = (2, 6, 1, 4, 3, 7, 5)


def dot_nn(left, right):
    return jnp.dot(left, right, preferred_element_type=F32)


def dot_nt(left, right):
    return lax.dot_general(left, right, (((1,), (1,)), ((), ())), preferred_element_type=F32)


def dot_tn(left, right):
    return lax.dot_general(left, right, (((0,), (0,)), ((), ())), preferred_element_type=F32)


def rms_scale(values):
    return lax.rsqrt(jnp.mean(values * values, axis=-1, keepdims=True) + EPSILON)


def norm_back(values, scaling, gradient):
    inner_mean = jnp.mean(gradient * values, axis=-1, keepdims=True)
    return scaling * (gradient - values * (scaling * scaling) * inner_mean)


def angle_tables(first, count):
    half_width = HD // 2
    frequency = ROPE_BASE ** (-jnp.arange(half_width).astype(F32) / half_width)
    positions = (first + jnp.arange(count)).astype(F32)
    angles = positions[:, None] * frequency[None, :]
    return jnp.cos(angles), jnp.sin(angles)


def rotate(values, cosine, sine):
    half_width = HD // 2
    lower_half = values[..., :half_width]
    upper_half = values[..., half_width:]
    cosine = cosine[:, None, :]
    sine = sine[:, None, :]
    return jnp.concatenate(
        [lower_half * cosine - upper_half * sine, upper_half * cosine + lower_half * sine], axis=-1
    )


def place():
    seq = lax.axis_index("seq")
    tp = lax.axis_index("tp")
    return seq, seq // 2, seq % 2, tp


def run_exchange(peers, jobs, locals_, send_sems, recv_sems):
    barrier = pltpu.get_barrier_semaphore()
    for peer in peers:
        pl.semaphore_signal(barrier, inc=1, device_id=peer, device_id_type=MESH)
    pl.semaphore_wait(barrier, len(peers))
    copies = []
    for number, (source, target, device, *when) in enumerate(jobs):
        copy = pltpu.make_async_remote_copy(
            src_ref=source,
            dst_ref=target,
            send_sem=send_sems.at[number],
            recv_sem=recv_sems.at[number],
            device_id=device,
            device_id_type=MESH,
        )
        if when:
            pl.when(when[0])(copy.start)
        else:
            copy.start()
        copies.append((copy, when))
    for source, bounce, target, sem in locals_:
        copy = pltpu.make_async_copy(source, bounce, sem)
        copy.start()
        copy.wait()
        copy = pltpu.make_async_copy(bounce, target, sem)
        copy.start()
        copy.wait()
    for copy, when in copies:
        if when:
            pl.when(when[0])(copy.wait_send)
            pl.when(when[1])(copy.wait_recv)
        else:
            copy.wait()


def exchange(kernel, name, collective_id, ins, outs, copies, bounces):
    return pl.pallas_call(
        kernel,
        name=name,
        out_shape=outs,
        in_specs=[ANY] * len(ins),
        out_specs=[ANY] * len(outs),
        scratch_shapes=[
            pltpu.SemaphoreType.DMA((copies,)),
            pltpu.SemaphoreType.DMA((copies,)),
            pltpu.SemaphoreType.DMA,
        ]
        + [pltpu.VMEM(shape, dtype) for shape, dtype in bounces],
        compiler_params=pltpu.CompilerParams(
            collective_id=collective_id, has_side_effects=True, vmem_limit_bytes=16 * MIB
        ),
    )(*ins)


def tp_peers(seq, tp, order=TP_ORDER):
    return [(seq, lax.rem(tp + hop, TP)) for hop in order]


def chip_peers(chip, core, tp, order=CHIP_ORDER):
    return [(lax.rem(chip + hop, CHIPS) * 2 + core, tp) for hop in order]


def keys_kernel(
    kv, query, out_w, kv_all, query_two, w_half, send_sems, recv_sems, sem, kv_bounce, query_bounce, w_bounce
):
    seq, chip, core, tp = place()
    partner = (chip * 2 + 1 - core, tp)
    half = pl.ds(core * FR, FR)
    peers = [partner]
    jobs = []
    for hop in CHIP_ORDER:
        there = lax.rem(chip + hop, CHIPS)
        later = there > chip
        earlier = lax.rem(chip - hop + CHIPS, CHIPS) < chip
        for head in (core, 1 - core):
            other = (there * 2 + head, tp)
            peers.append(other)
            jobs.append((kv.at[head], kv_all.at[seq], other, later, earlier))
    for other in tp_peers(seq, tp):
        peers.append(other)
        jobs.append((out_w.at[other[1], half], w_half.at[tp], other))
    jobs.append((query.at[1 - core], query_two.at[core], partner))
    jobs.append((kv.at[1 - core], kv_all.at[seq], partner))
    run_exchange(
        peers,
        jobs,
        [
            (kv.at[core], kv_bounce, kv_all.at[seq], sem),
            (query.at[core], query_bounce, query_two.at[core], sem),
            (out_w.at[tp, half], w_bounce, w_half.at[tp], sem),
        ],
        send_sems,
        recv_sems,
    )


def exchange_keys(kv, query, out_w):
    return exchange(
        keys_kernel,
        "exchange_keys",
        1,
        (kv, query, out_w),
        [
            jax.ShapeDtypeStruct((2 * CHIPS, FR, 2 * HD), BF16),
            jax.ShapeDtypeStruct((2, FR, HD), BF16),
            jax.ShapeDtypeStruct((TP, FR, 2 * HD), BF16),
        ],
        23,
        [((FR, 2 * HD), BF16), ((FR, HD), BF16), ((FR, 2 * HD), BF16)],
    )


def attended_kernel(
    source, w_half, normed, target, w_other, normed_other, send_sems, recv_sems, sem, bounce
):
    seq, chip, core, tp = place()
    slot = tp * 2 + core
    partner_seq = chip * 2 + 1 - core
    partner = (partner_seq, tp)
    peers = [partner] + tp_peers(seq, tp) + tp_peers(partner_seq, tp)
    own = pl.ds(core * FR, FR)
    other = pl.ds((1 - core) * FR, FR)
    rows = [other] + [own] * (TP - 1) + [other] * (TP - 1)
    jobs = [(source.at[part], target.at[slot], peer) for part, peer in zip(rows, peers)]
    jobs.append((w_half, w_other, partner))
    jobs.append((normed, normed_other, partner))
    run_exchange(
        peers, jobs, [(source.at[own], bounce, target.at[slot], sem)], send_sems, recv_sems
    )


def exchange_attended(attended, w_half, normed):
    return exchange(
        attended_kernel,
        "exchange_attended",
        2,
        (attended, w_half, normed),
        [
            jax.ShapeDtypeStruct((2 * TP, FR, HD), BF16),
            jax.ShapeDtypeStruct(w_half.shape, BF16),
            jax.ShapeDtypeStruct(normed.shape, BF16),
        ],
        17,
        [((FR, HD), BF16)],
    )


def latent_kernel(
    source, att_all, merged, target, att_other, merged_other, send_sems, recv_sems, sem, bounce
):
    seq, chip, core, tp = place()
    partner = (chip * 2 + 1 - core, tp)
    peers = tp_peers(seq, tp)
    jobs = [(source.at[peer[1]], target.at[tp], peer) for peer in peers]
    jobs.append((att_all, att_other, partner))
    jobs.append((merged, merged_other, partner))
    run_exchange(
        peers + [partner],
        jobs,
        [(source.at[tp], bounce, target.at[tp], sem)],
        send_sems,
        recv_sems,
    )


def exchange_latent(parts, att_all, merged):
    return exchange(
        latent_kernel,
        "exchange_latent",
        3,
        (parts, att_all, merged),
        [
            jax.ShapeDtypeStruct(parts.shape, parts.dtype),
            jax.ShapeDtypeStruct(att_all.shape, BF16),
            jax.ShapeDtypeStruct(merged.shape, BF16),
        ],
        9,
        [(parts.shape[1:], parts.dtype)],
    )


def message_kernel(source, grads, target, grads_other, send_sems, recv_sems, sem, bounce):
    seq, chip, core, tp = place()
    partner_seq = chip * 2 + 1 - core
    peers = tp_peers(seq, tp) + tp_peers(partner_seq, tp) + [(partner_seq, tp)]
    jobs = [(source, target.at[core, tp], peer) for peer in peers]
    jobs.append((grads.at[:, 1 - core], grads_other, peers[-1]))
    run_exchange(peers, jobs, [(source, bounce, target.at[core, tp], sem)], send_sems, recv_sems)


def exchange_message(message, grads):
    return exchange(
        message_kernel,
        "exchange_message",
        4,
        (message, grads),
        [
            jax.ShapeDtypeStruct((2, TP) + message.shape, message.dtype),
            jax.ShapeDtypeStruct((CHIPS, TP) + grads.shape[3:], BF16),
        ],
        16,
        [(message.shape, message.dtype)],
    )


def cotangent_kernel(
    source, side, target, side_all, send_sems, recv_sems, sem, bounce, side_bounce
):
    seq, chip, core, tp = place()
    partner_seq = chip * 2 + 1 - core
    peers = [(partner_seq, tp)] + tp_peers(seq, tp) + tp_peers(partner_seq, tp)
    heads = [1 - core] + [core] * (TP - 1) + [1 - core] * (TP - 1)
    jobs = [
        (source.at[peer[1] * 2 + head], target.at[core, tp], peer)
        for head, peer in zip(heads, peers)
    ]
    for other in chip_peers(chip, core, tp):
        peers.append(other)
        jobs.append((side.at[other[0] // 2], side_all.at[chip], other))
    run_exchange(
        peers,
        jobs,
        [
            (source.at[tp * 2 + core], bounce, target.at[core, tp], sem),
            (side.at[chip], side_bounce, side_all.at[chip], sem),
        ],
        send_sems,
        recv_sems,
    )


def exchange_cotangent(parts, side):
    return exchange(
        cotangent_kernel,
        "exchange_cotangent",
        5,
        (parts, side),
        [
            jax.ShapeDtypeStruct((2, TP, FR, HD), BF16),
            jax.ShapeDtypeStruct(side.shape, BF16),
        ],
        22,
        [((FR, HD), BF16), (side.shape[1:], BF16)],
    )


def key_grads_kernel(source, grads, target, grads_z, send_sems, recv_sems, sem, bounce, grads_bounce):
    seq, chip, core, tp = place()
    row, depth_at = tp // 4, tp % 4
    peers = []
    jobs = []
    for hop in CHIP_ORDER:
        there = lax.rem(chip + hop, CHIPS)
        here = lax.rem(chip - hop + CHIPS, CHIPS)
        other = (there * 2 + core, tp)
        peers.append(other)
        jobs.append((source.at[there], target.at[chip], other, there < chip, here > chip))
    for hop in (1, 3, 2):
        there = lax.rem(depth_at + hop, 4)
        other = (seq, row * 4 + there)
        peers.append(other)
        jobs.append((grads.at[:, :, there], grads_z.at[depth_at], other))
    run_exchange(
        peers,
        jobs,
        [
            (source.at[chip], bounce, target.at[chip], sem),
            (grads.at[:, :, depth_at], grads_bounce, grads_z.at[depth_at], sem),
        ],
        send_sems,
        recv_sems,
    )


def exchange_key_grads(parts, grads):
    slab = (CHIPS, 2) + grads.shape[3:]
    return exchange(
        key_grads_kernel,
        "exchange_key_grads",
        6,
        (parts, grads),
        [
            jax.ShapeDtypeStruct(parts.shape, parts.dtype),
            jax.ShapeDtypeStruct((4,) + slab, BF16),
        ],
        10,
        [(parts.shape[1:], parts.dtype), (slab, BF16)],
    )


def weights_kernel(
    source, grads, out, target, grads_all, out_all, send_sems, recv_sems, sem, bounce, grads_bounce, out_bounce
):
    seq, chip, core, tp = place()
    row, depth_at = tp // 4, tp % 4
    partner = (chip * 2 + 1 - core, tp)
    peers = [partner] + chip_peers(chip, core, tp) + chip_peers(chip, 1 - core, tp)
    jobs = [(source.at[peer[0]], target.at[core, chip], peer) for peer in peers]
    for hop in CHIP_ORDER:
        there = lax.rem(chip + hop, CHIPS)
        jobs.append((grads.at[there, row], grads_all.at[chip, row], (there * 2 + core, tp)))
    across = (1 - row) * 4 + depth_at
    for hop in (0,) + CHIP_ORDER:
        there = lax.rem(chip + hop, CHIPS)
        other = (there * 2 + core, across)
        if hop:
            peers.append(other)
        jobs.append((grads.at[there, 1 - row], grads_all.at[chip, row], other))
    for other in tp_peers(seq, tp):
        peers.append(other)
        jobs.append((out.at[other[1]], out_all.at[tp], other))
    run_exchange(
        peers,
        jobs,
        [
            (source.at[seq], bounce, target.at[core, chip], sem),
            (grads.at[chip, row], grads_bounce, grads_all.at[chip, row], sem),
            (out.at[tp], out_bounce, out_all.at[tp], sem),
        ],
        send_sems,
        recv_sems,
    )


def exchange_weights(parts, grads, out):
    return exchange(
        weights_kernel,
        "exchange_weights",
        7,
        (parts, grads, out),
        [
            jax.ShapeDtypeStruct((2, CHIPS) + parts.shape[1:], parts.dtype),
            jax.ShapeDtypeStruct(grads.shape, BF16),
            jax.ShapeDtypeStruct(out.shape, BF16),
        ],
        37,
        [(parts.shape[1:], BF16), (grads.shape[2:], BF16), (out.shape[1:], BF16)],
    )


def compute(kernel, name, ins, outs, scratch=(), limit=48, hbm=0):
    return pl.pallas_call(
        kernel,
        name=name,
        out_shape=outs,
        in_specs=[VMEM] * (len(ins) - hbm) + [ANY] * hbm,
        out_specs=[VMEM] * len(outs),
        scratch_shapes=list(scratch),
        compiler_params=pltpu.CompilerParams(vmem_limit_bytes=limit * MIB),
    )(*ins)


def attend_kernel(kv_ref, query_ref, out_ref, prob_ref, out_t_ref, inverse_ref, score_ref):
    chip = lax.axis_index("seq") // 2
    blocks = 2 * chip + 2
    query = query_ref[...].reshape(FR2, HD)
    key_at = lax.broadcasted_iota(jnp.int32, (FR, FR2), 0)
    query_at = lax.broadcasted_iota(jnp.int32, (FR, FR2), 1) + chip * FR2

    def scores(block, top):
        score = dot_nt(kv_ref[block][:, :HD], query) * (1.0 / math.sqrt(HD))
        score = jnp.where(key_at + block * FR <= query_at, score, MASKED)
        score_ref[block] = score
        return jnp.maximum(top, jnp.max(score, axis=0, keepdims=True))

    top = lax.fori_loop(0, blocks, scores, jnp.full((1, FR2), MASKED, F32))

    def weigh(block, carry):
        total, mixed = carry
        prob = jnp.exp(score_ref[block] - top)
        total = total + jnp.sum(prob, axis=0, keepdims=True)
        prob = prob.astype(BF16)
        prob_ref[block] = prob
        return total, mixed + dot_tn(kv_ref[block][:, HD:], prob)

    total, mixed = lax.fori_loop(
        0, blocks, weigh, (jnp.zeros((1, FR2), F32), jnp.zeros((HD, FR2), F32))
    )
    inverse = 1.0 / total
    mixed = mixed * inverse
    out_t_ref[...] = mixed
    inverse_ref[...] = inverse
    out_ref[...] = mixed.T.astype(BF16)


def attend(kv_all, query_two):
    return compute(
        attend_kernel,
        "attend",
        (kv_all, query_two),
        [
            jax.ShapeDtypeStruct((FR2, HD), BF16),
            jax.ShapeDtypeStruct((2 * CHIPS, FR, FR2), BF16),
            jax.ShapeDtypeStruct((HD, FR2), F32),
            jax.ShapeDtypeStruct((1, FR2), F32),
        ],
        [pltpu.VMEM((2 * CHIPS, FR, FR2), F32)],
    )


def fetch(source, target, sem):
    copy = pltpu.make_async_copy(source, target, sem)
    copy.start()
    return copy


def order_halves(core, mine, other):
    return jnp.where(core == 0, mine, other), jnp.where(core == 0, other, mine)


def merge_kernel(
    att_ref, half_ref, other_ref, hidden_ref, depth_in_hbm, merged_ref, round_ref, part_ref, depth_in_ref, sem
):
    seq, chip, core, tp = place()
    copy = fetch(depth_in_hbm.at[:, tp], depth_in_ref, sem)
    width = hidden_ref.shape[1]
    group = width // 2
    row_at = lax.broadcasted_iota(jnp.int32, (group, FR), 0)
    col_at = lax.broadcasted_iota(jnp.int32, (group, FR), 1)
    wanted = (col_at // 32) * 256 + tp * 32 + col_at % 32
    pick = jnp.where(row_at == wanted, 1.0, 0.0).astype(BF16)
    merged = jnp.concatenate(
        [dot_nn(hidden_ref[:, :group], pick), dot_nn(hidden_ref[:, group:], pick)], axis=1
    )
    mine = jnp.zeros((FR, FR), F32)
    other = jnp.zeros((FR, FR), F32)
    for at in range(TP):
        pair = jnp.concatenate([att_ref[2 * at], att_ref[2 * at + 1]], axis=1)
        mine = mine + dot_nt(pair, half_ref[at])
        other = other + dot_nt(pair, other_ref[at])
    merged = merged + jnp.concatenate(order_halves(core, mine, other), axis=1)
    rounded = merged.astype(BF16)
    merged_ref[...] = merged
    round_ref[...] = rounded
    squares = jnp.sum(merged * merged, axis=-1, keepdims=True)
    copy.wait()
    latent = dot_nn(rounded, depth_in_ref[...].reshape(NS, DD))
    part_ref[:, :, :DD] = latent.reshape(TP, FR // TP, DD)
    part_ref[:, :, DD:] = jnp.broadcast_to(squares, (FR, HD)).reshape(TP, FR // TP, HD)


def merge(att_all, w_half, w_other, hidden, depth_in):
    return compute(
        merge_kernel,
        "merge",
        (att_all, w_half, w_other, hidden, depth_in),
        [
            jax.ShapeDtypeStruct((FR, NS), F32),
            jax.ShapeDtypeStruct((FR, NS), BF16),
            jax.ShapeDtypeStruct((TP, FR // TP, DD + HD), F32),
        ],
        [pltpu.VMEM((2 * CHIPS, 32, DD), BF16), pltpu.SemaphoreType.DMA],
        hbm=1,
    )


def depth_kernel(width, loss_scale, part_ref, stack_ref, before_ref, code_ref, message_ref, grad_ref, prob_ref):
    frames = part_ref.shape[1]
    books = before_ref.shape[0] // frames
    tokens = frames * books
    qkv_rows = stack_ref[: 3 * DD]
    out_rows = stack_ref[3 * DD : 4 * DD]
    head_rows = stack_ref[4 * DD : 4 * DD + VOCAB]
    embed_rows = stack_ref[4 * DD + VOCAB :]
    total = jnp.sum(part_ref[...], axis=0)
    raw = total[:, :DD]
    scale_in = lax.rsqrt(total[:, DD : DD + 1] * (1.0 / width) + EPSILON)
    latent = raw * scale_in
    latent = jnp.broadcast_to(latent[:, None, :], (frames, books, DD)).reshape(tokens, DD)
    vocab_at = lax.broadcasted_iota(jnp.int32, (tokens, VOCAB), 1)
    hot = jnp.where(before_ref[...] == vocab_at, 1.0, 0.0).astype(BF16)
    stream = latent + dot_nn(hot, embed_rows)
    stream_scale = rms_scale(stream)
    stream_norm = (stream * stream_scale).astype(BF16)
    proj = dot_nt(stream_norm, qkv_rows).astype(BF16)
    row_at = lax.broadcasted_iota(jnp.int32, (tokens, tokens), 0)
    col_at = lax.broadcasted_iota(jnp.int32, (tokens, tokens), 1)
    allowed = (row_at // books == col_at // books) & (col_at <= row_at)
    depth_scale = 1.0 / math.sqrt(DHD)
    mixed = []
    for head in range(DD // DHD):
        low = head * DHD
        queries = proj[:, low : low + DHD]
        keys = proj[:, DD + low : DD + low + DHD]
        values = proj[:, 2 * DD + low : 2 * DD + low + DHD]
        scores = jnp.where(allowed, dot_nt(queries, keys) * depth_scale, MASKED)
        weights = jnp.exp(scores - jnp.max(scores, axis=-1, keepdims=True))
        probs = weights / jnp.sum(weights, axis=-1, keepdims=True)
        prob_ref[head] = probs
        mixed.append(dot_nn(probs.astype(BF16), values))
    mixed = jnp.concatenate(mixed, axis=1).astype(BF16)
    resid = stream + dot_nt(mixed, out_rows)
    resid_scale = rms_scale(resid)
    resid_norm = (resid * resid_scale).astype(BF16)
    logits = dot_nt(resid_norm, head_rows)
    weights = jnp.exp(logits - jnp.max(logits, axis=-1, keepdims=True))
    logit_probs = weights / jnp.sum(weights, axis=-1, keepdims=True)
    target = jnp.where(code_ref[...] == vocab_at, 1.0, 0.0)
    logit_grad = ((logit_probs - target) * loss_scale).astype(BF16)
    grad_ref[4 * DD : 4 * DD + VOCAB] = dot_tn(logit_grad, resid_norm).astype(BF16)
    resid_grad = norm_back(resid, resid_scale, dot_nn(logit_grad, head_rows))
    resid_round = resid_grad.astype(BF16)
    grad_ref[3 * DD : 4 * DD] = dot_tn(resid_round, mixed).astype(BF16)
    mixed_grad = dot_nn(resid_round, out_rows).astype(BF16)
    query_grad, key_grad, value_grad = [], [], []
    for head in range(DD // DHD):
        low = head * DHD
        queries = proj[:, low : low + DHD]
        keys = proj[:, DD + low : DD + low + DHD]
        values = proj[:, 2 * DD + low : 2 * DD + low + DHD]
        probs = prob_ref[head]
        mix_grad = mixed_grad[:, low : low + DHD]
        value_grad.append(dot_tn(probs.astype(BF16), mix_grad))
        prob_grad = dot_nt(mix_grad, values)
        inner = jnp.sum(probs * prob_grad, axis=-1, keepdims=True)
        score_grad = (probs * (prob_grad - inner) * depth_scale).astype(BF16)
        query_grad.append(dot_nn(score_grad, keys))
        key_grad.append(dot_tn(score_grad, queries))
    proj_grad = jnp.concatenate(query_grad + key_grad + value_grad, axis=1).astype(BF16)
    grad_ref[: 3 * DD] = dot_tn(proj_grad, stream_norm).astype(BF16)
    stream_grad = resid_grad + norm_back(stream, stream_scale, dot_nn(proj_grad, qkv_rows))
    grad_ref[4 * DD + VOCAB :] = dot_tn(hot, stream_grad.astype(BF16)).astype(BF16)
    latent_grad = jnp.sum(stream_grad.reshape(frames, books, DD), axis=1)
    latent_grad = latent_grad.astype(BF16).astype(F32)
    inner = jnp.sum(latent_grad * raw, axis=-1, keepdims=True) * (1.0 / width)
    pull = scale_in * scale_in * scale_in * inner
    coarse = pull.astype(BF16)
    fine = (pull - coarse.astype(F32)).astype(BF16)
    message_ref[:, :DD] = (latent_grad * scale_in).astype(BF16)
    message_ref[:, DD : DD + HD] = jnp.broadcast_to(coarse, (frames, HD))
    message_ref[:, DD + HD :] = jnp.broadcast_to(fine, (frames, HD))


def depth(parts, stack, before, codes, width, loss_scale):
    tokens = before.shape[0]
    return compute(
        functools.partial(depth_kernel, width, loss_scale),
        "depth",
        (parts, stack, before, codes),
        [
            jax.ShapeDtypeStruct((parts.shape[1], DD + 2 * HD), BF16),
            jax.ShapeDtypeStruct(stack.shape, BF16),
        ],
        [pltpu.VMEM((DD // DHD, tokens, tokens), F32)],
    )


def merged_gradient(message, merged, depth_in):
    pull = message[:, DD : DD + 1].astype(F32) + message[:, DD + HD : DD + HD + 1].astype(F32)
    return dot_nt(message[:, :DD], depth_in) - merged * pull


def unmerge_kernel(
    message_ref,
    merged_ref,
    round_ref,
    round_other_ref,
    att_ref,
    att_other_ref,
    half_ref,
    other_ref,
    grads_other_ref,
    grads_hbm,
    depth_in_hbm,
    part_ref,
    side_ref,
    grads_ref,
    depth_in_ref,
    grads_own_ref,
    sems,
):
    seq, chip, core, tp = place()
    copy = fetch(depth_in_hbm.at[:, tp], depth_in_ref, sems.at[0])
    grads_copy = fetch(grads_hbm.at[:, core], grads_own_ref, sems.at[1])
    copy.wait()
    depth_in = depth_in_ref[...].reshape(NS, DD)
    message = message_ref[core].reshape(FR, DD + 2 * HD)
    message_other = message_ref[1 - core].reshape(FR, DD + 2 * HD)
    gradient = merged_gradient(message, merged_ref[...], depth_in)
    lower, upper = gradient[:, :FR], gradient[:, FR:]
    mine, other = order_halves(core, lower, upper)
    mine, other = mine.astype(BF16), other.astype(BF16)
    for at in range(TP):
        pair = (dot_nn(mine, half_ref[at]) + dot_nn(other, other_ref[at])).astype(BF16)
        part_ref[2 * at] = pair[:, :HD]
        part_ref[2 * at + 1] = pair[:, HD:]
    gradient_other = merged_gradient(
        message_other, round_other_ref[...].astype(F32), depth_in
    )

    def pick_rows(own, others):
        both = jnp.concatenate([own.T, others.T], axis=1).reshape(CHIPS, 2, 32, FR2)
        both = jnp.where(core == 0, both[:, 0], both[:, 1])
        return both.reshape(FR, FR2).astype(BF16)

    rows = pick_rows(gradient, gradient_other)
    for at in range(TP):
        pair = jnp.concatenate([att_ref[2 * at], att_ref[2 * at + 1]], axis=1)
        pair_other = jnp.concatenate([att_other_ref[2 * at], att_other_ref[2 * at + 1]], axis=1)
        term = dot_nn(rows, jnp.concatenate([pair, pair_other], axis=0)).astype(BF16)
        side_ref[:, :, at * FR : (at + 1) * FR] = term.reshape(CHIPS, 32, FR)
    rows = pick_rows(round_ref[...].astype(F32), round_other_ref[...].astype(F32))
    both = jnp.concatenate([message[:, :DD], message_other[:, :DD]], axis=0)
    side_ref[:, :, TP * FR :] = dot_nn(rows, both).astype(BF16).reshape(CHIPS, 32, DD)
    grads_copy.wait()
    for at in range(CHIPS):
        grads_ref[at] = (
            grads_own_ref[at].astype(F32) + grads_other_ref[at].astype(F32)
        ).astype(BF16)


def unmerge(
    messages, merged, rounded, rounded_other, att_all, att_other, w_half, w_other, grads_other, grads, depth_in
):
    return compute(
        unmerge_kernel,
        "unmerge",
        (
            messages,
            merged,
            rounded,
            rounded_other,
            att_all,
            att_other,
            w_half,
            w_other,
            grads_other,
            grads,
            depth_in,
        ),
        [
            jax.ShapeDtypeStruct((2 * TP, FR, HD), BF16),
            jax.ShapeDtypeStruct((CHIPS, 32, TP * FR + DD), BF16),
            jax.ShapeDtypeStruct(grads_other.shape, BF16),
        ],
        [
            pltpu.VMEM((2 * CHIPS, 32, DD), BF16),
            pltpu.VMEM(grads_other.shape, BF16),
            pltpu.SemaphoreType.DMA((2,)),
        ],
        hbm=2,
    )


def attend_back_kernel(
    prob_ref, kv_ref, query_ref, part_ref, out_t_ref, inverse_ref, cos_ref, sin_ref, grad_ref, query_grad_ref
):
    chip = lax.axis_index("seq") // 2
    blocks = 2 * chip + 2
    query = query_ref[...].reshape(FR2, HD)
    gradient = jnp.sum(part_ref[...].astype(F32), axis=1).reshape(FR2, HD)
    gradient = gradient.astype(BF16).astype(F32)
    gradient_t = (gradient.T * inverse_ref[...]).astype(BF16)
    wide_t = gradient_t.astype(F32)
    inner = jnp.sum(wide_t * out_t_ref[...], axis=0, keepdims=True)
    gradient = wide_t.T.astype(BF16)
    scale = 1.0 / math.sqrt(HD)

    def step(block, query_grad):
        prob = prob_ref[block]
        score_grad = prob.astype(F32) * (dot_nn(kv_ref[block, :, HD:], gradient_t) - inner)
        score_grad = score_grad.astype(BF16)
        grad_ref[block, :, :HD] = (dot_nn(score_grad, query) * scale).astype(BF16)
        grad_ref[block, :, HD:] = dot_nn(prob, gradient).astype(BF16)
        return query_grad + dot_tn(kv_ref[block, :, :HD], score_grad)

    query_grad = lax.fori_loop(0, blocks, step, jnp.zeros((HD, FR2), F32)) * scale

    query_grad = query_grad.T
    lower, upper = query_grad[:, : HD // 2], query_grad[:, HD // 2 :]
    cosine, sine = cos_ref[...], sin_ref[...]
    query_grad_ref[...] = jnp.concatenate(
        [lower * cosine + upper * sine, upper * cosine - lower * sine], axis=1
    ).astype(BF16)


def attend_back(probs, kv_all, query_two, parts, out_t, inverse, cosine, sine):
    return compute(
        attend_back_kernel,
        "attend_back",
        (probs, kv_all, query_two, parts, out_t, inverse, cosine, sine),
        [
            jax.ShapeDtypeStruct((2 * CHIPS, FR, 2 * HD), BF16),
            jax.ShapeDtypeStruct((FR2, HD), BF16),
        ],
    )


def weight_kernel(
    part_ref, query_grad_ref, cos_ref, sin_ref, normed_ref, other_ref, grads_z_ref, side_ref,
    out_ref, grads_ref, win_ref, out_w_ref,
):
    chip = lax.axis_index("seq") // 2
    core = lax.axis_index("seq") % 2
    total = lax.fori_loop(
        chip,
        CHIPS,
        lambda at, carry: carry + part_ref[at].astype(F32),
        jnp.zeros((FR2, 2 * HD), F32),
    )
    lower, upper = total[:, : HD // 2], total[:, HD // 2 : HD]
    cosine, sine = cos_ref[...], sin_ref[...]
    proj = jnp.concatenate(
        [
            query_grad_ref[...].astype(F32),
            lower * cosine + upper * sine,
            upper * cosine - lower * sine,
            total[:, HD:],
        ],
        axis=1,
    )
    proj_t = proj.T
    own, other = order_halves(core, proj_t[:, :FR], proj_t[:, FR:])
    own, other = own.astype(BF16), other.astype(BF16)
    for piece in range(2 * CHIPS):
        low = piece * FR
        term = dot_nn(own, normed_ref[:, low : low + FR])
        term = term + dot_nn(other, other_ref[:, low : low + FR])
        out_ref[piece] = term.astype(BF16)
    for at in range(CHIPS):
        grads_ref[at] = jnp.sum(grads_z_ref[:, at].astype(F32), axis=0).astype(BF16)
    side = jnp.sum(side_ref[...].astype(F32), axis=0)
    win_ref[...] = side[:, TP * FR :]
    for at in range(TP):
        out_w_ref[at] = side[:, at * FR : (at + 1) * FR].astype(BF16)


def weight_terms(parts, query_grad, cosine, sine, normed, normed_other, grads_z, side_all):
    return compute(
        weight_kernel,
        "weight_terms",
        (parts, query_grad, cosine, sine, normed, normed_other, grads_z, side_all),
        [
            jax.ShapeDtypeStruct((2 * CHIPS, 3 * HD, FR), BF16),
            jax.ShapeDtypeStruct(grads_z.shape[1:], BF16),
            jax.ShapeDtypeStruct((32, DD), F32),
            jax.ShapeDtypeStruct((TP, 32, FR), BF16),
        ],
    )


def weight_sum_kernel(part_ref, grads_ref, out_w_ref, out_ref, depth_ref):
    for head in range(2):
        total = jnp.sum(part_ref[head].astype(F32), axis=0).T
        for kind in range(3):
            out_ref[kind, :, head * HD : (head + 1) * HD] = total[:, kind * HD : (kind + 1) * HD]
    out_ref[3] = out_w_ref[...].astype(F32).reshape(FR, 2 * HD)
    depth_ref[...] = jnp.sum(jnp.sum(grads_ref[...].astype(F32), axis=0), axis=0)


def weight_sum(parts, grads_all, out_all):
    return compute(
        weight_sum_kernel,
        "weight_sum",
        (parts, grads_all, out_all),
        [
            jax.ShapeDtypeStruct((4, FR, 2 * HD), F32),
            jax.ShapeDtypeStruct(grads_all.shape[2:], F32),
        ],
    )


def per_device(hidden_in, temporal_weight_stack, depth_in, depth_stack, audio_codes):
    seq_index = lax.axis_index("seq")
    tp_index = lax.axis_index("tp")
    chip = seq_index // 2
    width = hidden_in.shape[1]
    depth_frames, book_count = audio_codes.shape
    seq_count = 2 * CHIPS
    total_frames = FR * seq_count
    loss_scale = 1.0 / math.sqrt(total_frames * book_count)

    hidden_full = hidden_in.astype(F32)
    normed = (hidden_full * rms_scale(hidden_full)).astype(BF16)
    projected = jnp.einsum(
        "wo,obu->wbu", normed, temporal_weight_stack[:, :3, :], preferred_element_type=F32
    )
    cosine, sine = angle_tables(seq_index * FR, FR)
    query = rotate(projected[:, 0].reshape(FR, 2, HD), cosine, sine).astype(BF16)
    key = rotate(projected[:, 1].reshape(FR, 2, HD), cosine, sine).astype(BF16)
    value = projected[:, 2].reshape(FR, 2, HD).astype(BF16)
    kv = jnp.concatenate([key, value], axis=-1).transpose(1, 0, 2)
    query = query.transpose(1, 0, 2)
    out_w = temporal_weight_stack[:, 3, :].reshape(seq_count, TP, -1, 2 * HD)
    out_w = out_w.transpose(1, 0, 2, 3).reshape(TP, NS, 2 * HD)
    kv_all, query_two, w_half = exchange_keys(kv, query, out_w)

    depth_in = depth_in.reshape(seq_count, TP, -1, DD)
    attended, probs, out_t, inverse = attend(kv_all, query_two)
    att_all, w_other, normed_other = exchange_attended(attended, w_half, normed)
    merged, rounded, latent_parts = merge(att_all, w_half, w_other, hidden_in, depth_in)
    latent_parts, att_other, rounded_other = exchange_latent(latent_parts, att_all, rounded)
    before = jnp.concatenate(
        [jnp.full((depth_frames, 1), -1, jnp.int32), audio_codes[:, :-1]], axis=1
    ).reshape(-1, 1)
    message, grads = depth(
        latent_parts, depth_stack, before, audio_codes.reshape(-1, 1), width, loss_scale
    )
    grads = grads.reshape(CHIPS, 2, TP, -1, DD)
    messages, grads_other = exchange_message(message, grads)
    cotangent_parts, side, grads = unmerge(
        messages,
        merged,
        rounded,
        rounded_other,
        att_all,
        att_other,
        w_half,
        w_other,
        grads_other,
        grads,
        depth_in,
    )
    cotangent_parts, side_all = exchange_cotangent(cotangent_parts, side)

    cosine, sine = angle_tables(chip * FR2, FR2)
    key_parts, query_grad = attend_back(
        probs, kv_all, query_two, cotangent_parts, out_t, inverse, cosine, sine
    )
    key_parts, grads_z = exchange_key_grads(
        key_parts.reshape(CHIPS, FR2, 2 * HD), grads.reshape(CHIPS, 2, 4, -1, DD)
    )
    parts, grads, grad_win, out_parts = weight_terms(
        key_parts, query_grad, cosine, sine, normed, normed_other, grads_z, side_all
    )
    grad_temporal, grad_depth = weight_sum(*exchange_weights(parts, grads, out_parts))
    return grad_temporal.transpose(1, 0, 2), grad_win, grad_depth


def solution(mesh):
    in_specs = (P("seq", None), P(None, None, "tp"), P(), P(), P(("seq", "tp"), None))
    out_specs = (P("seq", None, "tp"), P(("seq", "tp"), None), P(("seq", "tp"), None))
    return jax.shard_map(
        per_device, mesh=mesh, in_specs=in_specs, out_specs=out_specs, check_vma=False
    )
```

```python
import functools
import math

import jax
import jax.numpy as jnp
from jax import lax
from jax.experimental import pallas as pl
from jax.experimental.pallas import tpu as pltpu
from jax.sharding import PartitionSpec as P

HD = 128
DHD = 64
VOCAB = 1024
CHIPS = 8
TP = 8
FR = 256
FR2 = 512
DD = 512
NS = 512

EPSILON = 1e-05
MASKED = -1e30
ROPE_BASE = 10000.0
MIB = 2**20
MESH = pl.DeviceIdType.MESH
F32 = jnp.float32
BF16 = jnp.bfloat16
ANY = pl.BlockSpec(memory_space=pl.ANY)
VMEM = pl.BlockSpec(memory_space=pltpu.VMEM)
TP_ORDER = (4, 1, 3, 5, 7, 2, 6)
CHIP_ORDER = (2, 6, 1, 4, 3, 7, 5)


def dot_nn(left, right):
    return jnp.dot(left, right, preferred_element_type=F32)


def dot_nt(left, right):
    return lax.dot_general(left, right, (((1,), (1,)), ((), ())), preferred_element_type=F32)


def dot_tn(left, right):
    return lax.dot_general(left, right, (((0,), (0,)), ((), ())), preferred_element_type=F32)


def rms_scale(values):
    return lax.rsqrt(jnp.mean(values * values, axis=-1, keepdims=True) + EPSILON)


def norm_back(values, scaling, gradient):
    inner_mean = jnp.mean(gradient * values, axis=-1, keepdims=True)
    return scaling * (gradient - values * (scaling * scaling) * inner_mean)


def angle_tables(first, count):
    half_width = HD // 2
    frequency = ROPE_BASE ** (-jnp.arange(half_width).astype(F32) / half_width)
    positions = (first + jnp.arange(count)).astype(F32)
    angles = positions[:, None] * frequency[None, :]
    return jnp.cos(angles), jnp.sin(angles)


def place():
    seq = lax.axis_index("seq")
    tp = lax.axis_index("tp")
    return seq, seq // 2, seq % 2, tp


def run_exchange(peers, jobs, locals_, send_sems, recv_sems, forwards=()):
    barrier = pltpu.get_barrier_semaphore()
    for peer in peers:
        pl.semaphore_signal(barrier, inc=1, device_id=peer, device_id_type=MESH)
    pl.semaphore_wait(barrier, len(peers))
    copies = []

    def begin(source, target, device, *when):
        number = len(copies)
        copy = pltpu.make_async_remote_copy(
            src_ref=source,
            dst_ref=target,
            send_sem=send_sems.at[number],
            recv_sem=recv_sems.at[number],
            device_id=device,
            device_id_type=MESH,
        )
        if when:
            pl.when(when[0])(copy.start)
        else:
            copy.start()
        copies.append((copy, when))

    for job in jobs:
        begin(*job)
    for source, bounce, target, sem in locals_:
        copy = pltpu.make_async_copy(source, bounce, sem)
        copy.start()
        copy.wait()
        copy = pltpu.make_async_copy(bounce, target, sem)
        copy.start()
        copy.wait()
    arrived = set()
    for number, job in forwards:
        copies[number][0].wait_recv()
        arrived.add(number)
        begin(*job)
    for number, (copy, when) in enumerate(copies):
        if when:
            pl.when(when[0])(copy.wait_send)
            pl.when(when[1])(copy.wait_recv)
        else:
            copy.wait_send()
            if number not in arrived:
                copy.wait_recv()


def exchange(kernel, name, collective_id, ins, outs, copies, bounces):
    return pl.pallas_call(
        kernel,
        name=name,
        out_shape=outs,
        in_specs=[ANY] * len(ins),
        out_specs=[ANY] * len(outs),
        scratch_shapes=[
            pltpu.SemaphoreType.DMA((copies,)),
            pltpu.SemaphoreType.DMA((copies,)),
            pltpu.SemaphoreType.DMA,
        ]
        + [pltpu.VMEM(shape, dtype) for shape, dtype in bounces],
        compiler_params=pltpu.CompilerParams(
            collective_id=collective_id, has_side_effects=True, vmem_limit_bytes=4 * MIB
        ),
    )(*ins)


def tp_peers(seq, tp, order=TP_ORDER):
    return [(seq, lax.rem(tp + hop, TP)) for hop in order]


def chip_peers(chip, core, tp, order=CHIP_ORDER):
    return [(lax.rem(chip + hop, CHIPS) * 2 + core, tp) for hop in order]


def keys_kernel(
    kv, query, out_w, kv_all, query_two, w_half, send_sems, recv_sems, sem, kv_bounce, query_bounce, w_bounce
):
    seq, chip, core, tp = place()
    partner = (chip * 2 + 1 - core, tp)
    half = pl.ds(core * FR, FR)
    peers = [partner]
    jobs = []
    for hop in CHIP_ORDER:
        there = lax.rem(chip + hop, CHIPS)
        later = there > chip
        earlier = lax.rem(chip - hop + CHIPS, CHIPS) < chip
        for head in (core, 1 - core):
            other = (there * 2 + head, tp)
            peers.append(other)
            jobs.append((kv.at[head], kv_all.at[seq], other, later, earlier))
    for other in tp_peers(seq, tp):
        peers.append(other)
        jobs.append((out_w.at[other[1], half], w_half.at[tp], other))
    jobs.append((query.at[1 - core], query_two.at[core], partner))
    jobs.append((kv.at[1 - core], kv_all.at[seq], partner))
    run_exchange(
        peers,
        jobs,
        [
            (kv.at[core], kv_bounce, kv_all.at[seq], sem),
            (query.at[core], query_bounce, query_two.at[core], sem),
            (out_w.at[tp, half], w_bounce, w_half.at[tp], sem),
        ],
        send_sems,
        recv_sems,
    )


def exchange_keys(kv, query, out_w):
    return exchange(
        keys_kernel,
        "exchange_keys",
        1,
        (kv, query, out_w),
        [
            jax.ShapeDtypeStruct((2 * CHIPS, FR, 2 * HD), BF16),
            jax.ShapeDtypeStruct((2, FR, HD), BF16),
            jax.ShapeDtypeStruct((TP, FR, 2 * HD), BF16),
        ],
        23,
        [((FR, 2 * HD), BF16), ((FR, HD), BF16), ((FR, 2 * HD), BF16)],
    )


def attended_kernel(source, w_half, target, w_other, send_sems, recv_sems, sem, bounce):
    seq, chip, core, tp = place()
    slot = tp * 2 + core
    partner_seq = chip * 2 + 1 - core
    partner = (partner_seq, tp)
    peers = [partner] + tp_peers(seq, tp) + tp_peers(partner_seq, tp)
    own = pl.ds(core * FR, FR)
    other = pl.ds((1 - core) * FR, FR)
    rows = [other] + [own] * (TP - 1) + [other] * (TP - 1)
    jobs = [(source.at[part], target.at[slot], peer) for part, peer in zip(rows, peers)]
    jobs.append((w_half, w_other, partner))
    run_exchange(
        peers, jobs, [(source.at[own], bounce, target.at[slot], sem)], send_sems, recv_sems
    )


def exchange_attended(attended, w_half):
    return exchange(
        attended_kernel,
        "exchange_attended",
        2,
        (attended, w_half),
        [
            jax.ShapeDtypeStruct((2 * TP, FR, HD), BF16),
            jax.ShapeDtypeStruct(w_half.shape, BF16),
        ],
        16,
        [((FR, HD), BF16)],
    )


def latent_kernel(
    source, att_all, merged, target, att_other, merged_other, send_sems, recv_sems, sem, bounce
):
    seq, chip, core, tp = place()
    partner = (chip * 2 + 1 - core, tp)
    peers = tp_peers(seq, tp)
    jobs = [(source.at[peer[1]], target.at[tp], peer) for peer in peers]
    jobs.append((att_all, att_other, partner))
    jobs.append((merged, merged_other, partner))
    run_exchange(
        peers + [partner],
        jobs,
        [(source.at[tp], bounce, target.at[tp], sem)],
        send_sems,
        recv_sems,
    )


def exchange_latent(parts, att_all, merged):
    return exchange(
        latent_kernel,
        "exchange_latent",
        3,
        (parts, att_all, merged),
        [
            jax.ShapeDtypeStruct(parts.shape, parts.dtype),
            jax.ShapeDtypeStruct(att_all.shape, BF16),
            jax.ShapeDtypeStruct(merged.shape, BF16),
        ],
        9,
        [(parts.shape[1:], parts.dtype)],
    )


def message_kernel(source, grads, target, grads_other, send_sems, recv_sems, sem, bounce):
    seq, chip, core, tp = place()
    partner = (chip * 2 + 1 - core, tp)
    peers = tp_peers(seq, tp)
    jobs = [(source, target.at[core, tp], peer) for peer in peers]
    forwards = []
    for number, hop in enumerate(TP_ORDER):
        slot = target.at[core, lax.rem(tp - hop + TP, TP)]
        forwards.append((number, (slot, slot, partner)))
    jobs.append((source, target.at[core, tp], partner))
    jobs.append((grads.at[:, 1 - core], grads_other, partner))
    run_exchange(
        peers + [partner],
        jobs,
        [(source, bounce, target.at[core, tp], sem)],
        send_sems,
        recv_sems,
        forwards,
    )


def exchange_message(message, grads):
    return exchange(
        message_kernel,
        "exchange_message",
        4,
        (message, grads),
        [
            jax.ShapeDtypeStruct((2, TP) + message.shape, message.dtype),
            jax.ShapeDtypeStruct((CHIPS, TP) + grads.shape[3:], BF16),
        ],
        16,
        [(message.shape, message.dtype)],
    )


def cotangent_kernel(source, side, target, side_x, send_sems, recv_sems, sem, bounce, side_bounce):
    seq, chip, core, tp = place()
    partner_seq = chip * 2 + 1 - core
    at_x, at_y = chip // 2, chip % 2
    peers = [(partner_seq, tp)] + tp_peers(seq, tp) + tp_peers(partner_seq, tp)
    heads = [1 - core] + [core] * (TP - 1) + [1 - core] * (TP - 1)
    jobs = [
        (source.at[peer[1] * 2 + head], target.at[core, tp], peer)
        for head, peer in zip(heads, peers)
    ]
    for hop in (2, 1, 3):
        there = lax.rem(at_x + hop, 4)
        other = (there * 4 + at_y * 2 + core, tp)
        peers.append(other)
        jobs.append((side.at[there], side_x.at[at_x], other))
    run_exchange(
        peers,
        jobs,
        [
            (source.at[tp * 2 + core], bounce, target.at[core, tp], sem),
            (side.at[at_x], side_bounce, side_x.at[at_x], sem),
        ],
        send_sems,
        recv_sems,
    )


def exchange_cotangent(parts, side):
    return exchange(
        cotangent_kernel,
        "exchange_cotangent",
        5,
        (parts, side),
        [
            jax.ShapeDtypeStruct((2, TP, FR, HD), BF16),
            jax.ShapeDtypeStruct(side.shape, BF16),
        ],
        18,
        [((FR, HD), BF16), (side.shape[1:], BF16)],
    )


def key_grads_kernel(
    source, grads, side, normed, target, grads_z, side_in, normed_other,
    send_sems, recv_sems, sem, bounce, grads_bounce,
):
    seq, chip, core, tp = place()
    row, depth_at = tp // 4, tp % 4
    at_x, at_y = chip // 2, chip % 2
    peers = []
    jobs = []
    for hop in CHIP_ORDER:
        there = lax.rem(chip + hop, CHIPS)
        here = lax.rem(chip - hop + CHIPS, CHIPS)
        other = (there * 2 + core, tp)
        peers.append(other)
        jobs.append((source.at[there], target.at[chip], other, there < chip, here > chip))
    for hop in (1, 3, 2):
        there = lax.rem(depth_at + hop, 4)
        other = (seq, row * 4 + there)
        peers.append(other)
        jobs.append((grads.at[:, :, there], grads_z.at[depth_at], other))
    jobs.append((side.at[1 - at_y], side_in, (at_x * 4 + (1 - at_y) * 2 + core, tp)))
    partner = (chip * 2 + 1 - core, tp)
    jobs.append((normed, normed_other, partner))
    peers.append(partner)
    run_exchange(
        peers,
        jobs,
        [
            (source.at[chip], bounce, target.at[chip], sem),
            (grads.at[:, :, depth_at], grads_bounce, grads_z.at[depth_at], sem),
        ],
        send_sems,
        recv_sems,
    )


def exchange_key_grads(parts, grads, side, normed):
    slab = (CHIPS, 2) + grads.shape[3:]
    return exchange(
        key_grads_kernel,
        "exchange_key_grads",
        6,
        (parts, grads, side, normed),
        [
            jax.ShapeDtypeStruct(parts.shape, parts.dtype),
            jax.ShapeDtypeStruct((4,) + slab, BF16),
            jax.ShapeDtypeStruct(side.shape[1:], BF16),
            jax.ShapeDtypeStruct(normed.shape, BF16),
        ],
        12,
        [(parts.shape[1:], parts.dtype), (slab, BF16)],
    )


def weights_kernel(
    source, grads, out, target, grads_all, out_all, send_sems, recv_sems, sem, bounce, grads_bounce, out_bounce
):
    seq, chip, core, tp = place()
    row, depth_at = tp // 4, tp % 4
    partner = (chip * 2 + 1 - core, tp)
    peers = [partner] + chip_peers(chip, core, tp) + chip_peers(chip, 1 - core, tp)
    jobs = [(source.at[peer[0]], target.at[core, chip], peer) for peer in peers]
    for hop in CHIP_ORDER:
        there = lax.rem(chip + hop, CHIPS)
        jobs.append((grads.at[there, row], grads_all.at[chip, row], (there * 2 + core, tp)))
    across = (1 - row) * 4 + depth_at
    for hop in (0,) + CHIP_ORDER:
        there = lax.rem(chip + hop, CHIPS)
        other = (there * 2 + core, across)
        if hop:
            peers.append(other)
        jobs.append((grads.at[there, 1 - row], grads_all.at[chip, row], other))
    for other in tp_peers(seq, tp):
        peers.append(other)
        jobs.append((out.at[other[1]], out_all.at[tp], other))
    run_exchange(
        peers,
        jobs,
        [
            (source.at[seq], bounce, target.at[core, chip], sem),
            (grads.at[chip, row], grads_bounce, grads_all.at[chip, row], sem),
            (out.at[tp], out_bounce, out_all.at[tp], sem),
        ],
        send_sems,
        recv_sems,
    )


def exchange_weights(parts, grads, out):
    return exchange(
        weights_kernel,
        "exchange_weights",
        7,
        (parts, grads, out),
        [
            jax.ShapeDtypeStruct((2, CHIPS) + parts.shape[1:], parts.dtype),
            jax.ShapeDtypeStruct(grads.shape, BF16),
            jax.ShapeDtypeStruct(out.shape, BF16),
        ],
        37,
        [(parts.shape[1:], BF16), (grads.shape[2:], BF16), (out.shape[1:], BF16)],
    )


def compute(kernel, name, ins, outs, scratch=(), limit=48, hbm=0):
    return pl.pallas_call(
        kernel,
        name=name,
        out_shape=outs,
        in_specs=[VMEM] * (len(ins) - hbm) + [ANY] * hbm,
        out_specs=[VMEM] * len(outs),
        scratch_shapes=list(scratch),
        compiler_params=pltpu.CompilerParams(vmem_limit_bytes=limit * MIB),
    )(*ins)


def start_kernel(
    hidden_ref, w_ref, cos_ref, sin_ref, normed_ref, kv_ref, query_ref, out_w_ref, total_ref
):
    step = pl.program_id(0)
    depth_rows = w_ref.shape[0]

    @pl.when(step == 0)
    def _():
        hidden = hidden_ref[...].astype(F32)
        normed_ref[...] = (hidden * rms_scale(hidden)).astype(BF16)
        total_ref[...] = jnp.zeros_like(total_ref)

    normed = normed_ref[:, pl.ds(pl.multiple_of(step * depth_rows, depth_rows), depth_rows)]
    weights = w_ref[...].reshape(depth_rows, 8 * HD)
    total_ref[...] += dot_nn(normed, weights[:, : 6 * HD])
    out_w = weights[:, 6 * HD :].reshape(-1, TP, 32, 2 * HD)
    for at in range(TP):
        for piece in range(out_w.shape[0]):
            out_w_ref[at, piece * 32 : (piece + 1) * 32] = out_w[piece, at]

    @pl.when(step == pl.num_programs(0) - 1)
    def _():
        cosine, sine = cos_ref[...], sin_ref[...]

        def turned(at):
            lower = total_ref[:, at : at + HD // 2]
            upper = total_ref[:, at + HD // 2 : at + HD]
            return jnp.concatenate(
                [lower * cosine - upper * sine, upper * cosine + lower * sine], axis=1
            ).astype(BF16)

        for head in range(2):
            query_ref[head] = turned(head * HD)
            kv_ref[head, :, :HD] = turned((2 + head) * HD)
            at = (4 + head) * HD
            kv_ref[head, :, HD:] = total_ref[:, at : at + HD].astype(BF16)


def start(hidden, weights, cosine, sine):
    steps = 8
    depth_rows = weights.shape[0] // steps

    def whole(*shape):
        return pl.BlockSpec(shape, lambda step: (0,) * len(shape))

    return pl.pallas_call(
        start_kernel,
        name="start",
        grid=(steps,),
        out_shape=[
            jax.ShapeDtypeStruct(hidden.shape, BF16),
            jax.ShapeDtypeStruct((2, FR, 2 * HD), BF16),
            jax.ShapeDtypeStruct((2, FR, HD), BF16),
            jax.ShapeDtypeStruct((TP, NS, 2 * HD), BF16),
        ],
        in_specs=[
            whole(*hidden.shape),
            pl.BlockSpec((depth_rows, 4, 2 * HD), lambda step: (step, 0, 0)),
            whole(*cosine.shape),
            whole(*sine.shape),
        ],
        out_specs=[
            whole(*hidden.shape),
            whole(2, FR, 2 * HD),
            whole(2, FR, HD),
            pl.BlockSpec((TP, depth_rows // TP, 2 * HD), lambda step: (0, step, 0)),
        ],
        scratch_shapes=[pltpu.VMEM((FR, 6 * HD), F32)],
        compiler_params=pltpu.CompilerParams(vmem_limit_bytes=24 * MIB),
    )(hidden, weights, cosine, sine)


def attend_kernel(kv_ref, query_ref, out_ref, prob_ref, out_t_ref, inverse_ref, score_ref):
    chip = lax.axis_index("seq") // 2
    query = query_ref[...].reshape(FR2, HD)
    scale = math.log2(math.e) / math.sqrt(HD)
    key_at = lax.broadcasted_iota(jnp.int32, (FR2, FR2), 0)
    query_at = lax.broadcasted_iota(jnp.int32, (FR2, FR2), 1)

    def scores(block, top):
        score = dot_nt(kv_ref[block, :, :HD], query) * scale
        score_ref[block] = score
        return jnp.maximum(top, jnp.max(score, axis=0, keepdims=True))

    score = dot_nt(kv_ref[chip, :, :HD], query) * scale
    score = jnp.where(key_at <= query_at, score, MASKED)
    score_ref[chip] = score
    top = lax.fori_loop(0, chip, scores, jnp.max(score, axis=0, keepdims=True))

    def weigh(block, carry):
        total, mixed = carry
        prob = jnp.exp2(score_ref[block] - top)
        total = total + jnp.sum(prob, axis=0, keepdims=True)
        prob = prob.astype(BF16)
        prob_ref[block] = prob
        return total, mixed + dot_tn(kv_ref[block, :, HD:], prob)

    total, mixed = lax.fori_loop(
        0, chip + 1, weigh, (jnp.zeros((1, FR2), F32), jnp.zeros((HD, FR2), F32))
    )
    inverse = 1.0 / total
    mixed = mixed * inverse
    out_t_ref[...] = mixed
    inverse_ref[...] = inverse
    out_ref[...] = mixed.T.astype(BF16)


def attend(kv_all, query_two):
    return compute(
        attend_kernel,
        "attend",
        (kv_all, query_two),
        [
            jax.ShapeDtypeStruct((FR2, HD), BF16),
            jax.ShapeDtypeStruct((CHIPS, FR2, FR2), BF16),
            jax.ShapeDtypeStruct((HD, FR2), F32),
            jax.ShapeDtypeStruct((1, FR2), F32),
        ],
        [pltpu.VMEM((CHIPS, FR2, FR2), F32)],
        limit=24,
    )


def fetch(source, target, sem):
    copy = pltpu.make_async_copy(source, target, sem)
    copy.start()
    return copy


def order_halves(core, mine, other):
    return jnp.where(core == 0, mine, other), jnp.where(core == 0, other, mine)


def merge_kernel(
    att_ref, half_ref, other_ref, hidden_ref, depth_in_hbm, merged_ref, round_ref, part_ref, depth_in_ref, sem
):
    seq, chip, core, tp = place()
    copy = fetch(depth_in_hbm.at[:, tp], depth_in_ref, sem)
    width = hidden_ref.shape[1]
    group = width // 2
    row_at = lax.broadcasted_iota(jnp.int32, (group, FR), 0)
    col_at = lax.broadcasted_iota(jnp.int32, (group, FR), 1)
    wanted = (col_at // 32) * 256 + tp * 32 + col_at % 32
    pick = jnp.where(row_at == wanted, 1.0, 0.0).astype(BF16)
    merged = jnp.concatenate(
        [dot_nn(hidden_ref[:, :group], pick), dot_nn(hidden_ref[:, group:], pick)], axis=1
    )
    mine = jnp.zeros((FR, FR), F32)
    other = jnp.zeros((FR, FR), F32)
    for at in range(TP):
        pair = jnp.concatenate([att_ref[2 * at], att_ref[2 * at + 1]], axis=1)
        mine = mine + dot_nt(pair, half_ref[at])
        other = other + dot_nt(pair, other_ref[at])
    merged = merged + jnp.concatenate(order_halves(core, mine, other), axis=1)
    rounded = merged.astype(BF16)
    merged_ref[...] = merged
    round_ref[...] = rounded
    squares = jnp.sum(merged * merged, axis=-1, keepdims=True)
    copy.wait()
    latent = dot_nn(rounded, depth_in_ref[...].reshape(NS, DD))
    coarse = squares.astype(BF16)
    fine = (squares - coarse.astype(F32)).astype(BF16)
    part_ref[:, :, :DD] = latent.astype(BF16).reshape(TP, FR // TP, DD)
    part_ref[:, :, DD : DD + HD] = jnp.broadcast_to(coarse, (FR, HD)).reshape(TP, FR // TP, HD)
    part_ref[:, :, DD + HD :] = jnp.broadcast_to(fine, (FR, HD)).reshape(TP, FR // TP, HD)


def merge(att_all, w_half, w_other, hidden, depth_in):
    return compute(
        merge_kernel,
        "merge",
        (att_all, w_half, w_other, hidden, depth_in),
        [
            jax.ShapeDtypeStruct((FR, NS), F32),
            jax.ShapeDtypeStruct((FR, NS), BF16),
            jax.ShapeDtypeStruct((TP, FR // TP, DD + 2 * HD), BF16),
        ],
        [pltpu.VMEM((2 * CHIPS, 32, DD), BF16), pltpu.SemaphoreType.DMA],
        hbm=1,
        limit=24,
    )


def depth_kernel(width, loss_scale, part_ref, stack_ref, before_ref, code_ref, message_ref, grad_ref, prob_ref):
    frames = part_ref.shape[1]
    books = before_ref.shape[0] // frames
    tokens = frames * books
    qkv_rows = stack_ref[: 3 * DD]
    out_rows = stack_ref[3 * DD : 4 * DD]
    head_rows = stack_ref[4 * DD : 4 * DD + VOCAB]
    embed_rows = stack_ref[4 * DD + VOCAB :]
    total = jnp.sum(part_ref[...].astype(F32), axis=0)
    raw = total[:, :DD]
    squares = total[:, DD : DD + 1] + total[:, DD + HD : DD + HD + 1]
    scale_in = lax.rsqrt(squares * (1.0 / width) + EPSILON)
    latent = raw * scale_in
    latent = jnp.broadcast_to(latent[:, None, :], (frames, books, DD)).reshape(tokens, DD)
    vocab_at = lax.broadcasted_iota(jnp.int32, (tokens, VOCAB), 1)
    hot = jnp.where(before_ref[...] == vocab_at, 1.0, 0.0).astype(BF16)
    stream = latent + dot_nn(hot, embed_rows)
    stream_scale = rms_scale(stream)
    stream_norm = (stream * stream_scale).astype(BF16)
    proj = dot_nt(stream_norm, qkv_rows).astype(BF16)
    row_at = lax.broadcasted_iota(jnp.int32, (tokens, tokens), 0)
    col_at = lax.broadcasted_iota(jnp.int32, (tokens, tokens), 1)
    allowed = (row_at // books == col_at // books) & (col_at <= row_at)
    depth_scale = 1.0 / math.sqrt(DHD)
    mixed = []
    for head in range(DD // DHD):
        low = head * DHD
        queries = proj[:, low : low + DHD]
        keys = proj[:, DD + low : DD + low + DHD]
        values = proj[:, 2 * DD + low : 2 * DD + low + DHD]
        scores = jnp.where(allowed, dot_nt(queries, keys) * depth_scale, MASKED)
        weights = jnp.exp(scores - jnp.max(scores, axis=-1, keepdims=True))
        probs = weights / jnp.sum(weights, axis=-1, keepdims=True)
        prob_ref[head] = probs
        mixed.append(dot_nn(probs.astype(BF16), values))
    mixed = jnp.concatenate(mixed, axis=1).astype(BF16)
    resid = stream + dot_nt(mixed, out_rows)
    resid_scale = rms_scale(resid)
    resid_norm = (resid * resid_scale).astype(BF16)
    logits = dot_nt(resid_norm, head_rows)
    weights = jnp.exp(logits - jnp.max(logits, axis=-1, keepdims=True))
    logit_probs = weights / jnp.sum(weights, axis=-1, keepdims=True)
    target = jnp.where(code_ref[...] == vocab_at, 1.0, 0.0)
    logit_grad = ((logit_probs - target) * loss_scale).astype(BF16)
    grad_ref[4 * DD : 4 * DD + VOCAB] = dot_tn(logit_grad, resid_norm).astype(BF16)
    resid_grad = norm_back(resid, resid_scale, dot_nn(logit_grad, head_rows))
    resid_round = resid_grad.astype(BF16)
    grad_ref[3 * DD : 4 * DD] = dot_tn(resid_round, mixed).astype(BF16)
    mixed_grad = dot_nn(resid_round, out_rows).astype(BF16)
    query_grad, key_grad, value_grad = [], [], []
    for head in range(DD // DHD):
        low = head * DHD
        queries = proj[:, low : low + DHD]
        keys = proj[:, DD + low : DD + low + DHD]
        values = proj[:, 2 * DD + low : 2 * DD + low + DHD]
        probs = prob_ref[head]
        mix_grad = mixed_grad[:, low : low + DHD]
        value_grad.append(dot_tn(probs.astype(BF16), mix_grad))
        prob_grad = dot_nt(mix_grad, values)
        inner = jnp.sum(probs * prob_grad, axis=-1, keepdims=True)
        score_grad = (probs * (prob_grad - inner) * depth_scale).astype(BF16)
        query_grad.append(dot_nn(score_grad, keys))
        key_grad.append(dot_tn(score_grad, queries))
    proj_grad = jnp.concatenate(query_grad + key_grad + value_grad, axis=1).astype(BF16)
    grad_ref[: 3 * DD] = dot_tn(proj_grad, stream_norm).astype(BF16)
    stream_grad = resid_grad + norm_back(stream, stream_scale, dot_nn(proj_grad, qkv_rows))
    grad_ref[4 * DD + VOCAB :] = dot_tn(hot, stream_grad.astype(BF16)).astype(BF16)
    latent_grad = jnp.sum(stream_grad.reshape(frames, books, DD), axis=1)
    latent_grad = latent_grad.astype(BF16).astype(F32)
    inner = jnp.sum(latent_grad * raw, axis=-1, keepdims=True) * (1.0 / width)
    pull = scale_in * scale_in * scale_in * inner
    coarse = pull.astype(BF16)
    fine = (pull - coarse.astype(F32)).astype(BF16)
    message_ref[:, :DD] = (latent_grad * scale_in).astype(BF16)
    message_ref[:, DD : DD + HD] = jnp.broadcast_to(coarse, (frames, HD))
    message_ref[:, DD + HD :] = jnp.broadcast_to(fine, (frames, HD))


def depth(parts, stack, before, codes, width, loss_scale):
    tokens = before.shape[0]
    return compute(
        functools.partial(depth_kernel, width, loss_scale),
        "depth",
        (parts, stack, before, codes),
        [
            jax.ShapeDtypeStruct((parts.shape[1], DD + 2 * HD), BF16),
            jax.ShapeDtypeStruct(stack.shape, BF16),
        ],
        [pltpu.VMEM((DD // DHD, tokens, tokens), F32)],
        limit=32,
    )


def merged_gradient(message, merged, depth_in):
    pull = message[:, DD : DD + 1].astype(F32) + message[:, DD + HD : DD + HD + 1].astype(F32)
    return dot_nt(message[:, :DD], depth_in) - merged * pull


def unmerge_kernel(
    message_ref,
    merged_ref,
    round_ref,
    round_other_ref,
    att_ref,
    att_other_ref,
    half_ref,
    other_ref,
    grads_other_ref,
    grads_hbm,
    depth_in_hbm,
    part_ref,
    side_ref,
    grads_ref,
    depth_in_ref,
    grads_own_ref,
    sems,
):
    seq, chip, core, tp = place()
    copy = fetch(depth_in_hbm.at[:, tp], depth_in_ref, sems.at[0])
    grads_copy = fetch(grads_hbm.at[:, core], grads_own_ref, sems.at[1])
    copy.wait()
    depth_in = depth_in_ref[...].reshape(NS, DD)
    message = message_ref[core].reshape(FR, DD + 2 * HD)
    message_other = message_ref[1 - core].reshape(FR, DD + 2 * HD)
    gradient = merged_gradient(message, merged_ref[...], depth_in)
    lower, upper = gradient[:, :FR], gradient[:, FR:]
    mine, other = order_halves(core, lower, upper)
    mine, other = mine.astype(BF16), other.astype(BF16)
    for at in range(TP):
        pair = (dot_nn(mine, half_ref[at]) + dot_nn(other, other_ref[at])).astype(BF16)
        part_ref[2 * at] = pair[:, :HD]
        part_ref[2 * at + 1] = pair[:, HD:]
    gradient_other = merged_gradient(
        message_other, round_other_ref[...].astype(F32), depth_in
    )

    def pick_rows(own, others):
        both = jnp.concatenate([own.T, others.T], axis=1).reshape(CHIPS, 2, 32, FR2)
        both = jnp.where(core == 0, both[:, 0], both[:, 1])
        return both.reshape(FR, FR2).astype(BF16)

    rows = pick_rows(gradient, gradient_other)
    for at in range(TP):
        pair = jnp.concatenate([att_ref[2 * at], att_ref[2 * at + 1]], axis=1)
        pair_other = jnp.concatenate([att_other_ref[2 * at], att_other_ref[2 * at + 1]], axis=1)
        term = dot_nn(rows, jnp.concatenate([pair, pair_other], axis=0)).astype(BF16)
        side_ref[:, :, at * FR : (at + 1) * FR] = term.reshape(CHIPS, 32, FR)
    rows = pick_rows(round_ref[...].astype(F32), round_other_ref[...].astype(F32))
    both = jnp.concatenate([message[:, :DD], message_other[:, :DD]], axis=0)
    side_ref[:, :, TP * FR :] = dot_nn(rows, both).astype(BF16).reshape(CHIPS, 32, DD)
    grads_copy.wait()
    for at in range(CHIPS):
        grads_ref[at] = (
            grads_own_ref[at].astype(F32) + grads_other_ref[at].astype(F32)
        ).astype(BF16)


def unmerge(
    messages, merged, rounded, rounded_other, att_all, att_other, w_half, w_other, grads_other, grads, depth_in
):
    return compute(
        unmerge_kernel,
        "unmerge",
        (
            messages,
            merged,
            rounded,
            rounded_other,
            att_all,
            att_other,
            w_half,
            w_other,
            grads_other,
            grads,
            depth_in,
        ),
        [
            jax.ShapeDtypeStruct((2 * TP, FR, HD), BF16),
            jax.ShapeDtypeStruct((CHIPS, 32, TP * FR + DD), BF16),
            jax.ShapeDtypeStruct(grads_other.shape, BF16),
        ],
        [
            pltpu.VMEM((2 * CHIPS, 32, DD), BF16),
            pltpu.VMEM(grads_other.shape, BF16),
            pltpu.SemaphoreType.DMA((2,)),
        ],
        hbm=2,
        limit=28,
    )


def attend_back_kernel(
    prob_ref, kv_ref, query_ref, part_ref, out_t_ref, inverse_ref, cos_ref, sin_ref, side_x_ref,
    grad_ref, query_grad_ref, side_ref,
):
    chip = lax.axis_index("seq") // 2
    query = query_ref[...].reshape(FR2, HD)
    gradient = jnp.sum(part_ref[...].astype(F32), axis=1).reshape(FR2, HD)
    gradient = gradient.astype(BF16).astype(F32)
    gradient_t = (gradient.T * inverse_ref[...]).astype(BF16)
    wide_t = gradient_t.astype(F32)
    inner = jnp.sum(wide_t * out_t_ref[...], axis=0, keepdims=True)
    gradient = wide_t.T.astype(BF16)
    scale = 1.0 / math.sqrt(HD)

    def step(block, query_grad):
        prob = prob_ref[block]
        score_grad = prob.astype(F32) * (dot_nn(kv_ref[block, :, HD:], gradient_t) - inner)
        score_grad = score_grad.astype(BF16)
        grad_ref[block, :, :HD] = (dot_nn(score_grad, query) * scale).astype(BF16)
        grad_ref[block, :, HD:] = dot_nn(prob, gradient).astype(BF16)
        return query_grad + dot_tn(kv_ref[block, :, :HD], score_grad)

    query_grad = lax.fori_loop(0, chip + 1, step, jnp.zeros((HD, FR2), F32)) * scale
    query_grad = query_grad.T
    lower, upper = query_grad[:, : HD // 2], query_grad[:, HD // 2 :]
    cosine, sine = cos_ref[...], sin_ref[...]
    query_grad_ref[...] = jnp.concatenate(
        [lower * cosine + upper * sine, upper * cosine - lower * sine], axis=1
    ).astype(BF16)
    side_ref[...] = jnp.sum(side_x_ref[...].astype(F32), axis=0).astype(BF16)


def attend_back(probs, kv_all, query_two, parts, out_t, inverse, cosine, sine, side_x):
    return compute(
        attend_back_kernel,
        "attend_back",
        (probs, kv_all, query_two, parts, out_t, inverse, cosine, sine, side_x),
        [
            jax.ShapeDtypeStruct((CHIPS, FR2, 2 * HD), BF16),
            jax.ShapeDtypeStruct((FR2, HD), BF16),
            jax.ShapeDtypeStruct(side_x.shape[1:], BF16),
        ],
        limit=28,
    )


def weight_kernel(
    part_ref, query_grad_ref, cos_ref, sin_ref, normed_ref, other_ref, grads_z_ref, side_ref,
    side_in_ref, out_ref, grads_ref, win_ref, out_w_ref,
):
    chip = lax.axis_index("seq") // 2
    core = lax.axis_index("seq") % 2
    total = lax.fori_loop(
        chip,
        CHIPS,
        lambda at, carry: carry + part_ref[at].astype(F32),
        jnp.zeros((FR2, 2 * HD), F32),
    )
    lower, upper = total[:, : HD // 2], total[:, HD // 2 : HD]
    cosine, sine = cos_ref[...], sin_ref[...]
    proj = jnp.concatenate(
        [
            query_grad_ref[...].astype(F32),
            lower * cosine + upper * sine,
            upper * cosine - lower * sine,
            total[:, HD:],
        ],
        axis=1,
    )
    proj_t = proj.T
    own, other = order_halves(core, proj_t[:, :FR], proj_t[:, FR:])
    own, other = own.astype(BF16), other.astype(BF16)
    for piece in range(2 * CHIPS):
        low = piece * FR
        term = dot_nn(own, normed_ref[:, low : low + FR])
        term = term + dot_nn(other, other_ref[:, low : low + FR])
        out_ref[piece] = term.astype(BF16)
    for at in range(CHIPS):
        grads_ref[at] = jnp.sum(grads_z_ref[:, at].astype(F32), axis=0).astype(BF16)
    side = side_ref[chip % 2].astype(F32) + side_in_ref[...].astype(F32)
    win_ref[...] = side[:, TP * FR :]
    for at in range(TP):
        out_w_ref[at] = side[:, at * FR : (at + 1) * FR].astype(BF16)


def weight_terms(parts, query_grad, cosine, sine, normed, normed_other, grads_z, side, side_in):
    return compute(
        weight_kernel,
        "weight_terms",
        (parts, query_grad, cosine, sine, normed, normed_other, grads_z, side, side_in),
        [
            jax.ShapeDtypeStruct((2 * CHIPS, 3 * HD, FR), BF16),
            jax.ShapeDtypeStruct(grads_z.shape[1:], BF16),
            jax.ShapeDtypeStruct((32, DD), F32),
            jax.ShapeDtypeStruct((TP, 32, FR), BF16),
        ],
        limit=28,
    )


def weight_sum_kernel(part_ref, grads_ref, out_w_ref, out_ref, depth_ref):
    for head in range(2):
        total = jnp.sum(part_ref[head].astype(F32), axis=0).T
        for kind in range(3):
            out_ref[kind, :, head * HD : (head + 1) * HD] = total[:, kind * HD : (kind + 1) * HD]
    out_ref[3] = out_w_ref[...].astype(F32).reshape(FR, 2 * HD)
    depth_ref[...] = jnp.sum(jnp.sum(grads_ref[...].astype(F32), axis=0), axis=0)


def weight_sum(parts, grads_all, out_all):
    return compute(
        weight_sum_kernel,
        "weight_sum",
        (parts, grads_all, out_all),
        [
            jax.ShapeDtypeStruct((4, FR, 2 * HD), F32),
            jax.ShapeDtypeStruct(grads_all.shape[2:], F32),
        ],
        limit=16,
    )


def per_device(hidden_in, temporal_weight_stack, depth_in, depth_stack, audio_codes):
    seq_index = lax.axis_index("seq")
    tp_index = lax.axis_index("tp")
    chip = seq_index // 2
    width = hidden_in.shape[1]
    depth_frames, book_count = audio_codes.shape
    seq_count = 2 * CHIPS
    total_frames = FR * seq_count
    loss_scale = 1.0 / math.sqrt(total_frames * book_count)

    cosine, sine = angle_tables(seq_index * FR, FR)
    normed, kv, query, out_w = start(hidden_in, temporal_weight_stack, cosine, sine)
    kv_all, query_two, w_half = exchange_keys(kv, query, out_w)
    kv_all = kv_all.reshape(CHIPS, FR2, 2 * HD)

    depth_in = depth_in.reshape(seq_count, TP, -1, DD)
    attended, probs, out_t, inverse = attend(kv_all, query_two)
    att_all, w_other = exchange_attended(attended, w_half)
    merged, rounded, latent_parts = merge(att_all, w_half, w_other, hidden_in, depth_in)
    latent_parts, att_other, rounded_other = exchange_latent(latent_parts, att_all, rounded)
    before = jnp.concatenate(
        [jnp.full((depth_frames, 1), -1, jnp.int32), audio_codes[:, :-1]], axis=1
    ).reshape(-1, 1)
    message, grads = depth(
        latent_parts, depth_stack, before, audio_codes.reshape(-1, 1), width, loss_scale
    )
    grads = grads.reshape(CHIPS, 2, TP, -1, DD)
    messages, grads_other = exchange_message(message, grads)
    cotangent_parts, side, grads = unmerge(
        messages,
        merged,
        rounded,
        rounded_other,
        att_all,
        att_other,
        w_half,
        w_other,
        grads_other,
        grads,
        depth_in,
    )
    cotangent_parts, side = exchange_cotangent(cotangent_parts, side.reshape(4, 2, 32, -1))

    cosine, sine = angle_tables(chip * FR2, FR2)
    key_parts, query_grad, side = attend_back(
        probs, kv_all, query_two, cotangent_parts, out_t, inverse, cosine, sine, side
    )
    key_parts, grads_z, side_in, normed_other = exchange_key_grads(
        key_parts, grads.reshape(CHIPS, 2, 4, -1, DD), side, normed
    )
    parts, grads, grad_win, out_parts = weight_terms(
        key_parts, query_grad, cosine, sine, normed, normed_other, grads_z, side, side_in
    )
    grad_temporal, grad_depth = weight_sum(*exchange_weights(parts, grads, out_parts))
    return grad_temporal.transpose(1, 0, 2), grad_win, grad_depth


def solution(mesh):
    in_specs = (P("seq", None), P(None, None, "tp"), P(), P(), P(("seq", "tp"), None))
    out_specs = (P("seq", None, "tp"), P(("seq", "tp"), None), P(("seq", "tp"), None))
    return jax.shard_map(
        per_device, mesh=mesh, in_specs=in_specs, out_specs=out_specs, check_vma=False
    )
```

```python
import functools
import math

import jax
import jax.numpy as jnp
from jax import lax
from jax.experimental import pallas as pl
from jax.experimental.pallas import tpu as pltpu
from jax.sharding import PartitionSpec as P

HD = 128
DHD = 64
VOCAB = 1024
CHIPS = 8
TP = 8
FR = 256
FR2 = 512
DD = 512
NS = 512

EPSILON = 1e-05
MASKED = -1e30
ROPE_BASE = 10000.0
MIB = 2**20
MESH = pl.DeviceIdType.MESH
F32 = jnp.float32
BF16 = jnp.bfloat16
ANY = pl.BlockSpec(memory_space=pl.ANY)
VMEM = pl.BlockSpec(memory_space=pltpu.VMEM)
HBM = pl.BlockSpec(memory_space=pltpu.HBM)
TP_ORDER = (4, 1, 3, 5, 7, 2, 6)
CHIP_ORDER = (2, 6, 1, 4, 3, 7, 5)
LOG_SCALE = math.log2(math.e) / math.sqrt(HD)
Z_EARLY = 3
Z_LATE = CHIPS - Z_EARLY
X_ROWS = 160
Y_ROWS = 224


def dot_nn(left, right):
    return jnp.dot(left, right, preferred_element_type=F32)


def dot_nt(left, right):
    return lax.dot_general(left, right, (((1,), (1,)), ((), ())), preferred_element_type=F32)


def dot_tn(left, right):
    return lax.dot_general(left, right, (((0,), (0,)), ((), ())), preferred_element_type=F32)


def rms_scale(values):
    return lax.rsqrt(jnp.mean(values * values, axis=-1, keepdims=True) + EPSILON)


def norm_back(values, scaling, gradient):
    inner_mean = jnp.mean(gradient * values, axis=-1, keepdims=True)
    return scaling * (gradient - values * (scaling * scaling) * inner_mean)


def angle_tables(first, count):
    half_width = HD // 2
    frequency = ROPE_BASE ** (-jnp.arange(half_width).astype(F32) / half_width)
    positions = (first + jnp.arange(count)).astype(F32)
    angles = positions[:, None] * frequency[None, :]
    return jnp.cos(angles), jnp.sin(angles)


def place():
    seq = lax.axis_index("seq")
    tp = lax.axis_index("tp")
    return seq, seq // 2, seq % 2, tp


def run_exchange(
    peers, jobs, locals_, send_sems, recv_sems, forwards=(), relay=None, relay_after=()
):
    barrier = pltpu.get_barrier_semaphore()
    for peer in peers:
        pl.semaphore_signal(barrier, inc=1, device_id=peer, device_id_type=MESH)
    pl.semaphore_wait(barrier, len(peers))
    copies = []

    def begin(source, target, device, *when):
        number = len(copies)
        copy = pltpu.make_async_remote_copy(
            src_ref=source,
            dst_ref=target,
            send_sem=send_sems.at[number],
            recv_sem=recv_sems.at[number],
            device_id=device,
            device_id_type=MESH,
        )
        if when:
            pl.when(when[0])(copy.start)
        else:
            copy.start()
        copies.append((copy, when))

    for job in jobs:
        begin(*job)
    for source, bounce, target, sem in locals_:
        copy = pltpu.make_async_copy(source, bounce, sem)
        copy.start()
        copy.wait()
        copy = pltpu.make_async_copy(bounce, target, sem)
        copy.start()
        copy.wait()
    arrived = set()
    for number, job in forwards:
        copies[number][0].wait_recv()
        arrived.add(number)
        begin(*job)
    if relay is not None:
        for number in relay_after:
            copies[number][0].wait_recv()
            arrived.add(number)
        relay(len(copies), send_sems, recv_sems)
    for number, (copy, when) in enumerate(copies):
        if when:
            pl.when(when[0])(copy.wait_send)
            pl.when(when[1])(copy.wait_recv)
        else:
            copy.wait_send()
            if number not in arrived:
                copy.wait_recv()


def exchange(kernel, name, collective_id, ins, outs, copies, bounces):
    return pl.pallas_call(
        kernel,
        name=name,
        out_shape=outs,
        in_specs=[ANY] * len(ins),
        out_specs=[ANY] * len(outs),
        scratch_shapes=[
            pltpu.SemaphoreType.DMA((copies,)),
            pltpu.SemaphoreType.DMA((copies,)),
            pltpu.SemaphoreType.DMA,
        ]
        + [pltpu.VMEM(shape, dtype) for shape, dtype in bounces],
        compiler_params=pltpu.CompilerParams(
            collective_id=collective_id, has_side_effects=True, vmem_limit_bytes=4 * MIB
        ),
    )(*ins)


RELAY_COPIES = 23


def relay_blocks(own, slot, mirrored, base, send_sems, recv_sems):
    seq, chip, core, tp = place()
    at_x, at_y = chip // 2, chip % 2
    column = 3 - at_x if mirrored else at_x
    line = 1 - at_y if mirrored else at_y

    def real(x):
        return 3 - x if mirrored else x

    def block(source, item):
        row = 1 - at_y if item == 2 else at_y
        return slot(real(source) * 2 + row, 0 if item == 0 else 1)

    def copy(number, source, target, x, y):
        return pltpu.make_async_remote_copy(
            src_ref=source,
            dst_ref=target,
            send_sem=send_sems.at[base + number],
            recv_sem=recv_sems.at[base + number],
            device_id=(x * 4 + y * 2 + core, tp),
            device_id_type=MESH,
        )

    paths = ((0, 1), (0, 3), (0, 2), (1, 2), (1, 3), (2, 3))
    hops = {}
    for at, (source, target) in enumerate(paths):
        relayed = (source, target) in ((0, 2), (1, 3))
        for item in range(3):
            there = block(source, item)
            here = there if relayed or item == 2 else own(item)
            hops[source, target, item] = copy(at * 3 + item, here, there, real(target), at_y)
    across_a = copy(18, own(0), slot(chip, 0), at_x, 1 - at_y)
    across_b = copy(19, own(1), slot(chip, 1), at_x, 1 - at_y)
    across = [
        copy(20 + source, block(source, 0), block(source, 0), at_x, 1 - at_y)
        for source in range(3)
    ]
    sends_b = (line == 0) | (column < 3)
    gets_b = (line == 1) | (column < 3)
    pl.when(line == 0)(across_a.start)
    pl.when(sends_b)(across_b.start)

    def begin(items):
        for at in range(3):

            @pl.when(column == at)
            def _():
                for item in items:
                    hops[at, at + 1, item].start()
                    if at == 0:
                        hops[0, 3, item].start()

    begin((0, 1))
    pl.when(gets_b)(across_b.wait_recv)
    begin((2,))

    @pl.when(column == 1)
    def _():
        for item in range(3):
            hops[0, 1, item].wait_recv()
            if item == 0:
                across[0].start()

    @pl.when(column == 2)
    def _():
        for item in range(3):
            hops[1, 2, item].wait_recv()
            hops[1, 3, item].start()
            if item == 0:
                across[1].start()
        for item in range(3):
            hops[0, 2, item].wait_recv()
            if item == 0:
                across[0].start()

    @pl.when(column == 3)
    def _():
        for item in range(3):
            hops[0, 3, item].wait_recv()
            hops[0, 2, item].start()
            if item == 0:
                across[0].start()
        for source in (2, 1):
            for item in range(3):
                hops[source, 3, item].wait_recv()
                if item == 0:
                    across[source].start()

    pl.when(line == 0)(across_a.wait_send)
    pl.when(line == 1)(across_a.wait_recv)
    pl.when(sends_b)(across_b.wait_send)
    sent = (((0, 1), (0, 3)), ((1, 2),), ((2, 3), (1, 3)), ((0, 2),))
    for at in range(4):

        @pl.when(column == at)
        def _():
            for source, target in sent[at]:
                for item in range(3):
                    hops[source, target, item].wait_send()
            for source in range(at):
                across[source].wait()


def near_peers(seq, chip, core, tp):
    x, y = chip // 2, chip % 2
    return [
        (lax.rem(x + 1, 4) * 4 + y * 2 + core, tp),
        (lax.rem(x + 3, 4) * 4 + y * 2 + core, tp),
        (x * 4 + (1 - y) * 2 + core, tp),
        (x * 4 + y * 2 + 1 - core, tp),
    ]


def tp_peers(seq, tp, order=TP_ORDER):
    return [(seq, lax.rem(tp + hop, TP)) for hop in order]


def chip_peers(chip, core, tp, order=CHIP_ORDER):
    return [(lax.rem(chip + hop, CHIPS) * 2 + core, tp) for hop in order]


def keys_kernel(
    kv, query, out_w, kv_all, query_two, w_half, send_sems, recv_sems, sem, kv_bounce, query_bounce, w_bounce
):
    seq, chip, core, tp = place()
    peers = near_peers(seq, chip, core, tp)
    partner = peers[-1]
    half = pl.ds(core * FR, FR)
    jobs = [(kv.at[1 - core], kv_all.at[chip, core], partner)]
    jobs.append((query.at[1 - core], query_two.at[core], partner))
    for other in tp_peers(seq, tp):
        peers.append(other)
        jobs.append((out_w.at[other[1], half], w_half.at[tp], other))

    def relay(base, send_sems, recv_sems):
        relay_blocks(
            lambda part: kv_all.at[chip, part],
            lambda source, part: kv_all.at[source, part],
            False,
            base,
            send_sems,
            recv_sems,
        )

    run_exchange(
        peers,
        jobs,
        [
            (kv.at[core], kv_bounce, kv_all.at[chip, core], sem),
            (query.at[core], query_bounce, query_two.at[core], sem),
            (out_w.at[tp, half], w_bounce, w_half.at[tp], sem),
        ],
        send_sems,
        recv_sems,
        relay=relay,
        relay_after=(0,),
    )


def exchange_keys(kv, query, out_w):
    return exchange(
        keys_kernel,
        "exchange_keys",
        1,
        (kv, query, out_w),
        [
            jax.ShapeDtypeStruct((CHIPS, 2, FR, 2 * HD), BF16),
            jax.ShapeDtypeStruct((2, FR, HD), BF16),
            jax.ShapeDtypeStruct((TP, FR, 2 * HD), BF16),
        ],
        9 + RELAY_COPIES,
        [((FR, 2 * HD), BF16), ((FR, HD), BF16), ((FR, 2 * HD), BF16)],
    )


def attended_kernel(source, w_half, target, w_other, send_sems, recv_sems, sem, bounce):
    seq, chip, core, tp = place()
    slot = tp * 2 + core
    partner_seq = chip * 2 + 1 - core
    partner = (partner_seq, tp)
    peers = [partner] + tp_peers(seq, tp) + tp_peers(partner_seq, tp)
    own = pl.ds(core * FR, FR)
    other = pl.ds((1 - core) * FR, FR)
    rows = [other] + [own] * (TP - 1) + [other] * (TP - 1)
    jobs = [(source.at[part], target.at[slot], peer) for part, peer in zip(rows, peers)]
    jobs.append((w_half, w_other, partner))
    run_exchange(
        peers, jobs, [(source.at[own], bounce, target.at[slot], sem)], send_sems, recv_sems
    )


def exchange_attended(attended, w_half):
    return exchange(
        attended_kernel,
        "exchange_attended",
        2,
        (attended, w_half),
        [
            jax.ShapeDtypeStruct((2 * TP, FR, HD), BF16),
            jax.ShapeDtypeStruct(w_half.shape, BF16),
        ],
        16,
        [((FR, HD), BF16)],
    )


def latent_kernel(
    source, att_all, merged, target, att_other, merged_other, send_sems, recv_sems, sem, bounce
):
    seq, chip, core, tp = place()
    partner = (chip * 2 + 1 - core, tp)
    peers = tp_peers(seq, tp)
    jobs = [(source.at[peer[1]], target.at[tp], peer) for peer in peers]
    jobs.append((att_all, att_other, partner))
    jobs.append((merged, merged_other, partner))
    run_exchange(
        peers + [partner],
        jobs,
        [(source.at[tp], bounce, target.at[tp], sem)],
        send_sems,
        recv_sems,
    )


def exchange_latent(parts, att_all, merged):
    return exchange(
        latent_kernel,
        "exchange_latent",
        3,
        (parts, att_all, merged),
        [
            jax.ShapeDtypeStruct(parts.shape, parts.dtype),
            jax.ShapeDtypeStruct(att_all.shape, BF16),
            jax.ShapeDtypeStruct(merged.shape, BF16),
        ],
        9,
        [(parts.shape[1:], parts.dtype)],
    )


def message_kernel(source, grads, target, grads_other, send_sems, recv_sems, sem, bounce):
    seq, chip, core, tp = place()
    partner = (chip * 2 + 1 - core, tp)
    peers = tp_peers(seq, tp)
    jobs = [(source, target.at[core, tp], peer) for peer in peers]
    forwards = []
    for number, hop in enumerate(TP_ORDER):
        slot = target.at[core, lax.rem(tp - hop + TP, TP)]
        forwards.append((number, (slot, slot, partner)))
    jobs.append((source, target.at[core, tp], partner))
    jobs.append((grads.at[:, 1 - core], grads_other, partner))
    run_exchange(
        peers + [partner],
        jobs,
        [(source, bounce, target.at[core, tp], sem)],
        send_sems,
        recv_sems,
        forwards,
    )


def exchange_message(message, grads):
    return exchange(
        message_kernel,
        "exchange_message",
        4,
        (message, grads),
        [
            jax.ShapeDtypeStruct((2, TP) + message.shape, message.dtype),
            jax.ShapeDtypeStruct((CHIPS, TP) + grads.shape[3:], BF16),
        ],
        16,
        [(message.shape, message.dtype)],
    )


def cotangent_kernel(
    source, side, grads, target, side_x, grads_z, send_sems, recv_sems, sem, bounce, side_bounce, grads_bounce
):
    seq, chip, core, tp = place()
    partner_seq = chip * 2 + 1 - core
    at_x, at_y = chip // 2, chip % 2
    row, depth_at = tp // 4, tp % 4
    peers = [(partner_seq, tp)] + tp_peers(seq, tp) + tp_peers(partner_seq, tp)
    heads = [1 - core] + [core] * (TP - 1) + [1 - core] * (TP - 1)
    jobs = [
        (source.at[peer[1] * 2 + head], target.at[core, tp], peer)
        for head, peer in zip(heads, peers)
    ]
    for hop in (2, 1, 3):
        there = lax.rem(at_x + hop, 4)
        other = (there * 4 + at_y * 2 + core, tp)
        peers.append(other)
        jobs.append((side.at[there], side_x.at[at_x], other))
    early = pl.ds(0, Z_EARLY)
    for hop in (2, 1, 3):
        there = lax.rem(depth_at + hop, 4)
        other = (seq, row * 4 + there)
        jobs.append((grads.at[early, :, there], grads_z.at[depth_at], other))
    run_exchange(
        peers,
        jobs,
        [
            (source.at[tp * 2 + core], bounce, target.at[core, tp], sem),
            (side.at[at_x], side_bounce, side_x.at[at_x], sem),
            (grads.at[early, :, depth_at], grads_bounce, grads_z.at[depth_at], sem),
        ],
        send_sems,
        recv_sems,
    )


def exchange_cotangent(parts, side, grads):
    slab = (Z_EARLY, 2) + grads.shape[3:]
    return exchange(
        cotangent_kernel,
        "exchange_cotangent",
        5,
        (parts, side, grads),
        [
            jax.ShapeDtypeStruct((2, TP, FR, HD), BF16),
            jax.ShapeDtypeStruct(side.shape, BF16),
            jax.ShapeDtypeStruct((4,) + slab, BF16),
        ],
        21,
        [((FR, HD), BF16), (side.shape[1:], BF16), (slab, BF16)],
    )


def grads_kernel(
    pair, stats, grads, side, normed, pair_all, stats_all, grads_z, side_in, normed_other,
    send_sems, recv_sems, sem, bounce, stats_bounce, grads_bounce,
):
    seq, chip, core, tp = place()
    row, depth_at = tp // 4, tp % 4
    at_x, at_y = chip // 2, chip % 2
    peers = []
    jobs = []
    for hop in CHIP_ORDER:
        there = lax.rem(chip + hop, CHIPS)
        here = lax.rem(chip - hop + CHIPS, CHIPS)
        other = (there * 2 + core, tp)
        peers.append(other)
        jobs.append((stats, stats_all.at[chip], other, there < chip, here > chip))
    for hop in (2, 1, 3):
        there = lax.rem(depth_at + hop, 4)
        other = (seq, row * 4 + there)
        peers.append(other)
        jobs.append((grads.at[pl.ds(Z_EARLY, Z_LATE), :, there], grads_z.at[depth_at], other))
    jobs.append((side.at[1 - at_y], side_in, (at_x * 4 + (1 - at_y) * 2 + core, tp)))
    partner = (chip * 2 + 1 - core, tp)
    jobs.append((normed, normed_other, partner))
    peers.append(partner)

    def relay(base, send_sems, recv_sems):
        relay_blocks(
            lambda part: pair.at[part],
            lambda source, part: pair_all.at[source, part],
            True,
            base,
            send_sems,
            recv_sems,
        )

    run_exchange(
        peers,
        jobs,
        [
            (pair, bounce, pair_all.at[chip], sem),
            (stats, stats_bounce, stats_all.at[chip], sem),
            (
                grads.at[pl.ds(Z_EARLY, Z_LATE), :, depth_at],
                grads_bounce,
                grads_z.at[depth_at],
                sem,
            ),
        ],
        send_sems,
        recv_sems,
        relay=relay,
    )


def exchange_grads(pair, stats, grads, side, normed):
    slab = (Z_LATE, 2) + grads.shape[3:]
    return exchange(
        grads_kernel,
        "exchange_grads",
        6,
        (pair, stats, grads, side, normed),
        [
            jax.ShapeDtypeStruct((CHIPS,) + pair.shape, BF16),
            jax.ShapeDtypeStruct((CHIPS,) + stats.shape, F32),
            jax.ShapeDtypeStruct((4,) + slab, BF16),
            jax.ShapeDtypeStruct(side.shape[1:], BF16),
            jax.ShapeDtypeStruct(normed.shape, BF16),
        ],
        12 + RELAY_COPIES,
        [(pair.shape, BF16), (stats.shape, F32), (slab, BF16)],
    )


def first_kernel(
    x_first, y_first, grads, out, x_in, y_in, grads_x, out_all,
    send_sems, recv_sems, sem, x_bounce, y_bounce, grads_bounce, out_bounce,
):
    seq, chip, core, tp = place()
    at_x, at_y = chip // 2, chip % 2

    def device(x, y, c):
        return x * 4 + y * 2 + c, tp

    peers = []
    jobs = []
    for hop in (2, 1, 3):
        x = lax.rem(at_x + hop, 4)
        for c in (core, 1 - core):
            peers.append(device(x, at_y, c))
            jobs.append((x_first.at[x, c], x_in.at[at_x, core], peers[-1]))
    for c in (core, 1 - core):
        peers.append(device(at_x, 1 - at_y, c))
        jobs.append((y_first.at[1 - at_y, c], y_in.at[at_y, core], peers[-1]))
    for hop in (2, 1, 3):
        x = lax.rem(at_x + hop, 4)
        jobs.append((grads.at[x], grads_x.at[at_x], device(x, at_y, core)))
    for other in tp_peers(seq, tp):
        peers.append(other)
        jobs.append((out.at[other[1]], out_all.at[tp], other))
    peers.append(device(at_x, at_y, 1 - core))
    jobs.append((x_first.at[at_x, 1 - core], x_in.at[at_x, core], peers[-1]))
    jobs.append((y_first.at[at_y, 1 - core], y_in.at[at_y, core], peers[-1]))
    run_exchange(
        peers,
        jobs,
        [
            (x_first.at[at_x, core], x_bounce, x_in.at[at_x, core], sem),
            (y_first.at[at_y, core], y_bounce, y_in.at[at_y, core], sem),
            (grads.at[at_x], grads_bounce, grads_x.at[at_x], sem),
            (out.at[tp], out_bounce, out_all.at[tp], sem),
        ],
        send_sems,
        recv_sems,
    )


def exchange_first(x_first, y_first, grads, out):
    arrays = (x_first, y_first, grads, out)
    tails = (x_first.shape[2:], y_first.shape[2:], grads.shape[1:], out.shape[1:])
    return exchange(
        first_kernel,
        "exchange_first",
        7,
        arrays,
        [jax.ShapeDtypeStruct(array.shape, BF16) for array in arrays],
        20,
        [(tail, BF16) for tail in tails],
    )


def second_kernel(
    x_sum, y_sum, grads, x_in, y_in, grads_in, send_sems, recv_sems, sem, y_bounce, grads_bounce
):
    seq, chip, core, tp = place()
    at_x, at_y = chip // 2, chip % 2
    row, depth_at = tp // 4, tp % 4
    peers = []
    jobs = []
    for hop in (2, 1, 3):
        x = lax.rem(at_x + hop, 4)
        peers.append((x * 4 + at_y * 2 + core, tp))
        jobs.append((y_sum.at[x], y_in.at[at_x], peers[-1]))
    peers.append((at_x * 4 + (1 - at_y) * 2 + core, tp))
    jobs.append((x_sum.at[1 - at_y], x_in, peers[-1]))
    jobs.append((grads.at[1 - at_y, row], grads_in.at[at_y, row], peers[-1]))
    for y in (at_y, 1 - at_y):
        peers.append((at_x * 4 + y * 2 + core, (1 - row) * 4 + depth_at))
        jobs.append((grads.at[y, 1 - row], grads_in.at[at_y, row], peers[-1]))
    run_exchange(
        peers,
        jobs,
        [
            (y_sum.at[at_x], y_bounce, y_in.at[at_x], sem),
            (grads.at[at_y, row], grads_bounce, grads_in.at[at_y, row], sem),
        ],
        send_sems,
        recv_sems,
    )


def exchange_second(x_sum, y_sum, grads):
    return exchange(
        second_kernel,
        "exchange_second",
        8,
        (x_sum, y_sum, grads),
        [
            jax.ShapeDtypeStruct(x_sum.shape[1:], BF16),
            jax.ShapeDtypeStruct(y_sum.shape, BF16),
            jax.ShapeDtypeStruct(grads.shape, BF16),
        ],
        7,
        [(y_sum.shape[1:], BF16), (grads.shape[2:], BF16)],
    )


def compute(kernel, name, ins, outs, scratch=(), limit=48, hbm=0):
    return pl.pallas_call(
        kernel,
        name=name,
        out_shape=outs,
        in_specs=[VMEM] * (len(ins) - hbm) + [HBM] * hbm,
        out_specs=[VMEM] * len(outs),
        scratch_shapes=list(scratch),
        compiler_params=pltpu.CompilerParams(vmem_limit_bytes=limit * MIB),
    )(*ins)


def start_kernel(
    hidden_ref, w_ref, cos_ref, sin_ref, normed_ref, kv_ref, query_ref, out_w_ref, total_ref
):
    step = pl.program_id(0)
    own = pl.ds(pl.multiple_of(lax.axis_index("seq") % 2 * FR, FR), FR)
    depth_rows = w_ref.shape[0]

    @pl.when(step == 0)
    def _():
        hidden = hidden_ref[...].astype(F32)
        normed_ref[...] = (hidden * rms_scale(hidden)).astype(BF16)
        total_ref[...] = jnp.zeros_like(total_ref)

    normed = normed_ref[:, pl.ds(pl.multiple_of(step * depth_rows, depth_rows), depth_rows)]
    weights = w_ref[...].reshape(depth_rows, 8 * HD)
    total_ref[...] += dot_nn(normed, weights[:, : 6 * HD])
    out_w = weights[:, 6 * HD :].reshape(-1, TP, 32, 2 * HD)
    for at in range(TP):
        for piece in range(out_w.shape[0]):
            out_w_ref[at, piece * 32 : (piece + 1) * 32] = out_w[piece, at]

    @pl.when(step == pl.num_programs(0) - 1)
    def _():
        cosine, sine = cos_ref[own], sin_ref[own]

        def turned(at):
            lower = total_ref[:, at : at + HD // 2]
            upper = total_ref[:, at + HD // 2 : at + HD]
            return jnp.concatenate(
                [lower * cosine - upper * sine, upper * cosine + lower * sine], axis=1
            ).astype(BF16)

        for head in range(2):
            query_ref[head] = turned(head * HD)
            kv_ref[head, :, :HD] = turned((2 + head) * HD)
            at = (4 + head) * HD
            kv_ref[head, :, HD:] = total_ref[:, at : at + HD].astype(BF16)


def start(hidden, weights, cosine, sine):
    steps = 8
    depth_rows = weights.shape[0] // steps

    def whole(*shape):
        return pl.BlockSpec(shape, lambda step: (0,) * len(shape))

    return pl.pallas_call(
        start_kernel,
        name="start",
        grid=(steps,),
        out_shape=[
            jax.ShapeDtypeStruct(hidden.shape, BF16),
            jax.ShapeDtypeStruct((2, FR, 2 * HD), BF16),
            jax.ShapeDtypeStruct((2, FR, HD), BF16),
            jax.ShapeDtypeStruct((TP, NS, 2 * HD), BF16),
        ],
        in_specs=[
            whole(*hidden.shape),
            pl.BlockSpec((depth_rows, 4, 2 * HD), lambda step: (step, 0, 0)),
            whole(*cosine.shape),
            whole(*sine.shape),
        ],
        out_specs=[
            whole(*hidden.shape),
            whole(2, FR, 2 * HD),
            whole(2, FR, HD),
            pl.BlockSpec((TP, depth_rows // TP, 2 * HD), lambda step: (0, step, 0)),
        ],
        scratch_shapes=[pltpu.VMEM((FR, 6 * HD), F32)],
        compiler_params=pltpu.CompilerParams(vmem_limit_bytes=24 * MIB),
    )(hidden, weights, cosine, sine)


def attend_kernel(kv_ref, query_ref, out_ref, out_t_ref, level_ref, score_ref):
    chip = lax.axis_index("seq") // 2
    query = query_ref[...]
    key_at = lax.broadcasted_iota(jnp.int32, (FR2, FR2), 0)
    query_at = lax.broadcasted_iota(jnp.int32, (FR2, FR2), 1)

    def scores(block, top):
        score = dot_nt(kv_ref[block, :, :HD], query) * LOG_SCALE
        score_ref[block] = score
        return jnp.maximum(top, jnp.max(score, axis=0, keepdims=True))

    score = dot_nt(kv_ref[chip, :, :HD], query) * LOG_SCALE
    score = jnp.where(key_at <= query_at, score, MASKED)
    score_ref[chip] = score
    top = lax.fori_loop(0, chip, scores, jnp.max(score, axis=0, keepdims=True))

    def weigh(block, carry):
        total, mixed = carry
        prob = jnp.exp2(score_ref[block] - top)
        total = total + jnp.sum(prob, axis=0, keepdims=True)
        return total, mixed + dot_tn(kv_ref[block, :, HD:], prob.astype(BF16))

    total, mixed = lax.fori_loop(
        0, chip + 1, weigh, (jnp.zeros((1, FR2), F32), jnp.zeros((HD, FR2), F32))
    )
    mixed = mixed * (1.0 / total)
    out_t_ref[...] = mixed
    level_ref[...] = top + jnp.log2(total)
    out_ref[...] = mixed.T.astype(BF16)


def attend(kv_all, query):
    return compute(
        attend_kernel,
        "attend",
        (kv_all, query),
        [
            jax.ShapeDtypeStruct((FR2, HD), BF16),
            jax.ShapeDtypeStruct((HD, FR2), F32),
            jax.ShapeDtypeStruct((1, FR2), F32),
        ],
        [pltpu.VMEM((CHIPS, FR2, FR2), F32)],
        limit=20,
    )


def fetch(source, target, sem):
    copy = pltpu.make_async_copy(source, target, sem)
    copy.start()
    return copy


def order_halves(core, mine, other):
    return jnp.where(core == 0, mine, other), jnp.where(core == 0, other, mine)


def merge_kernel(
    att_ref, half_ref, other_ref, hidden_ref, depth_in_hbm, merged_ref, round_ref, part_ref, depth_in_ref, sem
):
    seq, chip, core, tp = place()
    copy = fetch(depth_in_hbm.at[:, tp], depth_in_ref, sem)
    width = hidden_ref.shape[1]
    group = width // 2
    row_at = lax.broadcasted_iota(jnp.int32, (group, FR), 0)
    col_at = lax.broadcasted_iota(jnp.int32, (group, FR), 1)
    wanted = (col_at // 32) * 256 + tp * 32 + col_at % 32
    pick = jnp.where(row_at == wanted, 1.0, 0.0).astype(BF16)
    merged = jnp.concatenate(
        [dot_nn(hidden_ref[:, :group], pick), dot_nn(hidden_ref[:, group:], pick)], axis=1
    )
    mine = jnp.zeros((FR, FR), F32)
    other = jnp.zeros((FR, FR), F32)
    for at in range(TP):
        pair = jnp.concatenate([att_ref[2 * at], att_ref[2 * at + 1]], axis=1)
        mine = mine + dot_nt(pair, half_ref[at])
        other = other + dot_nt(pair, other_ref[at])
    merged = merged + jnp.concatenate(order_halves(core, mine, other), axis=1)
    rounded = merged.astype(BF16)
    merged_ref[...] = merged
    round_ref[...] = rounded
    squares = jnp.sum(merged * merged, axis=-1, keepdims=True)
    copy.wait()
    latent = dot_nn(rounded, depth_in_ref[...].reshape(NS, DD))
    coarse = squares.astype(BF16)
    fine = (squares - coarse.astype(F32)).astype(BF16)
    part_ref[:, :, :DD] = latent.astype(BF16).reshape(TP, FR // TP, DD)
    part_ref[:, :, DD : DD + HD] = jnp.broadcast_to(coarse, (FR, HD)).reshape(TP, FR // TP, HD)
    part_ref[:, :, DD + HD :] = jnp.broadcast_to(fine, (FR, HD)).reshape(TP, FR // TP, HD)


def merge(att_all, w_half, w_other, hidden, depth_in):
    return compute(
        merge_kernel,
        "merge",
        (att_all, w_half, w_other, hidden, depth_in),
        [
            jax.ShapeDtypeStruct((FR, NS), F32),
            jax.ShapeDtypeStruct((FR, NS), BF16),
            jax.ShapeDtypeStruct((TP, FR // TP, DD + 2 * HD), BF16),
        ],
        [pltpu.VMEM((2 * CHIPS, 32, DD), BF16), pltpu.SemaphoreType.DMA],
        hbm=1,
        limit=24,
    )


def depth_kernel(
    width, loss_scale, part_ref, code_ref, stack_hbm, message_ref, grad_ref, prob_ref, stack_ref, sems
):
    frames, books = code_ref.shape
    pieces = ((3072, 1024), (0, 1536), (1536, 512), (2048, 1024))
    copies = [
        fetch(stack_hbm.at[pl.ds(low, rows)], stack_ref.at[pl.ds(low, rows)], sems.at[at])
        for at, (low, rows) in enumerate(pieces)
    ]
    grid = (frames, books, books)
    row_at = lax.broadcasted_iota(jnp.int32, grid, 1)
    col_at = lax.broadcasted_iota(jnp.int32, grid, 2)
    spread = jnp.broadcast_to(code_ref[...][:, None, :], grid)

    def column(wanted):
        picked = jnp.where(wanted, spread + 1, 0).astype(F32)
        picked = jnp.sum(picked, axis=-1, keepdims=True).reshape(frames * books, 1)
        return picked - 1.0

    codes = column(col_at == row_at)
    before = column(col_at == row_at - 1)
    tokens = frames * books
    total = jnp.sum(part_ref[...].astype(F32), axis=0)
    raw = total[:, :DD]
    squares = total[:, DD : DD + 1] + total[:, DD + HD : DD + HD + 1]
    scale_in = lax.rsqrt(squares * (1.0 / width) + EPSILON)
    latent = raw * scale_in
    latent = jnp.broadcast_to(latent[:, None, :], (frames, books, DD)).reshape(tokens, DD)
    vocab_at = lax.broadcasted_iota(jnp.int32, (tokens, VOCAB), 1).astype(F32)
    hot = jnp.where(before == vocab_at, 1.0, 0.0).astype(BF16)
    copies[0].wait()
    stream = latent + dot_nn(hot, stack_ref[4 * DD + VOCAB :])
    stream_scale = rms_scale(stream)
    stream_norm = (stream * stream_scale).astype(BF16)
    copies[1].wait()
    qkv_rows = stack_ref[: 3 * DD]
    proj = dot_nt(stream_norm, qkv_rows).astype(BF16)
    row_at = lax.broadcasted_iota(jnp.int32, (tokens, tokens), 0)
    col_at = lax.broadcasted_iota(jnp.int32, (tokens, tokens), 1)
    allowed = (row_at // books == col_at // books) & (col_at <= row_at)
    depth_scale = 1.0 / math.sqrt(DHD)
    mixed = []
    for head in range(DD // DHD):
        low = head * DHD
        queries = proj[:, low : low + DHD]
        keys = proj[:, DD + low : DD + low + DHD]
        values = proj[:, 2 * DD + low : 2 * DD + low + DHD]
        scores = jnp.where(allowed, dot_nt(queries, keys) * depth_scale, MASKED)
        weights = jnp.exp(scores - jnp.max(scores, axis=-1, keepdims=True))
        probs = weights / jnp.sum(weights, axis=-1, keepdims=True)
        prob_ref[head] = probs
        mixed.append(dot_nn(probs.astype(BF16), values))
    mixed = jnp.concatenate(mixed, axis=1).astype(BF16)
    copies[2].wait()
    out_rows = stack_ref[3 * DD : 4 * DD]
    resid = stream + dot_nt(mixed, out_rows)
    resid_scale = rms_scale(resid)
    resid_norm = (resid * resid_scale).astype(BF16)
    copies[3].wait()
    head_rows = stack_ref[4 * DD : 4 * DD + VOCAB]
    logits = dot_nt(resid_norm, head_rows)
    weights = jnp.exp(logits - jnp.max(logits, axis=-1, keepdims=True))
    logit_probs = weights / jnp.sum(weights, axis=-1, keepdims=True)
    target = jnp.where(codes == vocab_at, 1.0, 0.0)
    logit_grad = ((logit_probs - target) * loss_scale).astype(BF16)
    grad_ref[4 * DD : 4 * DD + VOCAB] = dot_tn(logit_grad, resid_norm).astype(BF16)
    resid_grad = norm_back(resid, resid_scale, dot_nn(logit_grad, head_rows))
    resid_round = resid_grad.astype(BF16)
    grad_ref[3 * DD : 4 * DD] = dot_tn(resid_round, mixed).astype(BF16)
    mixed_grad = dot_nn(resid_round, out_rows).astype(BF16)
    query_grad, key_grad, value_grad = [], [], []
    for head in range(DD // DHD):
        low = head * DHD
        queries = proj[:, low : low + DHD]
        keys = proj[:, DD + low : DD + low + DHD]
        values = proj[:, 2 * DD + low : 2 * DD + low + DHD]
        probs = prob_ref[head]
        mix_grad = mixed_grad[:, low : low + DHD]
        value_grad.append(dot_tn(probs.astype(BF16), mix_grad))
        prob_grad = dot_nt(mix_grad, values)
        inner = jnp.sum(probs * prob_grad, axis=-1, keepdims=True)
        score_grad = (probs * (prob_grad - inner) * depth_scale).astype(BF16)
        query_grad.append(dot_nn(score_grad, keys))
        key_grad.append(dot_tn(score_grad, queries))
    proj_grad = jnp.concatenate(query_grad + key_grad + value_grad, axis=1).astype(BF16)
    grad_ref[: 3 * DD] = dot_tn(proj_grad, stream_norm).astype(BF16)
    stream_grad = resid_grad + norm_back(stream, stream_scale, dot_nn(proj_grad, qkv_rows))
    grad_ref[4 * DD + VOCAB :] = dot_tn(hot, stream_grad.astype(BF16)).astype(BF16)
    latent_grad = jnp.sum(stream_grad.reshape(frames, books, DD), axis=1)
    latent_grad = latent_grad.astype(BF16).astype(F32)
    inner = jnp.sum(latent_grad * raw, axis=-1, keepdims=True) * (1.0 / width)
    pull = scale_in * scale_in * scale_in * inner
    coarse = pull.astype(BF16)
    fine = (pull - coarse.astype(F32)).astype(BF16)
    message_ref[:, :DD] = (latent_grad * scale_in).astype(BF16)
    message_ref[:, DD : DD + HD] = jnp.broadcast_to(coarse, (frames, HD))
    message_ref[:, DD + HD :] = jnp.broadcast_to(fine, (frames, HD))


def depth(parts, codes, stack, width, loss_scale):
    tokens = codes.shape[0] * codes.shape[1]
    return compute(
        functools.partial(depth_kernel, width, loss_scale),
        "depth",
        (parts, codes, stack),
        [
            jax.ShapeDtypeStruct((parts.shape[1], DD + 2 * HD), BF16),
            jax.ShapeDtypeStruct(stack.shape, BF16),
        ],
        [
            pltpu.VMEM((DD // DHD, tokens, tokens), F32),
            pltpu.VMEM(stack.shape, BF16),
            pltpu.SemaphoreType.DMA((4,)),
        ],
        hbm=1,
        limit=32,
    )


def merged_gradient(message, merged, depth_in):
    pull = message[:, DD : DD + 1].astype(F32) + message[:, DD + HD : DD + HD + 1].astype(F32)
    return dot_nt(message[:, :DD], depth_in) - merged * pull


def unmerge_kernel(
    message_ref,
    merged_ref,
    round_ref,
    round_other_ref,
    att_ref,
    att_other_ref,
    half_ref,
    other_ref,
    grads_other_ref,
    grads_hbm,
    depth_in_hbm,
    part_ref,
    side_ref,
    grads_ref,
    depth_in_ref,
    grads_own_ref,
    sems,
):
    seq, chip, core, tp = place()
    copy = fetch(depth_in_hbm.at[:, tp], depth_in_ref, sems.at[0])
    grads_copy = fetch(grads_hbm.at[:, core], grads_own_ref, sems.at[1])
    copy.wait()
    depth_in = depth_in_ref[...].reshape(NS, DD)
    message = message_ref[core].reshape(FR, DD + 2 * HD)
    message_other = message_ref[1 - core].reshape(FR, DD + 2 * HD)
    gradient = merged_gradient(message, merged_ref[...], depth_in)
    lower, upper = gradient[:, :FR], gradient[:, FR:]
    mine, other = order_halves(core, lower, upper)
    mine, other = mine.astype(BF16), other.astype(BF16)
    for at in range(TP):
        pair = (dot_nn(mine, half_ref[at]) + dot_nn(other, other_ref[at])).astype(BF16)
        part_ref[2 * at] = pair[:, :HD]
        part_ref[2 * at + 1] = pair[:, HD:]
    gradient_other = merged_gradient(
        message_other, round_other_ref[...].astype(F32), depth_in
    )

    def pick_rows(own, others):
        both = jnp.concatenate([own.T, others.T], axis=1).reshape(CHIPS, 2, 32, FR2)
        both = jnp.where(core == 0, both[:, 0], both[:, 1])
        return both.reshape(FR, FR2).astype(BF16)

    rows = pick_rows(gradient, gradient_other)
    for at in range(TP):
        pair = jnp.concatenate([att_ref[2 * at], att_ref[2 * at + 1]], axis=1)
        pair_other = jnp.concatenate([att_other_ref[2 * at], att_other_ref[2 * at + 1]], axis=1)
        term = dot_nn(rows, jnp.concatenate([pair, pair_other], axis=0)).astype(BF16)
        side_ref[:, :, at * FR : (at + 1) * FR] = term.reshape(CHIPS, 32, FR)
    rows = pick_rows(round_ref[...].astype(F32), round_other_ref[...].astype(F32))
    both = jnp.concatenate([message[:, :DD], message_other[:, :DD]], axis=0)
    side_ref[:, :, TP * FR :] = dot_nn(rows, both).astype(BF16).reshape(CHIPS, 32, DD)
    grads_copy.wait()
    for at in range(CHIPS):
        grads_ref[at] = (
            grads_own_ref[at].astype(F32) + grads_other_ref[at].astype(F32)
        ).astype(BF16)


def unmerge(
    messages, merged, rounded, rounded_other, att_all, att_other, w_half, w_other, grads_other, grads, depth_in
):
    return compute(
        unmerge_kernel,
        "unmerge",
        (
            messages,
            merged,
            rounded,
            rounded_other,
            att_all,
            att_other,
            w_half,
            w_other,
            grads_other,
            grads,
            depth_in,
        ),
        [
            jax.ShapeDtypeStruct((2 * TP, FR, HD), BF16),
            jax.ShapeDtypeStruct((CHIPS, 32, TP * FR + DD), BF16),
            jax.ShapeDtypeStruct(grads_other.shape, BF16),
        ],
        [
            pltpu.VMEM((2 * CHIPS, 32, DD), BF16),
            pltpu.VMEM(grads_other.shape, BF16),
            pltpu.SemaphoreType.DMA((2,)),
        ],
        hbm=2,
        limit=28,
    )


def prepare_kernel(
    part_ref, query_ref, out_t_ref, level_ref, side_x_ref, pair_ref, stats_ref, side_ref
):
    gradient = jnp.sum(part_ref[...].astype(F32), axis=1).reshape(FR2, HD).astype(BF16)
    pair_ref[:, :, :HD] = query_ref[...].reshape(2, FR, HD)
    pair_ref[:, :, HD:] = gradient.reshape(2, FR, HD)
    inner = jnp.sum(gradient.astype(F32).T * out_t_ref[...], axis=0, keepdims=True)
    stats_ref[...] = jnp.concatenate(
        [level_ref[...], inner, jnp.zeros((6, FR2), F32)], axis=0
    )
    side_ref[...] = jnp.sum(side_x_ref[...].astype(F32), axis=0).astype(BF16)


def prepare(parts, query, out_t, level, side_x):
    return compute(
        prepare_kernel,
        "prepare",
        (parts, query, out_t, level, side_x),
        [
            jax.ShapeDtypeStruct((2, FR, 2 * HD), BF16),
            jax.ShapeDtypeStruct((8, FR2), F32),
            jax.ShapeDtypeStruct(side_x.shape[1:], BF16),
        ],
        limit=16,
    )


def attend_back_kernel(
    stats_ref, cos_ref, sin_ref, side_ref, side_in_ref, kv_hbm, pair_hbm, early_hbm, late_hbm,
    normed_hbm, other_hbm, x_ref, y_ref, grads_ref, win_ref, out_w_ref,
    kv_ref, pair_ref, early_ref, late_ref, normed_ref, other_ref, sems,
):
    chip = lax.axis_index("seq") // 2
    core = lax.axis_index("seq") % 2
    places = (
        (kv_hbm, kv_ref),
        (pair_hbm, pair_ref),
        (normed_hbm, normed_ref),
        (other_hbm, other_ref),
        (early_hbm, early_ref),
        (late_hbm, late_ref),
    )
    copies = [fetch(source, target, sems.at[at]) for at, (source, target) in enumerate(places)]
    copies[0].wait()
    copies[1].wait()
    scale = 1.0 / math.sqrt(HD)

    def pair(queries, keys, diagonal):
        query = pair_ref[queries, :, :HD]
        gradient = pair_ref[queries, :, HD:]
        score = dot_nt(kv_ref[keys, :, :HD], query) * LOG_SCALE
        if diagonal:
            key_at = lax.broadcasted_iota(jnp.int32, (FR2, FR2), 0)
            query_at = lax.broadcasted_iota(jnp.int32, (FR2, FR2), 1)
            score = jnp.where(key_at <= query_at, score, MASKED)
        prob = jnp.exp2(score - stats_ref[queries, 0:1])
        prob_grad = dot_nt(kv_ref[keys, :, HD:], gradient)
        score_grad = (prob * (prob_grad - stats_ref[queries, 1:2])).astype(BF16)
        return query, gradient, prob.astype(BF16), score_grad

    def own_queries(block, total):
        score_grad = pair(chip, block, False)[3]
        return total + dot_tn(kv_ref[block, :, :HD], score_grad)

    def own_keys(block, totals):
        query, gradient, prob, score_grad = pair(block, chip, False)
        return totals[0] + dot_nn(score_grad, query), totals[1] + dot_nn(prob, gradient)

    query, gradient, prob, score_grad = pair(chip, chip, True)
    query_grad = dot_tn(kv_ref[chip, :, :HD], score_grad)
    key_grad = dot_nn(score_grad, query)
    value_grad = dot_nn(prob, gradient)
    query_grad = lax.fori_loop(0, chip, own_queries, query_grad)
    key_grad, value_grad = lax.fori_loop(chip + 1, CHIPS, own_keys, (key_grad, value_grad))
    query_grad = query_grad.T
    cosine, sine = cos_ref[...] * scale, sin_ref[...] * scale

    def turned(total):
        lower, upper = total[:, : HD // 2], total[:, HD // 2 :]
        return [lower * cosine + upper * sine, upper * cosine - lower * sine]

    proj = jnp.concatenate(turned(query_grad) + turned(key_grad) + [value_grad], axis=1)
    proj_t = proj.T
    own, other = order_halves(core, proj_t[:, :FR], proj_t[:, FR:])
    own, other = own.astype(BF16), other.astype(BF16)
    copies[2].wait()
    copies[3].wait()
    for piece in range(2 * CHIPS):
        low = piece * FR
        term = dot_nn(own, normed_ref[:, low : low + FR])
        term = (term + dot_nn(other, other_ref[:, low : low + FR])).astype(BF16)
        x, y, c = piece // 4, piece // 2 % 2, piece % 2
        x_ref[x, c, y] = term[:X_ROWS]
        y_ref[y, c, x] = term[X_ROWS:]
    copies[4].wait()
    copies[5].wait()
    for at in range(CHIPS):
        term = early_ref[:, at] if at < Z_EARLY else late_ref[:, at - Z_EARLY]
        grads_ref[at] = jnp.sum(term.astype(F32), axis=0).astype(BF16)
    side = side_ref[chip % 2].astype(F32) + side_in_ref[...].astype(F32)
    win_ref[...] = side[:, TP * FR :]
    for at in range(TP):
        out_w_ref[at] = side[:, at * FR : (at + 1) * FR].astype(BF16)


def attend_back(
    stats_all, cosine, sine, side, side_in, kv_all, pair_all, early, late, normed, normed_other
):
    streamed = (kv_all, pair_all, early, late, normed, normed_other)
    return compute(
        attend_back_kernel,
        "attend_back",
        (stats_all, cosine, sine, side, side_in) + streamed,
        [
            jax.ShapeDtypeStruct((4, 2, 2, X_ROWS, FR), BF16),
            jax.ShapeDtypeStruct((2, 2, 4, Y_ROWS, FR), BF16),
            jax.ShapeDtypeStruct((CHIPS,) + late.shape[2:], BF16),
            jax.ShapeDtypeStruct((32, DD), F32),
            jax.ShapeDtypeStruct((TP, 32, FR), BF16),
        ],
        [pltpu.VMEM(array.shape, BF16) for array in streamed] + [pltpu.SemaphoreType.DMA((6,))],
        hbm=6,
        limit=36,
    )


def middle_kernel(x_ref, y_ref, grads_x_ref, x_sum_ref, y_sum_ref, grads_ref):
    for y in range(2):
        for c in range(2):
            terms = [x_ref[x, c, y].astype(F32) for x in range(4)]
            x_sum_ref[y, c] = (terms[0] + terms[1] + terms[2] + terms[3]).astype(BF16)
    for x in range(4):
        for c in range(2):
            term = y_ref[0, c, x].astype(F32) + y_ref[1, c, x].astype(F32)
            y_sum_ref[x, c] = term.astype(BF16)
    grads_ref[...] = jnp.sum(grads_x_ref[...].astype(F32), axis=0).astype(BF16)


def middle_sum(x_in, y_in, grads_x):
    return compute(
        middle_kernel,
        "middle_sum",
        (x_in, y_in, grads_x),
        [
            jax.ShapeDtypeStruct((2, 2, X_ROWS, FR), BF16),
            jax.ShapeDtypeStruct((4, 2, Y_ROWS, FR), BF16),
            jax.ShapeDtypeStruct(grads_x.shape[1:], BF16),
        ],
        limit=16,
    )


def last_kernel(x_own_ref, x_in_ref, y_in_ref, grads_ref, out_w_ref, out_ref, depth_ref):
    at_y = lax.axis_index("seq") // 2 % 2
    totals = []
    for head in range(2):
        x_part = x_own_ref[at_y, head].astype(F32) + x_in_ref[head].astype(F32)
        terms = [y_in_ref[x, head].astype(F32) for x in range(4)]
        y_part = terms[0] + terms[1] + terms[2] + terms[3]
        totals.append(jnp.concatenate([x_part, y_part], axis=0).T)
    pieces = [totals[head][:, kind * HD : (kind + 1) * HD] for kind in range(3) for head in range(2)]
    pieces.append(out_w_ref[...].astype(F32).reshape(FR, 2 * HD))
    out_ref[...] = jnp.concatenate(pieces, axis=1).reshape(FR, 4, 2 * HD)
    depth_ref[...] = jnp.sum(jnp.sum(grads_ref[...].astype(F32), axis=0), axis=0)


def last_sum(x_own, x_in, y_in, grads, out_all):
    return compute(
        last_kernel,
        "last_sum",
        (x_own, x_in, y_in, grads, out_all),
        [
            jax.ShapeDtypeStruct((FR, 4, 2 * HD), F32),
            jax.ShapeDtypeStruct(grads.shape[2:], F32),
        ],
        limit=16,
    )


def per_device(hidden_in, temporal_weight_stack, depth_in, depth_stack, audio_codes):
    seq_index = lax.axis_index("seq")
    tp_index = lax.axis_index("tp")
    chip = seq_index // 2
    width = hidden_in.shape[1]
    depth_frames, book_count = audio_codes.shape
    seq_count = 2 * CHIPS
    total_frames = FR * seq_count
    loss_scale = 1.0 / math.sqrt(total_frames * book_count)

    cosine, sine = angle_tables(chip * FR2, FR2)
    normed, kv, query, out_w = start(hidden_in, temporal_weight_stack, cosine, sine)
    kv_all, query, w_half = exchange_keys(kv, query, out_w)
    kv_all = kv_all.reshape(CHIPS, FR2, 2 * HD)
    query = query.reshape(FR2, HD)

    depth_in = depth_in.reshape(seq_count, TP, -1, DD)
    attended, out_t, level = attend(kv_all, query)
    att_all, w_other = exchange_attended(attended, w_half)
    merged, rounded, latent_parts = merge(att_all, w_half, w_other, hidden_in, depth_in)
    latent_parts, att_other, rounded_other = exchange_latent(latent_parts, att_all, rounded)
    message, grads = depth(latent_parts, audio_codes, depth_stack, width, loss_scale)
    grads = grads.reshape(CHIPS, 2, TP, -1, DD)
    messages, grads_other = exchange_message(message, grads)
    cotangent_parts, side, grads = unmerge(
        messages,
        merged,
        rounded,
        rounded_other,
        att_all,
        att_other,
        w_half,
        w_other,
        grads_other,
        grads,
        depth_in,
    )
    grads = grads.reshape(CHIPS, 2, 4, -1, DD)
    cotangent_parts, side, early = exchange_cotangent(
        cotangent_parts, side.reshape(4, 2, 32, -1), grads
    )
    pair, stats, side = prepare(cotangent_parts, query, out_t, level, side)
    pair_all, stats_all, late, side_in, normed_other = exchange_grads(
        pair, stats, grads, side, normed
    )
    x_first, y_first, grads, grad_win, out_parts = attend_back(
        stats_all,
        cosine,
        sine,
        side,
        side_in,
        kv_all,
        pair_all.reshape(CHIPS, FR2, 2 * HD),
        early,
        late,
        normed,
        normed_other,
    )
    x_in, y_in, grads, out_all = exchange_first(
        x_first, y_first, grads.reshape(4, 2, 2, -1, DD), out_parts
    )
    x_own, y_sum, grads = middle_sum(x_in, y_in, grads)
    x_in, y_in, grads = exchange_second(x_own, y_sum, grads)
    grad_temporal, grad_depth = last_sum(x_own, x_in, y_in, grads, out_all)
    return grad_temporal, grad_win, grad_depth


def solution(mesh):
    in_specs = (P("seq", None), P(None, None, "tp"), P(), P(), P(("seq", "tp"), None))
    out_specs = (P("seq", None, "tp"), P(("seq", "tp"), None), P(("seq", "tp"), None))
    return jax.shard_map(
        per_device, mesh=mesh, in_specs=in_specs, out_specs=out_specs, check_vma=False
    )
```

```python
import functools
import math

import jax
import jax.numpy as jnp
from jax import lax
from jax.experimental import pallas as pl
from jax.experimental.pallas import tpu as pltpu
from jax.sharding import PartitionSpec as P

HD = 128
DHD = 64
VOCAB = 1024
CHIPS = 8
TP = 8
FR = 256
FR2 = 512
DD = 512
NS = 512

EPSILON = 1e-05
MASKED = -1e30
ROPE_BASE = 10000.0
MIB = 2**20
MESH = pl.DeviceIdType.MESH
F32 = jnp.float32
BF16 = jnp.bfloat16
ANY = pl.BlockSpec(memory_space=pl.ANY)
VMEM = pl.BlockSpec(memory_space=pltpu.VMEM)
HBM = pl.BlockSpec(memory_space=pltpu.HBM)
TP_ORDER = (4, 1, 3, 5, 7, 2, 6)
CHIP_ORDER = (2, 6, 1, 4, 3, 7, 5)
LOG_SCALE = math.log2(math.e) / math.sqrt(HD)
Z_EARLY = 1
Z_LATE = CHIPS - Z_EARLY
X_ROWS = 160
Y_ROWS = 224


def dot_nn(left, right):
    return jnp.dot(left, right, preferred_element_type=F32)


def dot_nt(left, right):
    return lax.dot_general(left, right, (((1,), (1,)), ((), ())), preferred_element_type=F32)


def dot_tn(left, right):
    return lax.dot_general(left, right, (((0,), (0,)), ((), ())), preferred_element_type=F32)


def rms_scale(values):
    return lax.rsqrt(jnp.mean(values * values, axis=-1, keepdims=True) + EPSILON)


def norm_back(values, scaling, gradient):
    inner_mean = jnp.mean(gradient * values, axis=-1, keepdims=True)
    return scaling * (gradient - values * (scaling * scaling) * inner_mean)


def angle_tables(first, count):
    half_width = HD // 2
    frequency = ROPE_BASE ** (-jnp.arange(half_width).astype(F32) / half_width)
    positions = (first + jnp.arange(count)).astype(F32)
    angles = positions[:, None] * frequency[None, :]
    return jnp.cos(angles), jnp.sin(angles)


def place():
    seq = lax.axis_index("seq")
    tp = lax.axis_index("tp")
    return seq, seq // 2, seq % 2, tp


def run_exchange(
    peers, jobs, locals_, send_sems, recv_sems, forwards=(), relay=None, relay_after=0
):
    barrier = pltpu.get_barrier_semaphore()
    for peer in peers:
        pl.semaphore_signal(barrier, inc=1, device_id=peer, device_id_type=MESH)
    pl.semaphore_wait(barrier, len(peers))
    copies = []
    arrived = set()

    def begin(source, target, device, *when):
        number = len(copies)
        copy = pltpu.make_async_remote_copy(
            src_ref=source,
            dst_ref=target,
            send_sem=send_sems.at[number],
            recv_sem=recv_sems.at[number],
            device_id=device,
            device_id_type=MESH,
        )
        if when:
            pl.when(when[0])(copy.start)
        else:
            copy.start()
        copies.append((copy, when))

    first = jobs if relay is None else jobs[:relay_after]
    for job in first:
        begin(*job)
    if relay is not None:
        total = len(jobs)

        def settle():
            for number in range(relay_after):
                copies[number][0].wait_recv()
                arrived.add(number)

        def go_on():
            for job in jobs[relay_after:]:
                begin(*job)

        finish = relay(total, send_sems, recv_sems, settle, go_on)
    for source, bounce, target, sem in locals_:
        copy = pltpu.make_async_copy(source, bounce, sem)
        copy.start()
        copy.wait()
        copy = pltpu.make_async_copy(bounce, target, sem)
        copy.start()
        copy.wait()
    for number, job in forwards:
        copies[number][0].wait_recv()
        arrived.add(number)
        begin(*job)
    if relay is not None:
        finish()
    for number, (copy, when) in enumerate(copies):
        if when:
            pl.when(when[0])(copy.wait_send)
            pl.when(when[1])(copy.wait_recv)
        else:
            copy.wait_send()
            if number not in arrived:
                copy.wait_recv()


def exchange(kernel, name, collective_id, ins, outs, copies, bounces):
    return pl.pallas_call(
        kernel,
        name=name,
        out_shape=outs,
        in_specs=[ANY] * len(ins),
        out_specs=[ANY] * len(outs),
        scratch_shapes=[
            pltpu.SemaphoreType.DMA((copies,)),
            pltpu.SemaphoreType.DMA((copies,)),
            pltpu.SemaphoreType.DMA,
        ]
        + [pltpu.VMEM(shape, dtype) for shape, dtype in bounces],
        compiler_params=pltpu.CompilerParams(
            collective_id=collective_id, has_side_effects=True, vmem_limit_bytes=4 * MIB
        ),
    )(*ins)


RELAY_COPIES = 23


def relay_blocks(own, slot, mirrored, base, send_sems, recv_sems, settle, go_on):
    seq, chip, core, tp = place()
    at_x, at_y = chip // 2, chip % 2
    column = 3 - at_x if mirrored else at_x
    line = 1 - at_y if mirrored else at_y

    def real(x):
        return 3 - x if mirrored else x

    def block(source, item):
        row = 1 - at_y if item == 2 else at_y
        return slot(real(source) * 2 + row, core if item == 0 else 1 - core)

    def copy(number, source, target, x, y):
        return pltpu.make_async_remote_copy(
            src_ref=source,
            dst_ref=target,
            send_sem=send_sems.at[base + number],
            recv_sem=recv_sems.at[base + number],
            device_id=(x * 4 + y * 2 + core, tp),
            device_id_type=MESH,
        )

    paths = ((0, 1), (0, 3), (0, 2), (1, 2), (1, 3), (2, 3))
    hops = {}
    for at, (source, target) in enumerate(paths):
        relayed = (source, target) in ((0, 2), (1, 3))
        for item in range(3):
            there = block(source, item)
            here = there if relayed or item == 2 else own(item)
            hops[source, target, item] = copy(at * 3 + item, here, there, real(target), at_y)
    across_a = copy(18, own(0), slot(chip, core), at_x, 1 - at_y)
    across_b = copy(19, own(1), slot(chip, 1 - core), at_x, 1 - at_y)
    across = [
        copy(20 + source, block(source, 0), block(source, 0), at_x, 1 - at_y)
        for source in range(3)
    ]
    sends_b = (line == 0) | (column < 3)
    gets_b = (line == 1) | (column < 3)

    def begin(items):
        for at in range(3):

            @pl.when(column == at)
            def _():
                for item in items:
                    hops[at, at + 1, item].start()
                    if at == 0:
                        hops[0, 3, item].start()

    pl.when(line == 0)(across_a.start)
    begin((0,))
    settle()
    pl.when(sends_b)(across_b.start)
    begin((1,))
    go_on()

    def finish():
        finish_relay(
            column, line, sends_b, gets_b, begin, hops, across_a, across_b, across
        )

    return finish


def finish_relay(column, line, sends_b, gets_b, begin, hops, across_a, across_b, across):
    pl.when(gets_b)(across_b.wait_recv)
    begin((2,))

    @pl.when(column == 1)
    def _():
        for item in range(3):
            hops[0, 1, item].wait_recv()
            if item == 0:
                across[0].start()

    @pl.when(column == 2)
    def _():
        for item in range(3):
            hops[1, 2, item].wait_recv()
            hops[1, 3, item].start()
            if item == 0:
                across[1].start()
        for item in range(3):
            hops[0, 2, item].wait_recv()
            if item == 0:
                across[0].start()

    @pl.when(column == 3)
    def _():
        for item in range(3):
            hops[0, 3, item].wait_recv()
            hops[0, 2, item].start()
            if item == 0:
                across[0].start()
        for source in (2, 1):
            for item in range(3):
                hops[source, 3, item].wait_recv()
                if item == 0:
                    across[source].start()

    pl.when(line == 0)(across_a.wait_send)
    pl.when(line == 1)(across_a.wait_recv)
    pl.when(sends_b)(across_b.wait_send)
    sent = (((0, 1), (0, 3)), ((1, 2),), ((2, 3), (1, 3)), ((0, 2),))
    for at in range(4):

        @pl.when(column == at)
        def _():
            for source, target in sent[at]:
                for item in range(3):
                    hops[source, target, item].wait_send()
            for source in range(at):
                across[source].wait()


def near_peers(seq, chip, core, tp):
    x, y = chip // 2, chip % 2
    return [
        (lax.rem(x + 1, 4) * 4 + y * 2 + core, tp),
        (lax.rem(x + 3, 4) * 4 + y * 2 + core, tp),
        (x * 4 + (1 - y) * 2 + core, tp),
        (x * 4 + y * 2 + 1 - core, tp),
    ]


def tp_peers(seq, tp, order=TP_ORDER):
    return [(seq, lax.rem(tp + hop, TP)) for hop in order]


def chip_peers(chip, core, tp, order=CHIP_ORDER):
    return [(lax.rem(chip + hop, CHIPS) * 2 + core, tp) for hop in order]


def keys_kernel(
    kv, query, out_w, kv_all, query_two, w_half, send_sems, recv_sems, sem, kv_bounce, query_bounce, w_bounce
):
    seq, chip, core, tp = place()
    peers = near_peers(seq, chip, core, tp)
    partner = peers[-1]
    half = pl.ds(core * FR, FR)
    jobs = [(kv.at[1 - core], kv_all.at[chip, core], partner)]
    jobs.append((query.at[1 - core], query_two.at[core], partner))
    for other in tp_peers(seq, tp):
        peers.append(other)
        jobs.append((out_w.at[other[1], half], w_half.at[tp], other))

    def relay(*rest):
        return relay_blocks(
            lambda item: kv_all.at[chip, 1 - core] if item else kv.at[core],
            lambda source, part: kv_all.at[source, part],
            False,
            *rest,
        )

    run_exchange(
        peers,
        jobs,
        [
            (kv.at[core], kv_bounce, kv_all.at[chip, core], sem),
            (query.at[core], query_bounce, query_two.at[core], sem),
            (out_w.at[tp, half], w_bounce, w_half.at[tp], sem),
        ],
        send_sems,
        recv_sems,
        relay=relay,
        relay_after=1,
    )


def exchange_keys(kv, query, out_w):
    return exchange(
        keys_kernel,
        "exchange_keys",
        1,
        (kv, query, out_w),
        [
            jax.ShapeDtypeStruct((CHIPS, 2, FR, 2 * HD), BF16),
            jax.ShapeDtypeStruct((2, FR, HD), BF16),
            jax.ShapeDtypeStruct((TP, FR, 2 * HD), BF16),
        ],
        9 + RELAY_COPIES,
        [((FR, 2 * HD), BF16), ((FR, HD), BF16), ((FR, 2 * HD), BF16)],
    )


def attended_kernel(source, w_half, target, w_other, send_sems, recv_sems, sem, bounce):
    seq, chip, core, tp = place()
    slot = tp * 2 + core
    partner_seq = chip * 2 + 1 - core
    partner = (partner_seq, tp)
    peers = [partner] + tp_peers(seq, tp) + tp_peers(partner_seq, tp)
    own = pl.ds(core * FR, FR)
    other = pl.ds((1 - core) * FR, FR)
    rows = [other] + [own] * (TP - 1) + [other] * (TP - 1)
    jobs = [(source.at[part], target.at[slot], peer) for part, peer in zip(rows, peers)]
    jobs.append((w_half, w_other, partner))
    run_exchange(
        peers, jobs, [(source.at[own], bounce, target.at[slot], sem)], send_sems, recv_sems
    )


def exchange_attended(attended, w_half):
    return exchange(
        attended_kernel,
        "exchange_attended",
        2,
        (attended, w_half),
        [
            jax.ShapeDtypeStruct((2 * TP, FR, HD), BF16),
            jax.ShapeDtypeStruct(w_half.shape, BF16),
        ],
        16,
        [((FR, HD), BF16)],
    )


def latent_kernel(
    source, att_all, merged, target, att_other, merged_other, send_sems, recv_sems, sem, bounce
):
    seq, chip, core, tp = place()
    partner = (chip * 2 + 1 - core, tp)
    peers = tp_peers(seq, tp)
    jobs = [(source.at[peer[1]], target.at[tp], peer) for peer in peers]
    jobs.append((att_all, att_other, partner))
    jobs.append((merged, merged_other, partner))
    run_exchange(
        peers + [partner],
        jobs,
        [(source.at[tp], bounce, target.at[tp], sem)],
        send_sems,
        recv_sems,
    )


def exchange_latent(parts, att_all, merged):
    return exchange(
        latent_kernel,
        "exchange_latent",
        3,
        (parts, att_all, merged),
        [
            jax.ShapeDtypeStruct(parts.shape, parts.dtype),
            jax.ShapeDtypeStruct(att_all.shape, BF16),
            jax.ShapeDtypeStruct(merged.shape, BF16),
        ],
        9,
        [(parts.shape[1:], parts.dtype)],
    )


def message_kernel(source, grads, target, grads_other, send_sems, recv_sems, sem, bounce):
    seq, chip, core, tp = place()
    partner = (chip * 2 + 1 - core, tp)
    peers = tp_peers(seq, tp)
    jobs = [(source, target.at[core, tp], peer) for peer in peers]
    forwards = []
    for number, hop in enumerate(TP_ORDER):
        slot = target.at[core, lax.rem(tp - hop + TP, TP)]
        forwards.append((number, (slot, slot, partner)))
    jobs.append((source, target.at[core, tp], partner))
    jobs.append((grads.at[:, 1 - core], grads_other, partner))
    run_exchange(
        peers + [partner],
        jobs,
        [(source, bounce, target.at[core, tp], sem)],
        send_sems,
        recv_sems,
        forwards,
    )


def exchange_message(message, grads):
    return exchange(
        message_kernel,
        "exchange_message",
        4,
        (message, grads),
        [
            jax.ShapeDtypeStruct((2, TP) + message.shape, message.dtype),
            jax.ShapeDtypeStruct((CHIPS, TP) + grads.shape[3:], BF16),
        ],
        16,
        [(message.shape, message.dtype)],
    )


def cotangent_kernel(
    source, side, grads, target, side_x, grads_z, send_sems, recv_sems, sem, bounce, side_bounce, grads_bounce
):
    seq, chip, core, tp = place()
    partner_seq = chip * 2 + 1 - core
    at_x, at_y = chip // 2, chip % 2
    row, depth_at = tp // 4, tp % 4
    peers = [(partner_seq, tp)] + tp_peers(seq, tp) + tp_peers(partner_seq, tp)
    heads = [1 - core] + [core] * (TP - 1) + [1 - core] * (TP - 1)
    jobs = [
        (source.at[peer[1] * 2 + head], target.at[core, tp], peer)
        for head, peer in zip(heads, peers)
    ]
    for hop in (2, 1, 3):
        there = lax.rem(at_x + hop, 4)
        other = (there * 4 + at_y * 2 + core, tp)
        peers.append(other)
        jobs.append((side.at[there], side_x.at[at_x], other))
    early = pl.ds(0, Z_EARLY)
    for hop in (2, 1, 3):
        there = lax.rem(depth_at + hop, 4)
        other = (seq, row * 4 + there)
        jobs.append((grads.at[early, :, there], grads_z.at[depth_at], other))
    run_exchange(
        peers,
        jobs,
        [
            (source.at[tp * 2 + core], bounce, target.at[core, tp], sem),
            (side.at[at_x], side_bounce, side_x.at[at_x], sem),
            (grads.at[early, :, depth_at], grads_bounce, grads_z.at[depth_at], sem),
        ],
        send_sems,
        recv_sems,
    )


def exchange_cotangent(parts, side, grads):
    slab = (Z_EARLY, 2) + grads.shape[3:]
    return exchange(
        cotangent_kernel,
        "exchange_cotangent",
        5,
        (parts, side, grads),
        [
            jax.ShapeDtypeStruct((2, TP, FR, HD), BF16),
            jax.ShapeDtypeStruct(side.shape, BF16),
            jax.ShapeDtypeStruct((4,) + slab, BF16),
        ],
        21,
        [((FR, HD), BF16), (side.shape[1:], BF16), (slab, BF16)],
    )


def grads_kernel(
    pair, stats, grads, side, normed, pair_all, stats_all, grads_z, side_in, normed_other,
    send_sems, recv_sems, sem, bounce, stats_bounce, grads_bounce,
):
    seq, chip, core, tp = place()
    row, depth_at = tp // 4, tp % 4
    at_x, at_y = chip // 2, chip % 2
    peers = []
    jobs = []
    for hop in CHIP_ORDER:
        there = lax.rem(chip + hop, CHIPS)
        here = lax.rem(chip - hop + CHIPS, CHIPS)
        other = (there * 2 + core, tp)
        peers.append(other)
        jobs.append((stats, stats_all.at[chip], other, there < chip, here > chip))
    for hop in (2, 1, 3):
        there = lax.rem(depth_at + hop, 4)
        other = (seq, row * 4 + there)
        peers.append(other)
        jobs.append((grads.at[pl.ds(Z_EARLY, Z_LATE), :, there], grads_z.at[depth_at], other))
    jobs.append((side.at[1 - at_y], side_in, (at_x * 4 + (1 - at_y) * 2 + core, tp)))
    partner = (chip * 2 + 1 - core, tp)
    jobs.append((normed, normed_other, partner))
    peers.append(partner)

    def relay(*rest):
        return relay_blocks(
            lambda item: pair.at[1 - core if item else core],
            lambda source, part: pair_all.at[source, part],
            True,
            *rest,
        )

    run_exchange(
        peers,
        jobs,
        [
            (pair, bounce, pair_all.at[chip], sem),
            (stats, stats_bounce, stats_all.at[chip], sem),
            (
                grads.at[pl.ds(Z_EARLY, Z_LATE), :, depth_at],
                grads_bounce,
                grads_z.at[depth_at],
                sem,
            ),
        ],
        send_sems,
        recv_sems,
        relay=relay,
    )


def exchange_grads(pair, stats, grads, side, normed):
    slab = (Z_LATE, 2) + grads.shape[3:]
    return exchange(
        grads_kernel,
        "exchange_grads",
        6,
        (pair, stats, grads, side, normed),
        [
            jax.ShapeDtypeStruct((CHIPS,) + pair.shape, BF16),
            jax.ShapeDtypeStruct((CHIPS,) + stats.shape, F32),
            jax.ShapeDtypeStruct((4,) + slab, BF16),
            jax.ShapeDtypeStruct(side.shape[1:], BF16),
            jax.ShapeDtypeStruct(normed.shape, BF16),
        ],
        12 + RELAY_COPIES,
        [(pair.shape, BF16), (stats.shape, F32), (slab, BF16)],
    )


def first_kernel(
    x_first, y_first, grads, out, x_in, y_in, grads_x, out_all,
    send_sems, recv_sems, sem, x_bounce, y_bounce, grads_bounce, out_bounce,
):
    seq, chip, core, tp = place()
    at_x, at_y = chip // 2, chip % 2

    def device(x, y, c):
        return x * 4 + y * 2 + c, tp

    peers = []
    jobs = []
    for hop in (2, 1, 3):
        x = lax.rem(at_x + hop, 4)
        for c in (core, 1 - core):
            peers.append(device(x, at_y, c))
            jobs.append((x_first.at[x, c], x_in.at[at_x, core], peers[-1]))
    for c in (core, 1 - core):
        peers.append(device(at_x, 1 - at_y, c))
        jobs.append((y_first.at[1 - at_y, c], y_in.at[at_y, core], peers[-1]))
    for hop in (2, 1, 3):
        x = lax.rem(at_x + hop, 4)
        jobs.append((grads.at[x], grads_x.at[at_x], device(x, at_y, core)))
    for other in tp_peers(seq, tp):
        peers.append(other)
        jobs.append((out.at[other[1]], out_all.at[tp], other))
    peers.append(device(at_x, at_y, 1 - core))
    jobs.append((x_first.at[at_x, 1 - core], x_in.at[at_x, core], peers[-1]))
    jobs.append((y_first.at[at_y, 1 - core], y_in.at[at_y, core], peers[-1]))
    run_exchange(
        peers,
        jobs,
        [
            (x_first.at[at_x, core], x_bounce, x_in.at[at_x, core], sem),
            (y_first.at[at_y, core], y_bounce, y_in.at[at_y, core], sem),
            (grads.at[at_x], grads_bounce, grads_x.at[at_x], sem),
            (out.at[tp], out_bounce, out_all.at[tp], sem),
        ],
        send_sems,
        recv_sems,
    )


def exchange_first(x_first, y_first, grads, out):
    arrays = (x_first, y_first, grads, out)
    tails = (x_first.shape[2:], y_first.shape[2:], grads.shape[1:], out.shape[1:])
    return exchange(
        first_kernel,
        "exchange_first",
        7,
        arrays,
        [jax.ShapeDtypeStruct(array.shape, BF16) for array in arrays],
        20,
        [(tail, BF16) for tail in tails],
    )


def second_kernel(
    x_sum, y_sum, grads, x_in, y_in, grads_in, send_sems, recv_sems, sem, y_bounce, grads_bounce
):
    seq, chip, core, tp = place()
    at_x, at_y = chip // 2, chip % 2
    row, depth_at = tp // 4, tp % 4
    peers = []
    jobs = []
    for hop in (2, 1, 3):
        x = lax.rem(at_x + hop, 4)
        peers.append((x * 4 + at_y * 2 + core, tp))
        jobs.append((y_sum.at[x], y_in.at[at_x], peers[-1]))
    peers.append((at_x * 4 + (1 - at_y) * 2 + core, tp))
    jobs.append((x_sum.at[1 - at_y], x_in, peers[-1]))
    jobs.append((grads.at[1 - at_y, row], grads_in.at[at_y, row], peers[-1]))
    for y in (at_y, 1 - at_y):
        peers.append((at_x * 4 + y * 2 + core, (1 - row) * 4 + depth_at))
        jobs.append((grads.at[y, 1 - row], grads_in.at[at_y, row], peers[-1]))
    run_exchange(
        peers,
        jobs,
        [
            (y_sum.at[at_x], y_bounce, y_in.at[at_x], sem),
            (grads.at[at_y, row], grads_bounce, grads_in.at[at_y, row], sem),
        ],
        send_sems,
        recv_sems,
    )


def exchange_second(x_sum, y_sum, grads):
    return exchange(
        second_kernel,
        "exchange_second",
        8,
        (x_sum, y_sum, grads),
        [
            jax.ShapeDtypeStruct(x_sum.shape[1:], BF16),
            jax.ShapeDtypeStruct(y_sum.shape, BF16),
            jax.ShapeDtypeStruct(grads.shape, BF16),
        ],
        7,
        [(y_sum.shape[1:], BF16), (grads.shape[2:], BF16)],
    )


def compute(kernel, name, ins, outs, scratch=(), limit=48, hbm=0):
    return pl.pallas_call(
        kernel,
        name=name,
        out_shape=outs,
        in_specs=[VMEM] * (len(ins) - hbm) + [HBM] * hbm,
        out_specs=[VMEM] * len(outs),
        scratch_shapes=list(scratch),
        compiler_params=pltpu.CompilerParams(vmem_limit_bytes=limit * MIB),
    )(*ins)


START_STEPS = 8


def start_kernel(
    hidden_ref, cos_ref, sin_ref, w_hbm, normed_ref, kv_ref, query_ref, out_w_ref, total_ref, w_ref, sems
):
    depth_rows = w_ref.shape[1]
    copies = [
        fetch(w_hbm.at[pl.ds(step * depth_rows, depth_rows)], w_ref.at[step], sems.at[step])
        for step in range(START_STEPS)
    ]
    hidden = hidden_ref[...].astype(F32)
    normed_ref[...] = (hidden * rms_scale(hidden)).astype(BF16)
    pieces = depth_rows // (TP * 32)
    for step in range(START_STEPS):
        copies[step].wait()
        weights = w_ref[step].reshape(depth_rows, 8 * HD)
        normed = normed_ref[:, step * depth_rows : (step + 1) * depth_rows]
        term = dot_nn(normed, weights[:, : 6 * HD])
        if step:
            total_ref[...] += term
        else:
            total_ref[...] = term
        out_w = weights[:, 6 * HD :].reshape(pieces, TP, 32, 2 * HD)
        for at in range(TP):
            for piece in range(pieces):
                low = (step * pieces + piece) * 32
                out_w_ref[at, low : low + 32] = out_w[piece, at]
    own = pl.ds(pl.multiple_of(lax.axis_index("seq") % 2 * FR, FR), FR)
    cosine, sine = cos_ref[own], sin_ref[own]

    def turned(at):
        lower = total_ref[:, at : at + HD // 2]
        upper = total_ref[:, at + HD // 2 : at + HD]
        return jnp.concatenate(
            [lower * cosine - upper * sine, upper * cosine + lower * sine], axis=1
        ).astype(BF16)

    for head in range(2):
        query_ref[head] = turned(head * HD)
        kv_ref[head, :, :HD] = turned((2 + head) * HD)
        at = (4 + head) * HD
        kv_ref[head, :, HD:] = total_ref[:, at : at + HD].astype(BF16)


def start(hidden, weights, cosine, sine):
    depth_rows = weights.shape[0] // START_STEPS
    return compute(
        start_kernel,
        "start",
        (hidden, cosine, sine, weights),
        [
            jax.ShapeDtypeStruct(hidden.shape, BF16),
            jax.ShapeDtypeStruct((2, FR, 2 * HD), BF16),
            jax.ShapeDtypeStruct((2, FR, HD), BF16),
            jax.ShapeDtypeStruct((TP, NS, 2 * HD), BF16),
        ],
        [
            pltpu.VMEM((FR, 6 * HD), F32),
            pltpu.VMEM((START_STEPS, depth_rows) + weights.shape[1:], BF16),
            pltpu.SemaphoreType.DMA((START_STEPS,)),
        ],
        hbm=1,
        limit=32,
    )


def attend_kernel(kv_ref, query_ref, out_ref, out_t_ref, level_ref, score_ref):
    chip = lax.axis_index("seq") // 2
    query = query_ref[...]
    key_at = lax.broadcasted_iota(jnp.int32, (FR2, FR2), 0)
    query_at = lax.broadcasted_iota(jnp.int32, (FR2, FR2), 1)

    def scores(block, top):
        score = dot_nt(kv_ref[block, :, :HD], query) * LOG_SCALE
        score_ref[block] = score
        return jnp.maximum(top, jnp.max(score, axis=0, keepdims=True))

    score = dot_nt(kv_ref[chip, :, :HD], query) * LOG_SCALE
    score = jnp.where(key_at <= query_at, score, MASKED)
    score_ref[chip] = score
    top = lax.fori_loop(0, chip, scores, jnp.max(score, axis=0, keepdims=True))

    def weigh(block, carry):
        total, mixed = carry
        prob = jnp.exp2(score_ref[block] - top)
        total = total + jnp.sum(prob, axis=0, keepdims=True)
        return total, mixed + dot_tn(kv_ref[block, :, HD:], prob.astype(BF16))

    total, mixed = lax.fori_loop(
        0, chip + 1, weigh, (jnp.zeros((1, FR2), F32), jnp.zeros((HD, FR2), F32))
    )
    mixed = mixed * (1.0 / total)
    out_t_ref[...] = mixed
    level_ref[...] = top + jnp.log2(total)
    out_ref[...] = mixed.T.astype(BF16)


def attend(kv_all, query):
    return compute(
        attend_kernel,
        "attend",
        (kv_all, query),
        [
            jax.ShapeDtypeStruct((FR2, HD), BF16),
            jax.ShapeDtypeStruct((HD, FR2), F32),
            jax.ShapeDtypeStruct((1, FR2), F32),
        ],
        [pltpu.VMEM((CHIPS, FR2, FR2), F32)],
        limit=20,
    )


def fetch(source, target, sem):
    copy = pltpu.make_async_copy(source, target, sem)
    copy.start()
    return copy


def order_halves(core, mine, other):
    return jnp.where(core == 0, mine, other), jnp.where(core == 0, other, mine)


def merge_kernel(
    att_ref, half_ref, other_ref, hidden_ref, depth_in_hbm, merged_ref, round_ref, part_ref, depth_in_ref, sem
):
    seq, chip, core, tp = place()
    copy = fetch(depth_in_hbm.at[:, tp], depth_in_ref, sem)
    width = hidden_ref.shape[1]
    group = width // 2
    row_at = lax.broadcasted_iota(jnp.int32, (group, FR), 0)
    col_at = lax.broadcasted_iota(jnp.int32, (group, FR), 1)
    wanted = (col_at // 32) * 256 + tp * 32 + col_at % 32
    pick = jnp.where(row_at == wanted, 1.0, 0.0).astype(BF16)
    merged = jnp.concatenate(
        [dot_nn(hidden_ref[:, :group], pick), dot_nn(hidden_ref[:, group:], pick)], axis=1
    )
    mine = jnp.zeros((FR, FR), F32)
    other = jnp.zeros((FR, FR), F32)
    for at in range(TP):
        pair = jnp.concatenate([att_ref[2 * at], att_ref[2 * at + 1]], axis=1)
        mine = mine + dot_nt(pair, half_ref[at])
        other = other + dot_nt(pair, other_ref[at])
    merged = merged + jnp.concatenate(order_halves(core, mine, other), axis=1)
    rounded = merged.astype(BF16)
    merged_ref[...] = merged
    round_ref[...] = rounded
    squares = jnp.sum(merged * merged, axis=-1, keepdims=True)
    copy.wait()
    latent = dot_nn(rounded, depth_in_ref[...].reshape(NS, DD))
    coarse = squares.astype(BF16)
    fine = (squares - coarse.astype(F32)).astype(BF16)
    part_ref[:, :, :DD] = latent.astype(BF16).reshape(TP, FR // TP, DD)
    part_ref[:, :, DD : DD + HD] = jnp.broadcast_to(coarse, (FR, HD)).reshape(TP, FR // TP, HD)
    part_ref[:, :, DD + HD :] = jnp.broadcast_to(fine, (FR, HD)).reshape(TP, FR // TP, HD)


def merge(att_all, w_half, w_other, hidden, depth_in):
    return compute(
        merge_kernel,
        "merge",
        (att_all, w_half, w_other, hidden, depth_in),
        [
            jax.ShapeDtypeStruct((FR, NS), F32),
            jax.ShapeDtypeStruct((FR, NS), BF16),
            jax.ShapeDtypeStruct((TP, FR // TP, DD + 2 * HD), BF16),
        ],
        [pltpu.VMEM((2 * CHIPS, 32, DD), BF16), pltpu.SemaphoreType.DMA],
        hbm=1,
        limit=24,
    )


def depth_kernel(
    width, loss_scale, part_ref, code_ref, stack_hbm, message_ref, grad_ref, prob_ref, stack_ref, sems
):
    frames, books = code_ref.shape
    pieces = ((3072, 1024), (0, 1536), (1536, 512), (2048, 1024))
    copies = [
        fetch(stack_hbm.at[pl.ds(low, rows)], stack_ref.at[pl.ds(low, rows)], sems.at[at])
        for at, (low, rows) in enumerate(pieces)
    ]
    grid = (frames, books, books)
    row_at = lax.broadcasted_iota(jnp.int32, grid, 1)
    col_at = lax.broadcasted_iota(jnp.int32, grid, 2)
    spread = jnp.broadcast_to(code_ref[...][:, None, :], grid)

    def column(wanted):
        picked = jnp.where(wanted, spread + 1, 0).astype(F32)
        picked = jnp.sum(picked, axis=-1, keepdims=True).reshape(frames * books, 1)
        return picked - 1.0

    codes = column(col_at == row_at)
    before = column(col_at == row_at - 1)
    tokens = frames * books
    total = jnp.sum(part_ref[...].astype(F32), axis=0)
    raw = total[:, :DD]
    squares = total[:, DD : DD + 1] + total[:, DD + HD : DD + HD + 1]
    scale_in = lax.rsqrt(squares * (1.0 / width) + EPSILON)
    latent = raw * scale_in
    latent = jnp.broadcast_to(latent[:, None, :], (frames, books, DD)).reshape(tokens, DD)
    vocab_at = lax.broadcasted_iota(jnp.int32, (tokens, VOCAB), 1).astype(F32)
    hot = jnp.where(before == vocab_at, 1.0, 0.0).astype(BF16)
    copies[0].wait()
    stream = latent + dot_nn(hot, stack_ref[4 * DD + VOCAB :])
    stream_scale = rms_scale(stream)
    stream_norm = (stream * stream_scale).astype(BF16)
    copies[1].wait()
    qkv_rows = stack_ref[: 3 * DD]
    proj = dot_nt(stream_norm, qkv_rows).astype(BF16)
    row_at = lax.broadcasted_iota(jnp.int32, (tokens, tokens), 0)
    col_at = lax.broadcasted_iota(jnp.int32, (tokens, tokens), 1)
    allowed = (row_at // books == col_at // books) & (col_at <= row_at)
    depth_scale = 1.0 / math.sqrt(DHD)
    mixed = []
    for head in range(DD // DHD):
        low = head * DHD
        queries = proj[:, low : low + DHD]
        keys = proj[:, DD + low : DD + low + DHD]
        values = proj[:, 2 * DD + low : 2 * DD + low + DHD]
        scores = jnp.where(allowed, dot_nt(queries, keys) * depth_scale, MASKED)
        weights = jnp.exp(scores - jnp.max(scores, axis=-1, keepdims=True))
        probs = weights / jnp.sum(weights, axis=-1, keepdims=True)
        prob_ref[head] = probs
        mixed.append(dot_nn(probs.astype(BF16), values))
    mixed = jnp.concatenate(mixed, axis=1).astype(BF16)
    copies[2].wait()
    out_rows = stack_ref[3 * DD : 4 * DD]
    resid = stream + dot_nt(mixed, out_rows)
    resid_scale = rms_scale(resid)
    resid_norm = (resid * resid_scale).astype(BF16)
    copies[3].wait()
    head_rows = stack_ref[4 * DD : 4 * DD + VOCAB]
    logits = dot_nt(resid_norm, head_rows)
    weights = jnp.exp(logits - jnp.max(logits, axis=-1, keepdims=True))
    logit_probs = weights / jnp.sum(weights, axis=-1, keepdims=True)
    target = jnp.where(codes == vocab_at, 1.0, 0.0)
    logit_grad = ((logit_probs - target) * loss_scale).astype(BF16)
    grad_ref[4 * DD : 4 * DD + VOCAB] = dot_tn(logit_grad, resid_norm).astype(BF16)
    resid_grad = norm_back(resid, resid_scale, dot_nn(logit_grad, head_rows))
    resid_round = resid_grad.astype(BF16)
    grad_ref[3 * DD : 4 * DD] = dot_tn(resid_round, mixed).astype(BF16)
    mixed_grad = dot_nn(resid_round, out_rows).astype(BF16)
    query_grad, key_grad, value_grad = [], [], []
    for head in range(DD // DHD):
        low = head * DHD
        queries = proj[:, low : low + DHD]
        keys = proj[:, DD + low : DD + low + DHD]
        values = proj[:, 2 * DD + low : 2 * DD + low + DHD]
        probs = prob_ref[head]
        mix_grad = mixed_grad[:, low : low + DHD]
        value_grad.append(dot_tn(probs.astype(BF16), mix_grad))
        prob_grad = dot_nt(mix_grad, values)
        inner = jnp.sum(probs * prob_grad, axis=-1, keepdims=True)
        score_grad = (probs * (prob_grad - inner) * depth_scale).astype(BF16)
        query_grad.append(dot_nn(score_grad, keys))
        key_grad.append(dot_tn(score_grad, queries))
    proj_grad = jnp.concatenate(query_grad + key_grad + value_grad, axis=1).astype(BF16)
    grad_ref[: 3 * DD] = dot_tn(proj_grad, stream_norm).astype(BF16)
    stream_grad = resid_grad + norm_back(stream, stream_scale, dot_nn(proj_grad, qkv_rows))
    grad_ref[4 * DD + VOCAB :] = dot_tn(hot, stream_grad.astype(BF16)).astype(BF16)
    latent_grad = jnp.sum(stream_grad.reshape(frames, books, DD), axis=1)
    latent_grad = latent_grad.astype(BF16).astype(F32)
    inner = jnp.sum(latent_grad * raw, axis=-1, keepdims=True) * (1.0 / width)
    pull = scale_in * scale_in * scale_in * inner
    coarse = pull.astype(BF16)
    fine = (pull - coarse.astype(F32)).astype(BF16)
    message_ref[:, :DD] = (latent_grad * scale_in).astype(BF16)
    message_ref[:, DD : DD + HD] = jnp.broadcast_to(coarse, (frames, HD))
    message_ref[:, DD + HD :] = jnp.broadcast_to(fine, (frames, HD))


def depth(parts, codes, stack, width, loss_scale):
    tokens = codes.shape[0] * codes.shape[1]
    return compute(
        functools.partial(depth_kernel, width, loss_scale),
        "depth",
        (parts, codes, stack),
        [
            jax.ShapeDtypeStruct((parts.shape[1], DD + 2 * HD), BF16),
            jax.ShapeDtypeStruct(stack.shape, BF16),
        ],
        [
            pltpu.VMEM((DD // DHD, tokens, tokens), F32),
            pltpu.VMEM(stack.shape, BF16),
            pltpu.SemaphoreType.DMA((4,)),
        ],
        hbm=1,
        limit=32,
    )


def merged_gradient(message, merged, depth_in):
    pull = message[:, DD : DD + 1].astype(F32) + message[:, DD + HD : DD + HD + 1].astype(F32)
    return dot_nt(message[:, :DD], depth_in) - merged * pull


def unmerge_kernel(
    message_ref,
    merged_ref,
    round_ref,
    round_other_ref,
    att_ref,
    att_other_ref,
    half_ref,
    other_ref,
    grads_other_ref,
    grads_hbm,
    depth_in_hbm,
    part_ref,
    side_ref,
    grads_ref,
    depth_in_ref,
    grads_own_ref,
    sems,
):
    seq, chip, core, tp = place()
    copy = fetch(depth_in_hbm.at[:, tp], depth_in_ref, sems.at[0])
    grads_copy = fetch(grads_hbm.at[:, core], grads_own_ref, sems.at[1])
    copy.wait()
    depth_in = depth_in_ref[...].reshape(NS, DD)
    message = message_ref[core].reshape(FR, DD + 2 * HD)
    message_other = message_ref[1 - core].reshape(FR, DD + 2 * HD)
    gradient = merged_gradient(message, merged_ref[...], depth_in)
    lower, upper = gradient[:, :FR], gradient[:, FR:]
    mine, other = order_halves(core, lower, upper)
    mine, other = mine.astype(BF16), other.astype(BF16)
    for at in range(TP):
        pair = (dot_nn(mine, half_ref[at]) + dot_nn(other, other_ref[at])).astype(BF16)
        part_ref[2 * at] = pair[:, :HD]
        part_ref[2 * at + 1] = pair[:, HD:]
    gradient_other = merged_gradient(
        message_other, round_other_ref[...].astype(F32), depth_in
    )

    def pick_rows(own, others):
        both = jnp.concatenate([own.T, others.T], axis=1).reshape(CHIPS, 2, 32, FR2)
        both = jnp.where(core == 0, both[:, 0], both[:, 1])
        return both.reshape(FR, FR2).astype(BF16)

    rows = pick_rows(gradient, gradient_other)
    for at in range(TP):
        pair = jnp.concatenate([att_ref[2 * at], att_ref[2 * at + 1]], axis=1)
        pair_other = jnp.concatenate([att_other_ref[2 * at], att_other_ref[2 * at + 1]], axis=1)
        term = dot_nn(rows, jnp.concatenate([pair, pair_other], axis=0)).astype(BF16)
        side_ref[:, :, at * FR : (at + 1) * FR] = term.reshape(CHIPS, 32, FR)
    rows = pick_rows(round_ref[...].astype(F32), round_other_ref[...].astype(F32))
    both = jnp.concatenate([message[:, :DD], message_other[:, :DD]], axis=0)
    side_ref[:, :, TP * FR :] = dot_nn(rows, both).astype(BF16).reshape(CHIPS, 32, DD)
    grads_copy.wait()
    for at in range(CHIPS):
        grads_ref[at] = (
            grads_own_ref[at].astype(F32) + grads_other_ref[at].astype(F32)
        ).astype(BF16)


def unmerge(
    messages, merged, rounded, rounded_other, att_all, att_other, w_half, w_other, grads_other, grads, depth_in
):
    return compute(
        unmerge_kernel,
        "unmerge",
        (
            messages,
            merged,
            rounded,
            rounded_other,
            att_all,
            att_other,
            w_half,
            w_other,
            grads_other,
            grads,
            depth_in,
        ),
        [
            jax.ShapeDtypeStruct((2 * TP, FR, HD), BF16),
            jax.ShapeDtypeStruct((CHIPS, 32, TP * FR + DD), BF16),
            jax.ShapeDtypeStruct(grads_other.shape, BF16),
        ],
        [
            pltpu.VMEM((2 * CHIPS, 32, DD), BF16),
            pltpu.VMEM(grads_other.shape, BF16),
            pltpu.SemaphoreType.DMA((2,)),
        ],
        hbm=2,
        limit=28,
    )


def prepare_kernel(
    part_ref, query_ref, out_t_ref, level_ref, side_x_ref, pair_ref, stats_ref, side_ref
):
    gradient = jnp.sum(part_ref[...].astype(F32), axis=1).reshape(FR2, HD).astype(BF16)
    pair_ref[:, :, :HD] = query_ref[...].reshape(2, FR, HD)
    pair_ref[:, :, HD:] = gradient.reshape(2, FR, HD)
    inner = jnp.sum(gradient.astype(F32).T * out_t_ref[...], axis=0, keepdims=True)
    stats_ref[...] = jnp.concatenate(
        [level_ref[...], inner, jnp.zeros((6, FR2), F32)], axis=0
    )
    side_ref[...] = jnp.sum(side_x_ref[...].astype(F32), axis=0).astype(BF16)


def prepare(parts, query, out_t, level, side_x):
    return compute(
        prepare_kernel,
        "prepare",
        (parts, query, out_t, level, side_x),
        [
            jax.ShapeDtypeStruct((2, FR, 2 * HD), BF16),
            jax.ShapeDtypeStruct((8, FR2), F32),
            jax.ShapeDtypeStruct(side_x.shape[1:], BF16),
        ],
        limit=16,
    )


def attend_back_kernel(
    stats_ref, cos_ref, sin_ref, side_ref, side_in_ref, kv_hbm, pair_hbm, early_hbm, late_hbm,
    normed_hbm, other_hbm, x_ref, y_ref, grads_ref, win_ref, out_w_ref,
    kv_ref, pair_ref, early_ref, late_ref, normed_ref, other_ref, sems,
):
    chip = lax.axis_index("seq") // 2
    core = lax.axis_index("seq") % 2
    places = (
        (kv_hbm, kv_ref),
        (pair_hbm, pair_ref),
        (normed_hbm, normed_ref),
        (other_hbm, other_ref),
        (early_hbm, early_ref),
        (late_hbm, late_ref),
    )
    copies = [fetch(source, target, sems.at[at]) for at, (source, target) in enumerate(places)]
    copies[0].wait()
    copies[1].wait()
    scale = 1.0 / math.sqrt(HD)

    def pair(queries, keys, diagonal):
        query = pair_ref[queries, :, :HD]
        gradient = pair_ref[queries, :, HD:]
        score = dot_nt(kv_ref[keys, :, :HD], query) * LOG_SCALE
        if diagonal:
            key_at = lax.broadcasted_iota(jnp.int32, (FR2, FR2), 0)
            query_at = lax.broadcasted_iota(jnp.int32, (FR2, FR2), 1)
            score = jnp.where(key_at <= query_at, score, MASKED)
        prob = jnp.exp2(score - stats_ref[queries, 0:1])
        prob_grad = dot_nt(kv_ref[keys, :, HD:], gradient)
        score_grad = (prob * (prob_grad - stats_ref[queries, 1:2])).astype(BF16)
        return query, gradient, prob.astype(BF16), score_grad

    def own_queries(block, total):
        score_grad = pair(chip, block, False)[3]
        return total + dot_tn(kv_ref[block, :, :HD], score_grad)

    def own_keys(block, totals):
        query, gradient, prob, score_grad = pair(block, chip, False)
        return totals[0] + dot_nn(score_grad, query), totals[1] + dot_nn(prob, gradient)

    query, gradient, prob, score_grad = pair(chip, chip, True)
    query_grad = dot_tn(kv_ref[chip, :, :HD], score_grad)
    key_grad = dot_nn(score_grad, query)
    value_grad = dot_nn(prob, gradient)
    query_grad = lax.fori_loop(0, chip, own_queries, query_grad)
    key_grad, value_grad = lax.fori_loop(chip + 1, CHIPS, own_keys, (key_grad, value_grad))
    query_grad = query_grad.T
    cosine, sine = cos_ref[...] * scale, sin_ref[...] * scale

    def turned(total):
        lower, upper = total[:, : HD // 2], total[:, HD // 2 :]
        return [lower * cosine + upper * sine, upper * cosine - lower * sine]

    proj = jnp.concatenate(turned(query_grad) + turned(key_grad) + [value_grad], axis=1)
    proj_t = proj.T
    own, other = order_halves(core, proj_t[:, :FR], proj_t[:, FR:])
    own, other = own.astype(BF16), other.astype(BF16)
    copies[2].wait()
    copies[3].wait()
    for piece in range(2 * CHIPS):
        low = piece * FR
        term = dot_nn(own, normed_ref[:, low : low + FR])
        term = (term + dot_nn(other, other_ref[:, low : low + FR])).astype(BF16)
        x, y, c = piece // 4, piece // 2 % 2, piece % 2
        x_ref[x, c, y] = term[:X_ROWS]
        y_ref[y, c, x] = term[X_ROWS:]
    copies[4].wait()
    copies[5].wait()
    for at in range(CHIPS):
        term = early_ref[:, at] if at < Z_EARLY else late_ref[:, at - Z_EARLY]
        grads_ref[at] = jnp.sum(term.astype(F32), axis=0).astype(BF16)
    side = side_ref[chip % 2].astype(F32) + side_in_ref[...].astype(F32)
    win_ref[...] = side[:, TP * FR :]
    for at in range(TP):
        out_w_ref[at] = side[:, at * FR : (at + 1) * FR].astype(BF16)


def attend_back(
    stats_all, cosine, sine, side, side_in, kv_all, pair_all, early, late, normed, normed_other
):
    streamed = (kv_all, pair_all, early, late, normed, normed_other)
    return compute(
        attend_back_kernel,
        "attend_back",
        (stats_all, cosine, sine, side, side_in) + streamed,
        [
            jax.ShapeDtypeStruct((4, 2, 2, X_ROWS, FR), BF16),
            jax.ShapeDtypeStruct((2, 2, 4, Y_ROWS, FR), BF16),
            jax.ShapeDtypeStruct((CHIPS,) + late.shape[2:], BF16),
            jax.ShapeDtypeStruct((32, DD), F32),
            jax.ShapeDtypeStruct((TP, 32, FR), BF16),
        ],
        [pltpu.VMEM(array.shape, BF16) for array in streamed] + [pltpu.SemaphoreType.DMA((6,))],
        hbm=6,
        limit=36,
    )


def middle_kernel(x_ref, y_ref, grads_x_ref, x_sum_ref, y_sum_ref, grads_ref):
    for y in range(2):
        for c in range(2):
            terms = [x_ref[x, c, y].astype(F32) for x in range(4)]
            x_sum_ref[y, c] = (terms[0] + terms[1] + terms[2] + terms[3]).astype(BF16)
    for x in range(4):
        for c in range(2):
            term = y_ref[0, c, x].astype(F32) + y_ref[1, c, x].astype(F32)
            y_sum_ref[x, c] = term.astype(BF16)
    grads_ref[...] = jnp.sum(grads_x_ref[...].astype(F32), axis=0).astype(BF16)


def middle_sum(x_in, y_in, grads_x):
    return compute(
        middle_kernel,
        "middle_sum",
        (x_in, y_in, grads_x),
        [
            jax.ShapeDtypeStruct((2, 2, X_ROWS, FR), BF16),
            jax.ShapeDtypeStruct((4, 2, Y_ROWS, FR), BF16),
            jax.ShapeDtypeStruct(grads_x.shape[1:], BF16),
        ],
        limit=16,
    )


def last_kernel(x_own_ref, x_in_ref, y_in_ref, grads_ref, out_w_ref, out_ref, depth_ref):
    at_y = lax.axis_index("seq") // 2 % 2
    totals = []
    for head in range(2):
        x_part = x_own_ref[at_y, head].astype(F32) + x_in_ref[head].astype(F32)
        terms = [y_in_ref[x, head].astype(F32) for x in range(4)]
        y_part = terms[0] + terms[1] + terms[2] + terms[3]
        totals.append(jnp.concatenate([x_part, y_part], axis=0).T)
    pieces = [totals[head][:, kind * HD : (kind + 1) * HD] for kind in range(3) for head in range(2)]
    pieces.append(out_w_ref[...].astype(F32).reshape(FR, 2 * HD))
    out_ref[...] = jnp.concatenate(pieces, axis=1).reshape(FR, 4, 2 * HD)
    depth_ref[...] = jnp.sum(jnp.sum(grads_ref[...].astype(F32), axis=0), axis=0)


def last_sum(x_own, x_in, y_in, grads, out_all):
    return compute(
        last_kernel,
        "last_sum",
        (x_own, x_in, y_in, grads, out_all),
        [
            jax.ShapeDtypeStruct((FR, 4, 2 * HD), F32),
            jax.ShapeDtypeStruct(grads.shape[2:], F32),
        ],
        limit=16,
    )


def per_device(hidden_in, temporal_weight_stack, depth_in, depth_stack, audio_codes):
    seq_index = lax.axis_index("seq")
    tp_index = lax.axis_index("tp")
    chip = seq_index // 2
    width = hidden_in.shape[1]
    depth_frames, book_count = audio_codes.shape
    seq_count = 2 * CHIPS
    total_frames = FR * seq_count
    loss_scale = 1.0 / math.sqrt(total_frames * book_count)

    cosine, sine = angle_tables(chip * FR2, FR2)
    normed, kv, query, out_w = start(hidden_in, temporal_weight_stack, cosine, sine)
    kv_all, query, w_half = exchange_keys(kv, query, out_w)
    kv_all = kv_all.reshape(CHIPS, FR2, 2 * HD)
    query = query.reshape(FR2, HD)

    depth_in = depth_in.reshape(seq_count, TP, -1, DD)
    attended, out_t, level = attend(kv_all, query)
    att_all, w_other = exchange_attended(attended, w_half)
    merged, rounded, latent_parts = merge(att_all, w_half, w_other, hidden_in, depth_in)
    latent_parts, att_other, rounded_other = exchange_latent(latent_parts, att_all, rounded)
    message, grads = depth(latent_parts, audio_codes, depth_stack, width, loss_scale)
    grads = grads.reshape(CHIPS, 2, TP, -1, DD)
    messages, grads_other = exchange_message(message, grads)
    cotangent_parts, side, grads = unmerge(
        messages,
        merged,
        rounded,
        rounded_other,
        att_all,
        att_other,
        w_half,
        w_other,
        grads_other,
        grads,
        depth_in,
    )
    grads = grads.reshape(CHIPS, 2, 4, -1, DD)
    cotangent_parts, side, early = exchange_cotangent(
        cotangent_parts, side.reshape(4, 2, 32, -1), grads
    )
    pair, stats, side = prepare(cotangent_parts, query, out_t, level, side)
    pair_all, stats_all, late, side_in, normed_other = exchange_grads(
        pair, stats, grads, side, normed
    )
    x_first, y_first, grads, grad_win, out_parts = attend_back(
        stats_all,
        cosine,
        sine,
        side,
        side_in,
        kv_all,
        pair_all.reshape(CHIPS, FR2, 2 * HD),
        early,
        late,
        normed,
        normed_other,
    )
    x_in, y_in, grads, out_all = exchange_first(
        x_first, y_first, grads.reshape(4, 2, 2, -1, DD), out_parts
    )
    x_own, y_sum, grads = middle_sum(x_in, y_in, grads)
    x_in, y_in, grads = exchange_second(x_own, y_sum, grads)
    grad_temporal, grad_depth = last_sum(x_own, x_in, y_in, grads, out_all)
    return grad_temporal, grad_win, grad_depth


def solution(mesh):
    in_specs = (P("seq", None), P(None, None, "tp"), P(), P(), P(("seq", "tp"), None))
    out_specs = (P("seq", None, "tp"), P(("seq", "tp"), None), P(("seq", "tp"), None))
    return jax.shard_map(
        per_device, mesh=mesh, in_specs=in_specs, out_specs=out_specs, check_vma=False
    )
```

```python
import functools
import math

import jax
import jax.numpy as jnp
from jax import lax
from jax.experimental import pallas as pl
from jax.experimental.pallas import tpu as pltpu
from jax.sharding import PartitionSpec as P

HD = 128
DHD = 64
VOCAB = 1024
CHIPS = 8
TP = 8
FR = 256
FR2 = 512
DD = 512
NS = 512

EPSILON = 1e-05
MASKED = -1e30
ROPE_BASE = 10000.0
MIB = 2**20
MESH = pl.DeviceIdType.MESH
F32 = jnp.float32
BF16 = jnp.bfloat16
ANY = pl.BlockSpec(memory_space=pl.ANY)
VMEM = pl.BlockSpec(memory_space=pltpu.VMEM)
HBM = pl.BlockSpec(memory_space=pltpu.HBM)
TP_ORDER = (4, 1, 3, 5, 7, 2, 6)
CHIP_ORDER = (2, 6, 1, 4, 3, 7, 5)
LOG_SCALE = math.log2(math.e) / math.sqrt(HD)
Z_EARLY = 1
Z_LATE = CHIPS - Z_EARLY
KEY_FIRST = 128
PAIR_FIRST = 256
X_ROWS = 176
Y_ROWS = 208


def dot_nn(left, right):
    return jnp.dot(left, right, preferred_element_type=F32)


def dot_nt(left, right):
    return lax.dot_general(left, right, (((1,), (1,)), ((), ())), preferred_element_type=F32)


def dot_tn(left, right):
    return lax.dot_general(left, right, (((0,), (0,)), ((), ())), preferred_element_type=F32)


def rms_scale(values):
    return lax.rsqrt(jnp.mean(values * values, axis=-1, keepdims=True) + EPSILON)


def norm_back(values, scaling, gradient):
    inner_mean = jnp.mean(gradient * values, axis=-1, keepdims=True)
    return scaling * (gradient - values * (scaling * scaling) * inner_mean)


def angle_tables(first, count):
    half_width = HD // 2
    frequency = ROPE_BASE ** (-jnp.arange(half_width).astype(F32) / half_width)
    positions = (first + jnp.arange(count)).astype(F32)
    angles = positions[:, None] * frequency[None, :]
    return jnp.cos(angles), jnp.sin(angles)


def place():
    seq = lax.axis_index("seq")
    tp = lax.axis_index("tp")
    return seq, seq // 2, seq % 2, tp


def run_exchange(
    peers, jobs, locals_, send_sems, recv_sems, forwards=(), relay=None, relay_after=0
):
    barrier = pltpu.get_barrier_semaphore()
    for peer in peers:
        pl.semaphore_signal(barrier, inc=1, device_id=peer, device_id_type=MESH)
    pl.semaphore_wait(barrier, len(peers))
    copies = []
    arrived = set()

    def begin(source, target, device, *when):
        number = len(copies)
        copy = pltpu.make_async_remote_copy(
            src_ref=source,
            dst_ref=target,
            send_sem=send_sems.at[number],
            recv_sem=recv_sems.at[number],
            device_id=device,
            device_id_type=MESH,
        )
        if when:
            pl.when(when[0])(copy.start)
        else:
            copy.start()
        copies.append((copy, when))

    first = jobs if relay is None else jobs[:relay_after]
    for job in first:
        begin(*job)
    if relay is not None:
        total = len(jobs)

        def settle():
            for number in range(relay_after):
                copies[number][0].wait_recv()
                arrived.add(number)

        def go_on():
            for job in jobs[relay_after:]:
                begin(*job)

        finish = relay(total, send_sems, recv_sems, settle, go_on)
    for source, bounce, target, sem in locals_:
        copy = pltpu.make_async_copy(source, bounce, sem)
        copy.start()
        copy.wait()
        copy = pltpu.make_async_copy(bounce, target, sem)
        copy.start()
        copy.wait()
    for number, job in forwards:
        copies[number][0].wait_recv()
        arrived.add(number)
        begin(*job)
    if relay is not None:
        finish()
    for number, (copy, when) in enumerate(copies):
        if when:
            pl.when(when[0])(copy.wait_send)
            pl.when(when[1])(copy.wait_recv)
        else:
            copy.wait_send()
            if number not in arrived:
                copy.wait_recv()


def exchange(kernel, name, collective_id, ins, outs, copies, bounces):
    return pl.pallas_call(
        kernel,
        name=name,
        out_shape=outs,
        in_specs=[ANY] * len(ins),
        out_specs=[ANY] * len(outs),
        scratch_shapes=[
            pltpu.SemaphoreType.DMA((copies,)),
            pltpu.SemaphoreType.DMA((copies,)),
            pltpu.SemaphoreType.DMA,
        ]
        + [pltpu.VMEM(shape, dtype) for shape, dtype in bounces],
        compiler_params=pltpu.CompilerParams(
            collective_id=collective_id, has_side_effects=True, vmem_limit_bytes=4 * MIB
        ),
    )(*ins)


RELAY_COPIES = 23


def relay_blocks(own, slot, mirrored, base, send_sems, recv_sems, settle, go_on):
    seq, chip, core, tp = place()
    at_x, at_y = chip // 2, chip % 2
    column = 3 - at_x if mirrored else at_x
    line = 1 - at_y if mirrored else at_y

    def real(x):
        return 3 - x if mirrored else x

    def block(source, item):
        row = 1 - at_y if item == 2 else at_y
        return slot(real(source) * 2 + row, item)

    def copy(number, source, target, x, y):
        return pltpu.make_async_remote_copy(
            src_ref=source,
            dst_ref=target,
            send_sem=send_sems.at[base + number],
            recv_sem=recv_sems.at[base + number],
            device_id=(x * 4 + y * 2 + core, tp),
            device_id_type=MESH,
        )

    paths = ((0, 1), (0, 3), (0, 2), (1, 2), (1, 3), (2, 3))
    hops = {}
    for at, (source, target) in enumerate(paths):
        relayed = (source, target) in ((0, 2), (1, 3))
        for item in range(3):
            there = block(source, item)
            here = there if relayed or item == 2 else own(item)
            hops[source, target, item] = copy(at * 3 + item, here, there, real(target), at_y)
    across_a = copy(18, own(0), slot(chip, 0), at_x, 1 - at_y)
    across_b = copy(19, own(1), slot(chip, 1), at_x, 1 - at_y)
    across = [
        copy(20 + source, block(source, 0), block(source, 0), at_x, 1 - at_y)
        for source in range(3)
    ]
    sends_b = (line == 0) | (column < 3)
    gets_b = (line == 1) | (column < 3)

    def begin(items):
        for at in range(3):

            @pl.when(column == at)
            def _():
                for item in items:
                    hops[at, at + 1, item].start()
                    if at == 0:
                        hops[0, 3, item].start()

    pl.when(line == 0)(across_a.start)
    begin((0,))
    settle()
    pl.when(sends_b)(across_b.start)
    begin((1,))
    go_on()

    def finish():
        finish_relay(
            column, line, sends_b, gets_b, begin, hops, across_a, across_b, across
        )

    return finish


def finish_relay(column, line, sends_b, gets_b, begin, hops, across_a, across_b, across):
    pl.when(gets_b)(across_b.wait_recv)
    begin((2,))

    @pl.when(column == 1)
    def _():
        for item in range(3):
            hops[0, 1, item].wait_recv()
            if item == 0:
                across[0].start()

    @pl.when(column == 2)
    def _():
        for item in range(3):
            hops[1, 2, item].wait_recv()
            hops[1, 3, item].start()
            if item == 0:
                across[1].start()
        for item in range(3):
            hops[0, 2, item].wait_recv()
            if item == 0:
                across[0].start()

    @pl.when(column == 3)
    def _():
        for item in range(3):
            hops[0, 3, item].wait_recv()
            hops[0, 2, item].start()
            if item == 0:
                across[0].start()
        for source in (2, 1):
            for item in range(3):
                hops[source, 3, item].wait_recv()
                if item == 0:
                    across[source].start()

    pl.when(line == 0)(across_a.wait_send)
    pl.when(line == 1)(across_a.wait_recv)
    pl.when(sends_b)(across_b.wait_send)
    sent = (((0, 1), (0, 3)), ((1, 2),), ((2, 3), (1, 3)), ((0, 2),))
    for at in range(4):

        @pl.when(column == at)
        def _():
            for source, target in sent[at]:
                for item in range(3):
                    hops[source, target, item].wait_send()
            for source in range(at):
                across[source].wait()


def first_part(core, rows):
    return pl.ds(pl.multiple_of(core * (FR2 - rows), 16), rows)


def rest_part(core, rows):
    return pl.ds(pl.multiple_of((1 - core) * rows, 16), FR2 - rows)


def near_peers(seq, chip, core, tp):
    x, y = chip // 2, chip % 2
    return [
        (lax.rem(x + 1, 4) * 4 + y * 2 + core, tp),
        (lax.rem(x + 3, 4) * 4 + y * 2 + core, tp),
        (x * 4 + (1 - y) * 2 + core, tp),
        (x * 4 + y * 2 + 1 - core, tp),
    ]


def tp_peers(seq, tp, order=TP_ORDER):
    return [(seq, lax.rem(tp + hop, TP)) for hop in order]


def chip_peers(chip, core, tp, order=CHIP_ORDER):
    return [(lax.rem(chip + hop, CHIPS) * 2 + core, tp) for hop in order]


def keys_kernel(
    kv, query, out_w, kv_all, query_two, w_half, send_sems, recv_sems, sem, kv_bounce, query_bounce, w_bounce
):
    seq, chip, core, tp = place()
    peers = near_peers(seq, chip, core, tp)
    partner = peers[-1]
    half = pl.ds(core * FR, FR)
    own = pl.ds(pl.multiple_of(core * FR, FR), FR)
    jobs = [(kv.at[1 - core], kv_all.at[chip, own], partner)]
    jobs.append((query.at[1 - core], query_two.at[core], partner))
    for other in tp_peers(seq, tp):
        peers.append(other)
        jobs.append((out_w.at[other[1], half], w_half.at[tp], other))

    def part(item):
        return rest_part(core, KEY_FIRST) if item else first_part(core, KEY_FIRST)

    inner = pl.ds(pl.multiple_of(core * (FR - KEY_FIRST), 16), KEY_FIRST)

    def relay(base, send_sems, recv_sems, settle, go_on):
        def settle_both():
            for source, target in ((kv.at[core], kv_bounce), (kv_bounce, kv_all.at[chip, own])):
                copy = pltpu.make_async_copy(source, target, sem)
                copy.start()
                copy.wait()
            settle()

        return relay_blocks(
            lambda item: kv_all.at[chip, part(1)] if item else kv.at[core, inner],
            lambda source, item: kv_all.at[source, part(1 if item else 0)],
            False,
            base,
            send_sems,
            recv_sems,
            settle_both,
            go_on,
        )

    run_exchange(
        peers,
        jobs,
        [
            (query.at[core], query_bounce, query_two.at[core], sem),
            (out_w.at[tp, half], w_bounce, w_half.at[tp], sem),
        ],
        send_sems,
        recv_sems,
        relay=relay,
        relay_after=1,
    )


def exchange_keys(kv, query, out_w):
    return exchange(
        keys_kernel,
        "exchange_keys",
        1,
        (kv, query, out_w),
        [
            jax.ShapeDtypeStruct((CHIPS, FR2, 2 * HD), BF16),
            jax.ShapeDtypeStruct((2, FR, HD), BF16),
            jax.ShapeDtypeStruct((TP, FR, 2 * HD), BF16),
        ],
        9 + RELAY_COPIES,
        [((FR, 2 * HD), BF16), ((FR, HD), BF16), ((FR, 2 * HD), BF16)],
    )


def attended_kernel(source, w_half, target, w_other, send_sems, recv_sems, sem, bounce):
    seq, chip, core, tp = place()
    slot = tp * 2 + core
    partner_seq = chip * 2 + 1 - core
    partner = (partner_seq, tp)
    peers = [partner] + tp_peers(seq, tp) + tp_peers(partner_seq, tp)
    own = pl.ds(core * FR, FR)
    other = pl.ds((1 - core) * FR, FR)
    rows = [other] + [own] * (TP - 1) + [other] * (TP - 1)
    jobs = [(source.at[part], target.at[slot], peer) for part, peer in zip(rows, peers)]
    jobs.append((w_half, w_other, partner))
    run_exchange(
        peers, jobs, [(source.at[own], bounce, target.at[slot], sem)], send_sems, recv_sems
    )


def exchange_attended(attended, w_half):
    return exchange(
        attended_kernel,
        "exchange_attended",
        2,
        (attended, w_half),
        [
            jax.ShapeDtypeStruct((2 * TP, FR, HD), BF16),
            jax.ShapeDtypeStruct(w_half.shape, BF16),
        ],
        16,
        [((FR, HD), BF16)],
    )


def latent_kernel(
    source, att_all, merged, target, att_other, merged_other, send_sems, recv_sems, sem, bounce
):
    seq, chip, core, tp = place()
    partner = (chip * 2 + 1 - core, tp)
    peers = tp_peers(seq, tp)
    jobs = [(source.at[peer[1]], target.at[tp], peer) for peer in peers]
    jobs.append((att_all, att_other, partner))
    jobs.append((merged, merged_other, partner))
    run_exchange(
        peers + [partner],
        jobs,
        [(source.at[tp], bounce, target.at[tp], sem)],
        send_sems,
        recv_sems,
    )


def exchange_latent(parts, att_all, merged):
    return exchange(
        latent_kernel,
        "exchange_latent",
        3,
        (parts, att_all, merged),
        [
            jax.ShapeDtypeStruct(parts.shape, parts.dtype),
            jax.ShapeDtypeStruct(att_all.shape, BF16),
            jax.ShapeDtypeStruct(merged.shape, BF16),
        ],
        9,
        [(parts.shape[1:], parts.dtype)],
    )


def message_kernel(source, grads, target, grads_other, send_sems, recv_sems, sem, bounce):
    seq, chip, core, tp = place()
    partner = (chip * 2 + 1 - core, tp)
    peers = tp_peers(seq, tp)
    jobs = [(source, target.at[core, tp], peer) for peer in peers]
    forwards = []
    for number, hop in enumerate(TP_ORDER):
        slot = target.at[core, lax.rem(tp - hop + TP, TP)]
        forwards.append((number, (slot, slot, partner)))
    jobs.append((source, target.at[core, tp], partner))
    jobs.append((grads.at[:, 1 - core], grads_other, partner))
    run_exchange(
        peers + [partner],
        jobs,
        [(source, bounce, target.at[core, tp], sem)],
        send_sems,
        recv_sems,
        forwards,
    )


def exchange_message(message, grads):
    return exchange(
        message_kernel,
        "exchange_message",
        4,
        (message, grads),
        [
            jax.ShapeDtypeStruct((2, TP) + message.shape, message.dtype),
            jax.ShapeDtypeStruct((CHIPS, TP) + grads.shape[3:], BF16),
        ],
        16,
        [(message.shape, message.dtype)],
    )


def cotangent_kernel(
    source, side, grads, target, side_x, grads_z, send_sems, recv_sems, sem, bounce, side_bounce, grads_bounce
):
    seq, chip, core, tp = place()
    partner_seq = chip * 2 + 1 - core
    at_x, at_y = chip // 2, chip % 2
    row, depth_at = tp // 4, tp % 4
    peers = [(partner_seq, tp)] + tp_peers(seq, tp) + tp_peers(partner_seq, tp)
    heads = [1 - core] + [core] * (TP - 1) + [1 - core] * (TP - 1)
    jobs = [
        (source.at[peer[1] * 2 + head], target.at[core, tp], peer)
        for head, peer in zip(heads, peers)
    ]
    for hop in (2, 1, 3):
        there = lax.rem(at_x + hop, 4)
        other = (there * 4 + at_y * 2 + core, tp)
        peers.append(other)
        jobs.append((side.at[there], side_x.at[at_x], other))
    early = pl.ds(0, Z_EARLY)
    for hop in (2, 1, 3):
        there = lax.rem(depth_at + hop, 4)
        other = (seq, row * 4 + there)
        jobs.append((grads.at[early, :, there], grads_z.at[depth_at], other))
    run_exchange(
        peers,
        jobs,
        [
            (source.at[tp * 2 + core], bounce, target.at[core, tp], sem),
            (side.at[at_x], side_bounce, side_x.at[at_x], sem),
            (grads.at[early, :, depth_at], grads_bounce, grads_z.at[depth_at], sem),
        ],
        send_sems,
        recv_sems,
    )


def exchange_cotangent(parts, side, grads):
    slab = (Z_EARLY, 2) + grads.shape[3:]
    return exchange(
        cotangent_kernel,
        "exchange_cotangent",
        5,
        (parts, side, grads),
        [
            jax.ShapeDtypeStruct((2, TP, FR, HD), BF16),
            jax.ShapeDtypeStruct(side.shape, BF16),
            jax.ShapeDtypeStruct((4,) + slab, BF16),
        ],
        21,
        [((FR, HD), BF16), (side.shape[1:], BF16), (slab, BF16)],
    )


def grads_kernel(
    pair, stats, grads, side, normed, pair_all, stats_all, grads_z, side_in, normed_other,
    send_sems, recv_sems, sem, bounce, stats_bounce, grads_bounce,
):
    seq, chip, core, tp = place()
    row, depth_at = tp // 4, tp % 4
    at_x, at_y = chip // 2, chip % 2
    peers = []
    jobs = []
    for hop in CHIP_ORDER:
        there = lax.rem(chip + hop, CHIPS)
        here = lax.rem(chip - hop + CHIPS, CHIPS)
        other = (there * 2 + core, tp)
        peers.append(other)
        jobs.append((stats, stats_all.at[chip], other, there < chip, here > chip))
    for hop in (2, 1, 3):
        there = lax.rem(depth_at + hop, 4)
        other = (seq, row * 4 + there)
        peers.append(other)
        jobs.append((grads.at[pl.ds(Z_EARLY, Z_LATE), :, there], grads_z.at[depth_at], other))
    jobs.append((side.at[1 - at_y], side_in, (at_x * 4 + (1 - at_y) * 2 + core, tp)))
    partner = (chip * 2 + 1 - core, tp)
    jobs.append((normed, normed_other, partner))
    peers.append(partner)

    def part(item):
        return rest_part(core, PAIR_FIRST) if item else first_part(core, PAIR_FIRST)

    def relay(*rest):
        return relay_blocks(
            lambda item: pair.at[part(item)],
            lambda source, item: pair_all.at[source, part(item)],
            True,
            *rest,
        )

    run_exchange(
        peers,
        jobs,
        [
            (pair, bounce, pair_all.at[chip], sem),
            (stats, stats_bounce, stats_all.at[chip], sem),
            (
                grads.at[pl.ds(Z_EARLY, Z_LATE), :, depth_at],
                grads_bounce,
                grads_z.at[depth_at],
                sem,
            ),
        ],
        send_sems,
        recv_sems,
        relay=relay,
    )


def exchange_grads(pair, stats, grads, side, normed):
    slab = (Z_LATE, 2) + grads.shape[3:]
    return exchange(
        grads_kernel,
        "exchange_grads",
        6,
        (pair, stats, grads, side, normed),
        [
            jax.ShapeDtypeStruct((CHIPS,) + pair.shape, BF16),
            jax.ShapeDtypeStruct((CHIPS,) + stats.shape, F32),
            jax.ShapeDtypeStruct((4,) + slab, BF16),
            jax.ShapeDtypeStruct(side.shape[1:], BF16),
            jax.ShapeDtypeStruct(normed.shape, BF16),
        ],
        12 + RELAY_COPIES,
        [(pair.shape, BF16), (stats.shape, F32), (slab, BF16)],
    )


def first_kernel(
    x_first, y_first, grads, out, x_in, y_in, grads_x, out_all,
    send_sems, recv_sems, sem, x_bounce, y_bounce, grads_bounce, out_bounce,
):
    seq, chip, core, tp = place()
    at_x, at_y = chip // 2, chip % 2

    def device(x, y, c):
        return x * 4 + y * 2 + c, tp

    peers = []
    jobs = []
    for hop in (2, 1, 3):
        x = lax.rem(at_x + hop, 4)
        for c in (core, 1 - core):
            peers.append(device(x, at_y, c))
            jobs.append((x_first.at[x, c], x_in.at[at_x, core], peers[-1]))
    for c in (core, 1 - core):
        peers.append(device(at_x, 1 - at_y, c))
        jobs.append((y_first.at[1 - at_y, c], y_in.at[at_y, core], peers[-1]))
    for hop in (2, 1, 3):
        x = lax.rem(at_x + hop, 4)
        jobs.append((grads.at[x], grads_x.at[at_x], device(x, at_y, core)))
    for other in tp_peers(seq, tp):
        peers.append(other)
        jobs.append((out.at[other[1]], out_all.at[tp], other))
    peers.append(device(at_x, at_y, 1 - core))
    jobs.append((x_first.at[at_x, 1 - core], x_in.at[at_x, core], peers[-1]))
    jobs.append((y_first.at[at_y, 1 - core], y_in.at[at_y, core], peers[-1]))
    run_exchange(
        peers,
        jobs,
        [
            (x_first.at[at_x, core], x_bounce, x_in.at[at_x, core], sem),
            (y_first.at[at_y, core], y_bounce, y_in.at[at_y, core], sem),
            (grads.at[at_x], grads_bounce, grads_x.at[at_x], sem),
            (out.at[tp], out_bounce, out_all.at[tp], sem),
        ],
        send_sems,
        recv_sems,
    )


def exchange_first(x_first, y_first, grads, out):
    arrays = (x_first, y_first, grads, out)
    tails = (x_first.shape[2:], y_first.shape[2:], grads.shape[1:], out.shape[1:])
    return exchange(
        first_kernel,
        "exchange_first",
        7,
        arrays,
        [jax.ShapeDtypeStruct(array.shape, BF16) for array in arrays],
        20,
        [(tail, BF16) for tail in tails],
    )


def second_kernel(
    x_sum, y_sum, grads, x_in, y_in, grads_in, send_sems, recv_sems, sem, y_bounce, grads_bounce
):
    seq, chip, core, tp = place()
    at_x, at_y = chip // 2, chip % 2
    row, depth_at = tp // 4, tp % 4
    peers = []
    jobs = []
    for hop in (2, 1, 3):
        x = lax.rem(at_x + hop, 4)
        peers.append((x * 4 + at_y * 2 + core, tp))
        jobs.append((y_sum.at[x], y_in.at[at_x], peers[-1]))
    peers.append((at_x * 4 + (1 - at_y) * 2 + core, tp))
    jobs.append((x_sum.at[1 - at_y], x_in, peers[-1]))
    jobs.append((grads.at[1 - at_y, row], grads_in.at[at_y, row], peers[-1]))
    for y in (at_y, 1 - at_y):
        peers.append((at_x * 4 + y * 2 + core, (1 - row) * 4 + depth_at))
        jobs.append((grads.at[y, 1 - row], grads_in.at[at_y, row], peers[-1]))
    run_exchange(
        peers,
        jobs,
        [
            (y_sum.at[at_x], y_bounce, y_in.at[at_x], sem),
            (grads.at[at_y, row], grads_bounce, grads_in.at[at_y, row], sem),
        ],
        send_sems,
        recv_sems,
    )


def exchange_second(x_sum, y_sum, grads):
    return exchange(
        second_kernel,
        "exchange_second",
        8,
        (x_sum, y_sum, grads),
        [
            jax.ShapeDtypeStruct(x_sum.shape[1:], BF16),
            jax.ShapeDtypeStruct(y_sum.shape, BF16),
            jax.ShapeDtypeStruct(grads.shape, BF16),
        ],
        7,
        [(y_sum.shape[1:], BF16), (grads.shape[2:], BF16)],
    )


def compute(kernel, name, ins, outs, scratch=(), limit=48, hbm=0):
    return pl.pallas_call(
        kernel,
        name=name,
        out_shape=outs,
        in_specs=[VMEM] * (len(ins) - hbm) + [HBM] * hbm,
        out_specs=[VMEM] * len(outs),
        scratch_shapes=list(scratch),
        compiler_params=pltpu.CompilerParams(vmem_limit_bytes=limit * MIB),
    )(*ins)


START_STEPS = 8


def start_kernel(
    hidden_ref, cos_ref, sin_ref, w_hbm, normed_ref, kv_ref, query_ref, out_w_ref, total_ref, w_ref, sems
):
    depth_rows = w_ref.shape[1]
    copies = [
        fetch(w_hbm.at[pl.ds(step * depth_rows, depth_rows)], w_ref.at[step], sems.at[step])
        for step in range(START_STEPS)
    ]
    hidden = hidden_ref[...].astype(F32)
    normed_ref[...] = (hidden * rms_scale(hidden)).astype(BF16)
    pieces = depth_rows // (TP * 32)
    for step in range(START_STEPS):
        copies[step].wait()
        weights = w_ref[step].reshape(depth_rows, 8 * HD)
        normed = normed_ref[:, step * depth_rows : (step + 1) * depth_rows]
        term = dot_nn(normed, weights[:, : 6 * HD])
        if step:
            total_ref[...] += term
        else:
            total_ref[...] = term
        out_w = weights[:, 6 * HD :].reshape(pieces, TP, 32, 2 * HD)
        for at in range(TP):
            for piece in range(pieces):
                low = (step * pieces + piece) * 32
                out_w_ref[at, low : low + 32] = out_w[piece, at]
    own = pl.ds(pl.multiple_of(lax.axis_index("seq") % 2 * FR, FR), FR)
    cosine, sine = cos_ref[own], sin_ref[own]

    def turned(at):
        lower = total_ref[:, at : at + HD // 2]
        upper = total_ref[:, at + HD // 2 : at + HD]
        return jnp.concatenate(
            [lower * cosine - upper * sine, upper * cosine + lower * sine], axis=1
        ).astype(BF16)

    for head in range(2):
        query_ref[head] = turned(head * HD)
        kv_ref[head, :, :HD] = turned((2 + head) * HD)
        at = (4 + head) * HD
        kv_ref[head, :, HD:] = total_ref[:, at : at + HD].astype(BF16)


def start(hidden, weights, cosine, sine):
    depth_rows = weights.shape[0] // START_STEPS
    return compute(
        start_kernel,
        "start",
        (hidden, cosine, sine, weights),
        [
            jax.ShapeDtypeStruct(hidden.shape, BF16),
            jax.ShapeDtypeStruct((2, FR, 2 * HD), BF16),
            jax.ShapeDtypeStruct((2, FR, HD), BF16),
            jax.ShapeDtypeStruct((TP, NS, 2 * HD), BF16),
        ],
        [
            pltpu.VMEM((FR, 6 * HD), F32),
            pltpu.VMEM((START_STEPS, depth_rows) + weights.shape[1:], BF16),
            pltpu.SemaphoreType.DMA((START_STEPS,)),
        ],
        hbm=1,
        limit=32,
    )


def attend_kernel(kv_ref, query_ref, out_ref, out_t_ref, level_ref, score_ref):
    chip = lax.axis_index("seq") // 2
    query = query_ref[...]
    key_at = lax.broadcasted_iota(jnp.int32, (FR2, FR2), 0)
    query_at = lax.broadcasted_iota(jnp.int32, (FR2, FR2), 1)

    def scores(block, top):
        score = dot_nt(kv_ref[block, :, :HD], query) * LOG_SCALE
        score_ref[block] = score
        return jnp.maximum(top, jnp.max(score, axis=0, keepdims=True))

    score = dot_nt(kv_ref[chip, :, :HD], query) * LOG_SCALE
    score = jnp.where(key_at <= query_at, score, MASKED)
    score_ref[chip] = score
    top = lax.fori_loop(0, chip, scores, jnp.max(score, axis=0, keepdims=True))

    def weigh(block, carry):
        total, mixed = carry
        prob = jnp.exp2(score_ref[block] - top)
        total = total + jnp.sum(prob, axis=0, keepdims=True)
        return total, mixed + dot_tn(kv_ref[block, :, HD:], prob.astype(BF16))

    total, mixed = lax.fori_loop(
        0, chip + 1, weigh, (jnp.zeros((1, FR2), F32), jnp.zeros((HD, FR2), F32))
    )
    mixed = mixed * (1.0 / total)
    out_t_ref[...] = mixed
    level_ref[...] = top + jnp.log2(total)
    out_ref[...] = mixed.T.astype(BF16)


def attend(kv_all, query):
    return compute(
        attend_kernel,
        "attend",
        (kv_all, query),
        [
            jax.ShapeDtypeStruct((FR2, HD), BF16),
            jax.ShapeDtypeStruct((HD, FR2), F32),
            jax.ShapeDtypeStruct((1, FR2), F32),
        ],
        [pltpu.VMEM((CHIPS, FR2, FR2), F32)],
        limit=20,
    )


def fetch(source, target, sem):
    copy = pltpu.make_async_copy(source, target, sem)
    copy.start()
    return copy


def order_halves(core, mine, other):
    return jnp.where(core == 0, mine, other), jnp.where(core == 0, other, mine)


def merge_kernel(
    att_ref, half_ref, other_ref, hidden_ref, depth_in_hbm, stack_hbm,
    merged_ref, round_ref, part_ref, stack_ref, depth_in_ref, sem, stack_sem,
):
    seq, chip, core, tp = place()
    copy = fetch(depth_in_hbm.at[:, tp], depth_in_ref, sem)
    stack_copy = fetch(stack_hbm, stack_ref, stack_sem)
    width = hidden_ref.shape[1]
    group = width // 2
    row_at = lax.broadcasted_iota(jnp.int32, (group, FR), 0)
    col_at = lax.broadcasted_iota(jnp.int32, (group, FR), 1)
    wanted = (col_at // 32) * 256 + tp * 32 + col_at % 32
    pick = jnp.where(row_at == wanted, 1.0, 0.0).astype(BF16)
    merged = jnp.concatenate(
        [dot_nn(hidden_ref[:, :group], pick), dot_nn(hidden_ref[:, group:], pick)], axis=1
    )
    mine = jnp.zeros((FR, FR), F32)
    other = jnp.zeros((FR, FR), F32)
    for at in range(TP):
        pair = jnp.concatenate([att_ref[2 * at], att_ref[2 * at + 1]], axis=1)
        mine = mine + dot_nt(pair, half_ref[at])
        other = other + dot_nt(pair, other_ref[at])
    merged = merged + jnp.concatenate(order_halves(core, mine, other), axis=1)
    rounded = merged.astype(BF16)
    merged_ref[...] = merged
    round_ref[...] = rounded
    squares = jnp.sum(merged * merged, axis=-1, keepdims=True)
    copy.wait()
    latent = dot_nn(rounded, depth_in_ref[...].reshape(NS, DD))
    coarse = squares.astype(BF16)
    fine = (squares - coarse.astype(F32)).astype(BF16)
    part_ref[:, :, :DD] = latent.astype(BF16).reshape(TP, FR // TP, DD)
    part_ref[:, :, DD : DD + HD] = jnp.broadcast_to(coarse, (FR, HD)).reshape(TP, FR // TP, HD)
    part_ref[:, :, DD + HD :] = jnp.broadcast_to(fine, (FR, HD)).reshape(TP, FR // TP, HD)
    stack_copy.wait()


def merge(att_all, w_half, w_other, hidden, depth_in, stack):
    return compute(
        merge_kernel,
        "merge",
        (att_all, w_half, w_other, hidden, depth_in, stack),
        [
            jax.ShapeDtypeStruct((FR, NS), F32),
            jax.ShapeDtypeStruct((FR, NS), BF16),
            jax.ShapeDtypeStruct((TP, FR // TP, DD + 2 * HD), BF16),
            jax.ShapeDtypeStruct(stack.shape, BF16),
        ],
        [
            pltpu.VMEM((2 * CHIPS, 32, DD), BF16),
            pltpu.SemaphoreType.DMA,
            pltpu.SemaphoreType.DMA,
        ],
        hbm=2,
        limit=24,
    )


def depth_kernel(
    width, loss_scale, part_ref, code_ref, stack_ref, message_ref, grad_ref, prob_ref
):
    books, frames = code_ref.shape
    grid = (frames, books, books)
    row_at = lax.broadcasted_iota(jnp.int32, grid, 1)
    col_at = lax.broadcasted_iota(jnp.int32, grid, 2)
    spread = jnp.broadcast_to(code_ref[...].astype(F32).T[:, None, :], grid)

    def column(wanted):
        picked = jnp.where(wanted, spread + 1.0, 0.0)
        picked = jnp.sum(picked, axis=-1, keepdims=True).reshape(frames * books, 1)
        return picked - 1.0

    codes = column(col_at == row_at)
    before = column(col_at == row_at - 1)
    tokens = frames * books
    total = jnp.sum(part_ref[...].astype(F32), axis=0)
    raw = total[:, :DD]
    squares = total[:, DD : DD + 1] + total[:, DD + HD : DD + HD + 1]
    scale_in = lax.rsqrt(squares * (1.0 / width) + EPSILON)
    latent = raw * scale_in
    latent = jnp.broadcast_to(latent[:, None, :], (frames, books, DD)).reshape(tokens, DD)
    vocab_at = lax.broadcasted_iota(jnp.int32, (tokens, VOCAB), 1).astype(F32)
    hot = jnp.where(before == vocab_at, 1.0, 0.0).astype(BF16)
    stream = latent + dot_nn(hot, stack_ref[4 * DD + VOCAB :])
    stream_scale = rms_scale(stream)
    stream_norm = (stream * stream_scale).astype(BF16)
    qkv_rows = stack_ref[: 3 * DD]
    proj = dot_nt(stream_norm, qkv_rows).astype(BF16)
    row_at = lax.broadcasted_iota(jnp.int32, (tokens, tokens), 0)
    col_at = lax.broadcasted_iota(jnp.int32, (tokens, tokens), 1)
    allowed = (row_at // books == col_at // books) & (col_at <= row_at)
    depth_scale = 1.0 / math.sqrt(DHD)
    mixed = []
    for head in range(DD // DHD):
        low = head * DHD
        queries = proj[:, low : low + DHD]
        keys = proj[:, DD + low : DD + low + DHD]
        values = proj[:, 2 * DD + low : 2 * DD + low + DHD]
        scores = jnp.where(allowed, dot_nt(queries, keys) * depth_scale, MASKED)
        weights = jnp.exp(scores - jnp.max(scores, axis=-1, keepdims=True))
        probs = weights / jnp.sum(weights, axis=-1, keepdims=True)
        prob_ref[head] = probs
        mixed.append(dot_nn(probs.astype(BF16), values))
    mixed = jnp.concatenate(mixed, axis=1).astype(BF16)
    out_rows = stack_ref[3 * DD : 4 * DD]
    resid = stream + dot_nt(mixed, out_rows)
    resid_scale = rms_scale(resid)
    resid_norm = (resid * resid_scale).astype(BF16)
    head_rows = stack_ref[4 * DD : 4 * DD + VOCAB]
    logits = dot_nt(resid_norm, head_rows)
    weights = jnp.exp(logits - jnp.max(logits, axis=-1, keepdims=True))
    logit_probs = weights / jnp.sum(weights, axis=-1, keepdims=True)
    target = jnp.where(codes == vocab_at, 1.0, 0.0)
    logit_grad = ((logit_probs - target) * loss_scale).astype(BF16)
    grad_ref[4 * DD : 4 * DD + VOCAB] = dot_tn(logit_grad, resid_norm).astype(BF16)
    resid_grad = norm_back(resid, resid_scale, dot_nn(logit_grad, head_rows))
    resid_round = resid_grad.astype(BF16)
    grad_ref[3 * DD : 4 * DD] = dot_tn(resid_round, mixed).astype(BF16)
    mixed_grad = dot_nn(resid_round, out_rows).astype(BF16)
    query_grad, key_grad, value_grad = [], [], []
    for head in range(DD // DHD):
        low = head * DHD
        queries = proj[:, low : low + DHD]
        keys = proj[:, DD + low : DD + low + DHD]
        values = proj[:, 2 * DD + low : 2 * DD + low + DHD]
        probs = prob_ref[head]
        mix_grad = mixed_grad[:, low : low + DHD]
        value_grad.append(dot_tn(probs.astype(BF16), mix_grad))
        prob_grad = dot_nt(mix_grad, values)
        inner = jnp.sum(probs * prob_grad, axis=-1, keepdims=True)
        score_grad = (probs * (prob_grad - inner) * depth_scale).astype(BF16)
        query_grad.append(dot_nn(score_grad, keys))
        key_grad.append(dot_tn(score_grad, queries))
    proj_grad = jnp.concatenate(query_grad + key_grad + value_grad, axis=1).astype(BF16)
    grad_ref[: 3 * DD] = dot_tn(proj_grad, stream_norm).astype(BF16)
    stream_grad = resid_grad + norm_back(stream, stream_scale, dot_nn(proj_grad, qkv_rows))
    grad_ref[4 * DD + VOCAB :] = dot_tn(hot, stream_grad.astype(BF16)).astype(BF16)
    latent_grad = jnp.sum(stream_grad.reshape(frames, books, DD), axis=1)
    latent_grad = latent_grad.astype(BF16).astype(F32)
    inner = jnp.sum(latent_grad * raw, axis=-1, keepdims=True) * (1.0 / width)
    pull = scale_in * scale_in * scale_in * inner
    coarse = pull.astype(BF16)
    fine = (pull - coarse.astype(F32)).astype(BF16)
    message_ref[:, :DD] = (latent_grad * scale_in).astype(BF16)
    message_ref[:, DD : DD + HD] = jnp.broadcast_to(coarse, (frames, HD))
    message_ref[:, DD + HD :] = jnp.broadcast_to(fine, (frames, HD))


def depth(parts, codes, stack, width, loss_scale):
    tokens = codes.shape[0] * codes.shape[1]
    return compute(
        functools.partial(depth_kernel, width, loss_scale),
        "depth",
        (parts, codes, stack),
        [
            jax.ShapeDtypeStruct((parts.shape[1], DD + 2 * HD), BF16),
            jax.ShapeDtypeStruct(stack.shape, BF16),
        ],
        [
            pltpu.VMEM((DD // DHD, tokens, tokens), F32),
        ],
        limit=32,
    )


def merged_gradient(message, merged, depth_in):
    pull = message[:, DD : DD + 1].astype(F32) + message[:, DD + HD : DD + HD + 1].astype(F32)
    return dot_nt(message[:, :DD], depth_in) - merged * pull


def unmerge_kernel(
    message_ref,
    merged_ref,
    round_ref,
    round_other_ref,
    att_ref,
    att_other_ref,
    half_ref,
    other_ref,
    grads_other_ref,
    grads_hbm,
    depth_in_hbm,
    part_ref,
    side_ref,
    grads_ref,
    depth_in_ref,
    grads_own_ref,
    sems,
):
    seq, chip, core, tp = place()
    copy = fetch(depth_in_hbm.at[:, tp], depth_in_ref, sems.at[0])
    grads_copy = fetch(grads_hbm.at[:, core], grads_own_ref, sems.at[1])
    copy.wait()
    depth_in = depth_in_ref[...].reshape(NS, DD)
    message = message_ref[core].reshape(FR, DD + 2 * HD)
    message_other = message_ref[1 - core].reshape(FR, DD + 2 * HD)
    gradient = merged_gradient(message, merged_ref[...], depth_in)
    lower, upper = gradient[:, :FR], gradient[:, FR:]
    mine, other = order_halves(core, lower, upper)
    mine, other = mine.astype(BF16), other.astype(BF16)
    for at in range(TP):
        pair = (dot_nn(mine, half_ref[at]) + dot_nn(other, other_ref[at])).astype(BF16)
        part_ref[2 * at] = pair[:, :HD]
        part_ref[2 * at + 1] = pair[:, HD:]
    gradient_other = merged_gradient(
        message_other, round_other_ref[...].astype(F32), depth_in
    )

    def pick_rows(own, others):
        both = jnp.concatenate([own.T, others.T], axis=1).reshape(CHIPS, 2, 32, FR2)
        both = jnp.where(core == 0, both[:, 0], both[:, 1])
        return both.reshape(FR, FR2).astype(BF16)

    rows = pick_rows(gradient, gradient_other)
    for at in range(TP):
        pair = jnp.concatenate([att_ref[2 * at], att_ref[2 * at + 1]], axis=1)
        pair_other = jnp.concatenate([att_other_ref[2 * at], att_other_ref[2 * at + 1]], axis=1)
        term = dot_nn(rows, jnp.concatenate([pair, pair_other], axis=0)).astype(BF16)
        side_ref[:, :, at * FR : (at + 1) * FR] = term.reshape(CHIPS, 32, FR)
    rows = pick_rows(round_ref[...].astype(F32), round_other_ref[...].astype(F32))
    both = jnp.concatenate([message[:, :DD], message_other[:, :DD]], axis=0)
    side_ref[:, :, TP * FR :] = dot_nn(rows, both).astype(BF16).reshape(CHIPS, 32, DD)
    grads_copy.wait()
    for at in range(CHIPS):
        grads_ref[at] = (
            grads_own_ref[at].astype(F32) + grads_other_ref[at].astype(F32)
        ).astype(BF16)


def unmerge(
    messages, merged, rounded, rounded_other, att_all, att_other, w_half, w_other, grads_other, grads, depth_in
):
    return compute(
        unmerge_kernel,
        "unmerge",
        (
            messages,
            merged,
            rounded,
            rounded_other,
            att_all,
            att_other,
            w_half,
            w_other,
            grads_other,
            grads,
            depth_in,
        ),
        [
            jax.ShapeDtypeStruct((2 * TP, FR, HD), BF16),
            jax.ShapeDtypeStruct((CHIPS, 32, TP * FR + DD), BF16),
            jax.ShapeDtypeStruct(grads_other.shape, BF16),
        ],
        [
            pltpu.VMEM((2 * CHIPS, 32, DD), BF16),
            pltpu.VMEM(grads_other.shape, BF16),
            pltpu.SemaphoreType.DMA((2,)),
        ],
        hbm=2,
        limit=28,
    )


def prepare_kernel(
    part_ref, query_ref, out_t_ref, level_ref, side_x_ref, pair_ref, stats_ref, side_ref
):
    gradient = jnp.sum(part_ref[...].astype(F32), axis=1).reshape(FR2, HD).astype(BF16)
    pair_ref[:, :HD] = query_ref[...]
    pair_ref[:, HD:] = gradient
    inner = jnp.sum(gradient.astype(F32).T * out_t_ref[...], axis=0, keepdims=True)
    stats_ref[...] = jnp.concatenate(
        [level_ref[...], inner, jnp.zeros((6, FR2), F32)], axis=0
    )
    side_ref[...] = jnp.sum(side_x_ref[...].astype(F32), axis=0).astype(BF16)


def prepare(parts, query, out_t, level, side_x):
    return compute(
        prepare_kernel,
        "prepare",
        (parts, query, out_t, level, side_x),
        [
            jax.ShapeDtypeStruct((FR2, 2 * HD), BF16),
            jax.ShapeDtypeStruct((8, FR2), F32),
            jax.ShapeDtypeStruct(side_x.shape[1:], BF16),
        ],
        limit=16,
    )


def attend_back_kernel(
    stats_ref, cos_ref, sin_ref, side_ref, side_in_ref, kv_hbm, pair_hbm, early_hbm, late_hbm,
    normed_hbm, other_hbm, x_ref, y_ref, grads_ref, win_ref, out_w_ref,
    kv_ref, pair_ref, early_ref, late_ref, normed_ref, other_ref, sems,
):
    chip = lax.axis_index("seq") // 2
    core = lax.axis_index("seq") % 2
    places = (
        (kv_hbm, kv_ref),
        (pair_hbm, pair_ref),
        (normed_hbm, normed_ref),
        (other_hbm, other_ref),
        (early_hbm, early_ref),
        (late_hbm, late_ref),
    )
    copies = [fetch(source, target, sems.at[at]) for at, (source, target) in enumerate(places)]
    copies[0].wait()
    copies[1].wait()
    scale = 1.0 / math.sqrt(HD)

    def pair(queries, keys, diagonal):
        query = pair_ref[queries, :, :HD]
        gradient = pair_ref[queries, :, HD:]
        score = dot_nt(kv_ref[keys, :, :HD], query) * LOG_SCALE
        if diagonal:
            key_at = lax.broadcasted_iota(jnp.int32, (FR2, FR2), 0)
            query_at = lax.broadcasted_iota(jnp.int32, (FR2, FR2), 1)
            score = jnp.where(key_at <= query_at, score, MASKED)
        prob = jnp.exp2(score - stats_ref[queries, 0:1])
        prob_grad = dot_nt(kv_ref[keys, :, HD:], gradient)
        score_grad = (prob * (prob_grad - stats_ref[queries, 1:2])).astype(BF16)
        return query, gradient, prob.astype(BF16), score_grad

    def own_queries(block, total):
        score_grad = pair(chip, block, False)[3]
        return total + dot_tn(kv_ref[block, :, :HD], score_grad)

    def own_keys(block, totals):
        query, gradient, prob, score_grad = pair(block, chip, False)
        return totals[0] + dot_nn(score_grad, query), totals[1] + dot_nn(prob, gradient)

    query, gradient, prob, score_grad = pair(chip, chip, True)
    query_grad = dot_tn(kv_ref[chip, :, :HD], score_grad)
    key_grad = dot_nn(score_grad, query)
    value_grad = dot_nn(prob, gradient)
    query_grad = lax.fori_loop(0, chip, own_queries, query_grad)
    key_grad, value_grad = lax.fori_loop(chip + 1, CHIPS, own_keys, (key_grad, value_grad))
    query_grad = query_grad.T
    cosine, sine = cos_ref[...] * scale, sin_ref[...] * scale

    def turned(total):
        lower, upper = total[:, : HD // 2], total[:, HD // 2 :]
        return [lower * cosine + upper * sine, upper * cosine - lower * sine]

    proj = jnp.concatenate(turned(query_grad) + turned(key_grad) + [value_grad], axis=1)
    proj_t = proj.T
    own, other = order_halves(core, proj_t[:, :FR], proj_t[:, FR:])
    own, other = own.astype(BF16), other.astype(BF16)
    copies[2].wait()
    copies[3].wait()
    for piece in range(2 * CHIPS):
        low = piece * FR
        term = dot_nn(own, normed_ref[:, low : low + FR])
        term = (term + dot_nn(other, other_ref[:, low : low + FR])).astype(BF16)
        x, y, c = piece // 4, piece // 2 % 2, piece % 2
        x_ref[x, c, y] = term[:X_ROWS]
        y_ref[y, c, x] = term[X_ROWS:]
    copies[4].wait()
    copies[5].wait()
    for at in range(CHIPS):
        term = early_ref[:, at] if at < Z_EARLY else late_ref[:, at - Z_EARLY]
        grads_ref[at] = jnp.sum(term.astype(F32), axis=0).astype(BF16)
    side = side_ref[chip % 2].astype(F32) + side_in_ref[...].astype(F32)
    win_ref[...] = side[:, TP * FR :]
    for at in range(TP):
        out_w_ref[at] = side[:, at * FR : (at + 1) * FR].astype(BF16)


def attend_back(
    stats_all, cosine, sine, side, side_in, kv_all, pair_all, early, late, normed, normed_other
):
    streamed = (kv_all, pair_all, early, late, normed, normed_other)
    return compute(
        attend_back_kernel,
        "attend_back",
        (stats_all, cosine, sine, side, side_in) + streamed,
        [
            jax.ShapeDtypeStruct((4, 2, 2, X_ROWS, FR), BF16),
            jax.ShapeDtypeStruct((2, 2, 4, Y_ROWS, FR), BF16),
            jax.ShapeDtypeStruct((CHIPS,) + late.shape[2:], BF16),
            jax.ShapeDtypeStruct((32, DD), F32),
            jax.ShapeDtypeStruct((TP, 32, FR), BF16),
        ],
        [pltpu.VMEM(array.shape, BF16) for array in streamed] + [pltpu.SemaphoreType.DMA((6,))],
        hbm=6,
        limit=36,
    )


def middle_kernel(x_ref, y_ref, grads_x_ref, x_sum_ref, y_sum_ref, grads_ref):
    for y in range(2):
        for c in range(2):
            terms = [x_ref[x, c, y].astype(F32) for x in range(4)]
            x_sum_ref[y, c] = (terms[0] + terms[1] + terms[2] + terms[3]).astype(BF16)
    for x in range(4):
        for c in range(2):
            term = y_ref[0, c, x].astype(F32) + y_ref[1, c, x].astype(F32)
            y_sum_ref[x, c] = term.astype(BF16)
    grads_ref[...] = jnp.sum(grads_x_ref[...].astype(F32), axis=0).astype(BF16)


def middle_sum(x_in, y_in, grads_x):
    return compute(
        middle_kernel,
        "middle_sum",
        (x_in, y_in, grads_x),
        [
            jax.ShapeDtypeStruct((2, 2, X_ROWS, FR), BF16),
            jax.ShapeDtypeStruct((4, 2, Y_ROWS, FR), BF16),
            jax.ShapeDtypeStruct(grads_x.shape[1:], BF16),
        ],
        limit=16,
    )


def last_kernel(x_own_ref, x_in_ref, y_in_ref, grads_ref, out_w_ref, out_ref, depth_ref):
    at_y = lax.axis_index("seq") // 2 % 2
    totals = []
    for head in range(2):
        x_part = x_own_ref[at_y, head].astype(F32) + x_in_ref[head].astype(F32)
        terms = [y_in_ref[x, head].astype(F32) for x in range(4)]
        y_part = terms[0] + terms[1] + terms[2] + terms[3]
        totals.append(jnp.concatenate([x_part, y_part], axis=0).T)
    pieces = [totals[head][:, kind * HD : (kind + 1) * HD] for kind in range(3) for head in range(2)]
    pieces.append(out_w_ref[...].astype(F32).reshape(FR, 2 * HD))
    out_ref[...] = jnp.concatenate(pieces, axis=1).reshape(FR, 4, 2 * HD)
    depth_ref[...] = jnp.sum(jnp.sum(grads_ref[...].astype(F32), axis=0), axis=0)


def last_sum(x_own, x_in, y_in, grads, out_all):
    return compute(
        last_kernel,
        "last_sum",
        (x_own, x_in, y_in, grads, out_all),
        [
            jax.ShapeDtypeStruct((FR, 4, 2 * HD), F32),
            jax.ShapeDtypeStruct(grads.shape[2:], F32),
        ],
        limit=16,
    )


def per_device(hidden_in, temporal_weight_stack, depth_in, depth_stack, audio_codes):
    seq_index = lax.axis_index("seq")
    tp_index = lax.axis_index("tp")
    chip = seq_index // 2
    width = hidden_in.shape[1]
    depth_frames, book_count = audio_codes.shape
    seq_count = 2 * CHIPS
    total_frames = FR * seq_count
    loss_scale = 1.0 / math.sqrt(total_frames * book_count)

    cosine, sine = angle_tables(chip * FR2, FR2)
    normed, kv, query, out_w = start(hidden_in, temporal_weight_stack, cosine, sine)
    kv_all, query, w_half = exchange_keys(kv, query, out_w)
    query = query.reshape(FR2, HD)

    depth_in = depth_in.reshape(seq_count, TP, -1, DD)
    attended, out_t, level = attend(kv_all, query)
    att_all, w_other = exchange_attended(attended, w_half)
    merged, rounded, latent_parts, depth_stack = merge(
        att_all, w_half, w_other, hidden_in, depth_in, depth_stack
    )
    latent_parts, att_other, rounded_other = exchange_latent(latent_parts, att_all, rounded)
    message, grads = depth(latent_parts, audio_codes.T, depth_stack, width, loss_scale)
    grads = grads.reshape(CHIPS, 2, TP, -1, DD)
    messages, grads_other = exchange_message(message, grads)
    cotangent_parts, side, grads = unmerge(
        messages,
        merged,
        rounded,
        rounded_other,
        att_all,
        att_other,
        w_half,
        w_other,
        grads_other,
        grads,
        depth_in,
    )
    grads = grads.reshape(CHIPS, 2, 4, -1, DD)
    cotangent_parts, side, early = exchange_cotangent(
        cotangent_parts, side.reshape(4, 2, 32, -1), grads
    )
    pair, stats, side = prepare(cotangent_parts, query, out_t, level, side)
    pair_all, stats_all, late, side_in, normed_other = exchange_grads(
        pair, stats, grads, side, normed
    )
    x_first, y_first, grads, grad_win, out_parts = attend_back(
        stats_all,
        cosine,
        sine,
        side,
        side_in,
        kv_all,
        pair_all,
        early,
        late,
        normed,
        normed_other,
    )
    x_in, y_in, grads, out_all = exchange_first(
        x_first, y_first, grads.reshape(4, 2, 2, -1, DD), out_parts
    )
    x_own, y_sum, grads = middle_sum(x_in, y_in, grads)
    x_in, y_in, grads = exchange_second(x_own, y_sum, grads)
    grad_temporal, grad_depth = last_sum(x_own, x_in, y_in, grads, out_all)
    return grad_temporal, grad_win, grad_depth


def solution(mesh):
    in_specs = (P("seq", None), P(None, None, "tp"), P(), P(), P(("seq", "tp"), None))
    out_specs = (P("seq", None, "tp"), P(("seq", "tp"), None), P(("seq", "tp"), None))
    return jax.shard_map(
        per_device, mesh=mesh, in_specs=in_specs, out_specs=out_specs, check_vma=False
    )
```

```python
import functools
import math

import jax
import jax.numpy as jnp
from jax import lax
from jax.experimental import pallas as pl
from jax.experimental.pallas import tpu as pltpu
from jax.sharding import PartitionSpec as P

HD = 128
DHD = 64
VOCAB = 1024
CHIPS = 8
TP = 8
FR = 256
FR2 = 512
DD = 512
NS = 512

EPSILON = 1e-05
MASKED = -1e30
ROPE_BASE = 10000.0
MIB = 2**20
MESH = pl.DeviceIdType.MESH
F32 = jnp.float32
BF16 = jnp.bfloat16
ANY = pl.BlockSpec(memory_space=pl.ANY)
VMEM = pl.BlockSpec(memory_space=pltpu.VMEM)
HBM = pl.BlockSpec(memory_space=pltpu.HBM)
TP_ORDER = (4, 1, 3, 5, 7, 2, 6)
CHIP_ORDER = (2, 6, 1, 4, 3, 7, 5)
LOG_SCALE = math.log2(math.e) / math.sqrt(HD)
Z_EARLY = 1
Z_LATE = CHIPS - Z_EARLY
KEY_FIRST = 128
PAIR_FIRST = 256
X_ROWS = 176
Y_ROWS = 208


def dot_nn(left, right):
    return jnp.dot(left, right, preferred_element_type=F32)


def dot_nt(left, right):
    return lax.dot_general(left, right, (((1,), (1,)), ((), ())), preferred_element_type=F32)


def dot_tn(left, right):
    return lax.dot_general(left, right, (((0,), (0,)), ((), ())), preferred_element_type=F32)


def rms_scale(values):
    return lax.rsqrt(jnp.mean(values * values, axis=-1, keepdims=True) + EPSILON)


def norm_back(values, scaling, gradient):
    inner_mean = jnp.mean(gradient * values, axis=-1, keepdims=True)
    return scaling * (gradient - values * (scaling * scaling) * inner_mean)


def angle_tables(first, count):
    half_width = HD // 2
    frequency = ROPE_BASE ** (-jnp.arange(half_width).astype(F32) / half_width)
    positions = (first + jnp.arange(count)).astype(F32)
    angles = positions[:, None] * frequency[None, :]
    return jnp.cos(angles), jnp.sin(angles)


def place():
    seq = lax.axis_index("seq")
    tp = lax.axis_index("tp")
    return seq, seq // 2, seq % 2, tp


def run_exchange(
    peers, jobs, locals_, send_sems, recv_sems, forwards=(), relay=None, relay_after=0
):
    barrier = pltpu.get_barrier_semaphore()
    for peer in peers:
        pl.semaphore_signal(barrier, inc=1, device_id=peer, device_id_type=MESH)
    pl.semaphore_wait(barrier, len(peers))
    copies = []
    arrived = set()

    def begin(source, target, device, *when):
        number = len(copies)
        copy = pltpu.make_async_remote_copy(
            src_ref=source,
            dst_ref=target,
            send_sem=send_sems.at[number],
            recv_sem=recv_sems.at[number],
            device_id=device,
            device_id_type=MESH,
        )
        if when:
            pl.when(when[0])(copy.start)
        else:
            copy.start()
        copies.append((copy, when))

    first = jobs if relay is None else jobs[:relay_after]
    for job in first:
        begin(*job)
    if relay is not None:
        total = len(jobs)

        def settle():
            for number in range(relay_after):
                copies[number][0].wait_recv()
                arrived.add(number)

        def go_on():
            for job in jobs[relay_after:]:
                begin(*job)

        finish = relay(total, send_sems, recv_sems, settle, go_on)
    for source, bounce, target, sem in locals_:
        copy = pltpu.make_async_copy(source, bounce, sem)
        copy.start()
        copy.wait()
        copy = pltpu.make_async_copy(bounce, target, sem)
        copy.start()
        copy.wait()
    for number, job in forwards:
        copies[number][0].wait_recv()
        arrived.add(number)
        begin(*job)
    if relay is not None:
        finish()
    for number, (copy, when) in enumerate(copies):
        if when:
            pl.when(when[0])(copy.wait_send)
            pl.when(when[1])(copy.wait_recv)
        else:
            copy.wait_send()
            if number not in arrived:
                copy.wait_recv()


def exchange(kernel, name, collective_id, ins, outs, copies, bounces):
    return pl.pallas_call(
        kernel,
        name=name,
        out_shape=outs,
        in_specs=[ANY] * len(ins),
        out_specs=[ANY] * len(outs),
        scratch_shapes=[
            pltpu.SemaphoreType.DMA((copies,)),
            pltpu.SemaphoreType.DMA((copies,)),
            pltpu.SemaphoreType.DMA,
        ]
        + [pltpu.VMEM(shape, dtype) for shape, dtype in bounces],
        compiler_params=pltpu.CompilerParams(
            collective_id=collective_id, has_side_effects=True, vmem_limit_bytes=4 * MIB
        ),
    )(*ins)


RELAY_COPIES = 23


def relay_blocks(own, slot, mirrored, base, send_sems, recv_sems, settle, go_on):
    seq, chip, core, tp = place()
    at_x, at_y = chip // 2, chip % 2
    column = 3 - at_x if mirrored else at_x
    line = 1 - at_y if mirrored else at_y

    def real(x):
        return 3 - x if mirrored else x

    def block(source, item):
        row = 1 - at_y if item == 2 else at_y
        return slot(real(source) * 2 + row, item)

    def copy(number, source, target, x, y):
        return pltpu.make_async_remote_copy(
            src_ref=source,
            dst_ref=target,
            send_sem=send_sems.at[base + number],
            recv_sem=recv_sems.at[base + number],
            device_id=(x * 4 + y * 2 + core, tp),
            device_id_type=MESH,
        )

    paths = ((0, 1), (0, 3), (0, 2), (1, 2), (1, 3), (2, 3))
    hops = {}
    for at, (source, target) in enumerate(paths):
        relayed = (source, target) in ((0, 2), (1, 3))
        for item in range(3):
            there = block(source, item)
            here = there if relayed or item == 2 else own(item)
            hops[source, target, item] = copy(at * 3 + item, here, there, real(target), at_y)
    across_a = copy(18, own(0), slot(chip, 0), at_x, 1 - at_y)
    across_b = copy(19, own(1), slot(chip, 1), at_x, 1 - at_y)
    across = [
        copy(20 + source, block(source, 0), block(source, 0), at_x, 1 - at_y)
        for source in range(3)
    ]
    sends_b = (line == 0) | (column < 3)
    gets_b = (line == 1) | (column < 3)

    def begin(items):
        for at in range(3):

            @pl.when(column == at)
            def _():
                for item in items:
                    hops[at, at + 1, item].start()
                    if at == 0:
                        hops[0, 3, item].start()

    pl.when(line == 0)(across_a.start)
    begin((0,))
    settle()
    pl.when(sends_b)(across_b.start)
    begin((1,))
    go_on()

    def finish():
        finish_relay(
            column, line, sends_b, gets_b, begin, hops, across_a, across_b, across
        )

    return finish


def finish_relay(column, line, sends_b, gets_b, begin, hops, across_a, across_b, across):
    pl.when(gets_b)(across_b.wait_recv)
    begin((2,))

    @pl.when(column == 1)
    def _():
        for item in range(3):
            hops[0, 1, item].wait_recv()
            if item == 0:
                across[0].start()

    @pl.when(column == 2)
    def _():
        for item in range(3):
            hops[1, 2, item].wait_recv()
            hops[1, 3, item].start()
            if item == 0:
                across[1].start()
        for item in range(3):
            hops[0, 2, item].wait_recv()
            if item == 0:
                across[0].start()

    @pl.when(column == 3)
    def _():
        for item in range(3):
            hops[0, 3, item].wait_recv()
            hops[0, 2, item].start()
            if item == 0:
                across[0].start()
        for source in (2, 1):
            for item in range(3):
                hops[source, 3, item].wait_recv()
                if item == 0:
                    across[source].start()

    pl.when(line == 0)(across_a.wait_send)
    pl.when(line == 1)(across_a.wait_recv)
    pl.when(sends_b)(across_b.wait_send)
    sent = (((0, 1), (0, 3)), ((1, 2),), ((2, 3), (1, 3)), ((0, 2),))
    for at in range(4):

        @pl.when(column == at)
        def _():
            for source, target in sent[at]:
                for item in range(3):
                    hops[source, target, item].wait_send()
            for source in range(at):
                across[source].wait()


def first_part(core, rows):
    return pl.ds(pl.multiple_of(core * (FR2 - rows), 16), rows)


def rest_part(core, rows):
    return pl.ds(pl.multiple_of((1 - core) * rows, 16), FR2 - rows)


def near_peers(seq, chip, core, tp):
    x, y = chip // 2, chip % 2
    return [
        (lax.rem(x + 1, 4) * 4 + y * 2 + core, tp),
        (lax.rem(x + 3, 4) * 4 + y * 2 + core, tp),
        (x * 4 + (1 - y) * 2 + core, tp),
        (x * 4 + y * 2 + 1 - core, tp),
    ]


def tp_peers(seq, tp, order=TP_ORDER):
    return [(seq, lax.rem(tp + hop, TP)) for hop in order]


def chip_peers(chip, core, tp, order=CHIP_ORDER):
    return [(lax.rem(chip + hop, CHIPS) * 2 + core, tp) for hop in order]


def keys_kernel(
    kv, query, out_w, kv_all, query_two, w_half, send_sems, recv_sems, sem, kv_bounce, query_bounce, w_bounce
):
    seq, chip, core, tp = place()
    peers = near_peers(seq, chip, core, tp)
    partner = peers[-1]
    half = pl.ds(core * FR, FR)
    own = pl.ds(pl.multiple_of(core * FR, FR), FR)
    jobs = [(kv.at[1 - core], kv_all.at[chip, own], partner)]
    jobs.append((query.at[1 - core], query_two.at[core], partner))
    for other in tp_peers(seq, tp):
        peers.append(other)
        jobs.append((out_w.at[other[1], half], w_half.at[tp], other))

    def part(item):
        return rest_part(core, KEY_FIRST) if item else first_part(core, KEY_FIRST)

    inner = pl.ds(pl.multiple_of(core * (FR - KEY_FIRST), 16), KEY_FIRST)

    def relay(base, send_sems, recv_sems, settle, go_on):
        def settle_both():
            for source, target in ((kv.at[core], kv_bounce), (kv_bounce, kv_all.at[chip, own])):
                copy = pltpu.make_async_copy(source, target, sem)
                copy.start()
                copy.wait()
            settle()

        return relay_blocks(
            lambda item: kv_all.at[chip, part(1)] if item else kv.at[core, inner],
            lambda source, item: kv_all.at[source, part(1 if item else 0)],
            False,
            base,
            send_sems,
            recv_sems,
            settle_both,
            go_on,
        )

    run_exchange(
        peers,
        jobs,
        [
            (query.at[core], query_bounce, query_two.at[core], sem),
            (out_w.at[tp, half], w_bounce, w_half.at[tp], sem),
        ],
        send_sems,
        recv_sems,
        relay=relay,
        relay_after=1,
    )


def exchange_keys(kv, query, out_w):
    return exchange(
        keys_kernel,
        "exchange_keys",
        1,
        (kv, query, out_w),
        [
            jax.ShapeDtypeStruct((CHIPS, FR2, 2 * HD), BF16),
            jax.ShapeDtypeStruct((2, FR, HD), BF16),
            jax.ShapeDtypeStruct((TP, FR, 2 * HD), BF16),
        ],
        9 + RELAY_COPIES,
        [((FR, 2 * HD), BF16), ((FR, HD), BF16), ((FR, 2 * HD), BF16)],
    )


def attended_kernel(source, w_half, target, w_other, send_sems, recv_sems, sem, bounce):
    seq, chip, core, tp = place()
    slot = tp * 2 + core
    partner_seq = chip * 2 + 1 - core
    partner = (partner_seq, tp)
    peers = [partner] + tp_peers(seq, tp) + tp_peers(partner_seq, tp)
    own = pl.ds(core * FR, FR)
    other = pl.ds((1 - core) * FR, FR)
    rows = [other] + [own] * (TP - 1) + [other] * (TP - 1)
    jobs = [(source.at[part], target.at[slot], peer) for part, peer in zip(rows, peers)]
    jobs.append((w_half, w_other, partner))
    run_exchange(
        peers, jobs, [(source.at[own], bounce, target.at[slot], sem)], send_sems, recv_sems
    )


def exchange_attended(attended, w_half):
    return exchange(
        attended_kernel,
        "exchange_attended",
        2,
        (attended, w_half),
        [
            jax.ShapeDtypeStruct((2 * TP, FR, HD), BF16),
            jax.ShapeDtypeStruct(w_half.shape, BF16),
        ],
        16,
        [((FR, HD), BF16)],
    )


def latent_kernel(
    source, att_all, merged, target, att_other, merged_other, send_sems, recv_sems, sem, bounce
):
    seq, chip, core, tp = place()
    partner = (chip * 2 + 1 - core, tp)
    peers = tp_peers(seq, tp)
    jobs = [(source.at[peer[1]], target.at[tp], peer) for peer in peers]
    jobs.append((att_all, att_other, partner))
    jobs.append((merged, merged_other, partner))
    run_exchange(
        peers + [partner],
        jobs,
        [(source.at[tp], bounce, target.at[tp], sem)],
        send_sems,
        recv_sems,
    )


def exchange_latent(parts, att_all, merged):
    return exchange(
        latent_kernel,
        "exchange_latent",
        3,
        (parts, att_all, merged),
        [
            jax.ShapeDtypeStruct(parts.shape, parts.dtype),
            jax.ShapeDtypeStruct(att_all.shape, BF16),
            jax.ShapeDtypeStruct(merged.shape, BF16),
        ],
        9,
        [(parts.shape[1:], parts.dtype)],
    )


def message_kernel(source, grads, target, grads_other, send_sems, recv_sems, sem, bounce):
    seq, chip, core, tp = place()
    partner = (chip * 2 + 1 - core, tp)
    peers = tp_peers(seq, tp)
    jobs = [(source, target.at[core, tp], peer) for peer in peers]
    forwards = []
    for number, hop in enumerate(TP_ORDER):
        slot = target.at[core, lax.rem(tp - hop + TP, TP)]
        forwards.append((number, (slot, slot, partner)))
    jobs.append((source, target.at[core, tp], partner))
    jobs.append((grads.at[:, 1 - core], grads_other, partner))
    run_exchange(
        peers + [partner],
        jobs,
        [(source, bounce, target.at[core, tp], sem)],
        send_sems,
        recv_sems,
        forwards,
    )


def exchange_message(message, grads):
    return exchange(
        message_kernel,
        "exchange_message",
        4,
        (message, grads),
        [
            jax.ShapeDtypeStruct((2, TP) + message.shape, message.dtype),
            jax.ShapeDtypeStruct((CHIPS, TP) + grads.shape[3:], BF16),
        ],
        16,
        [(message.shape, message.dtype)],
    )


def cotangent_kernel(
    source, side, grads, target, side_x, grads_z, send_sems, recv_sems, sem, bounce, side_bounce, grads_bounce
):
    seq, chip, core, tp = place()
    partner_seq = chip * 2 + 1 - core
    at_x, at_y = chip // 2, chip % 2
    row, depth_at = tp // 4, tp % 4
    peers = [(partner_seq, tp)] + tp_peers(seq, tp) + tp_peers(partner_seq, tp)
    heads = [1 - core] + [core] * (TP - 1) + [1 - core] * (TP - 1)
    jobs = [
        (source.at[peer[1] * 2 + head], target.at[core, tp], peer)
        for head, peer in zip(heads, peers)
    ]
    for hop in (2, 1, 3):
        there = lax.rem(at_x + hop, 4)
        other = (there * 4 + at_y * 2 + core, tp)
        peers.append(other)
        jobs.append((side.at[there], side_x.at[at_x], other))
    early = pl.ds(0, Z_EARLY)
    for hop in (2, 1, 3):
        there = lax.rem(depth_at + hop, 4)
        other = (seq, row * 4 + there)
        jobs.append((grads.at[early, :, there], grads_z.at[depth_at], other))
    run_exchange(
        peers,
        jobs,
        [
            (source.at[tp * 2 + core], bounce, target.at[core, tp], sem),
            (side.at[at_x], side_bounce, side_x.at[at_x], sem),
            (grads.at[early, :, depth_at], grads_bounce, grads_z.at[depth_at], sem),
        ],
        send_sems,
        recv_sems,
    )


def exchange_cotangent(parts, side, grads):
    slab = (Z_EARLY, 2) + grads.shape[3:]
    return exchange(
        cotangent_kernel,
        "exchange_cotangent",
        5,
        (parts, side, grads),
        [
            jax.ShapeDtypeStruct((2, TP, FR, HD), BF16),
            jax.ShapeDtypeStruct(side.shape, BF16),
            jax.ShapeDtypeStruct((4,) + slab, BF16),
        ],
        21,
        [((FR, HD), BF16), (side.shape[1:], BF16), (slab, BF16)],
    )


def grads_kernel(
    pair, stats, grads, side, normed, pair_all, stats_all, grads_z, side_in, normed_other,
    send_sems, recv_sems, sem, bounce, stats_bounce, grads_bounce,
):
    seq, chip, core, tp = place()
    row, depth_at = tp // 4, tp % 4
    at_x, at_y = chip // 2, chip % 2
    peers = []
    jobs = []
    for hop in CHIP_ORDER:
        there = lax.rem(chip + hop, CHIPS)
        here = lax.rem(chip - hop + CHIPS, CHIPS)
        other = (there * 2 + core, tp)
        peers.append(other)
        jobs.append((stats, stats_all.at[chip], other, there < chip, here > chip))
    for hop in (2, 1, 3):
        there = lax.rem(depth_at + hop, 4)
        other = (seq, row * 4 + there)
        peers.append(other)
        jobs.append((grads.at[pl.ds(Z_EARLY, Z_LATE), :, there], grads_z.at[depth_at], other))
    jobs.append((side.at[1 - at_y], side_in, (at_x * 4 + (1 - at_y) * 2 + core, tp)))
    partner = (chip * 2 + 1 - core, tp)
    jobs.append((normed, normed_other, partner))
    peers.append(partner)

    def part(item):
        return rest_part(core, PAIR_FIRST) if item else first_part(core, PAIR_FIRST)

    def relay(*rest):
        return relay_blocks(
            lambda item: pair.at[part(item)],
            lambda source, item: pair_all.at[source, part(item)],
            True,
            *rest,
        )

    run_exchange(
        peers,
        jobs,
        [
            (pair, bounce, pair_all.at[chip], sem),
            (stats, stats_bounce, stats_all.at[chip], sem),
            (
                grads.at[pl.ds(Z_EARLY, Z_LATE), :, depth_at],
                grads_bounce,
                grads_z.at[depth_at],
                sem,
            ),
        ],
        send_sems,
        recv_sems,
        relay=relay,
    )


def exchange_grads(pair, stats, grads, side, normed):
    slab = (Z_LATE, 2) + grads.shape[3:]
    return exchange(
        grads_kernel,
        "exchange_grads",
        6,
        (pair, stats, grads, side, normed),
        [
            jax.ShapeDtypeStruct((CHIPS,) + pair.shape, BF16),
            jax.ShapeDtypeStruct((CHIPS,) + stats.shape, F32),
            jax.ShapeDtypeStruct((4,) + slab, BF16),
            jax.ShapeDtypeStruct(side.shape[1:], BF16),
            jax.ShapeDtypeStruct(normed.shape, BF16),
        ],
        12 + RELAY_COPIES,
        [(pair.shape, BF16), (stats.shape, F32), (slab, BF16)],
    )


def first_kernel(
    x_first, y_first, grads, out, x_in, y_in, grads_x, out_all,
    send_sems, recv_sems, sem, x_bounce, y_bounce, grads_bounce, out_bounce,
):
    seq, chip, core, tp = place()
    at_x, at_y = chip // 2, chip % 2

    def device(x, y, c):
        return x * 4 + y * 2 + c, tp

    peers = []
    jobs = []
    for hop in (2, 1, 3):
        x = lax.rem(at_x + hop, 4)
        for c in (core, 1 - core):
            peers.append(device(x, at_y, c))
            jobs.append((x_first.at[x, c], x_in.at[at_x, core], peers[-1]))
    for c in (core, 1 - core):
        peers.append(device(at_x, 1 - at_y, c))
        jobs.append((y_first.at[1 - at_y, c], y_in.at[at_y, core], peers[-1]))
    for hop in (2, 1, 3):
        x = lax.rem(at_x + hop, 4)
        jobs.append((grads.at[x], grads_x.at[at_x], device(x, at_y, core)))
    for other in tp_peers(seq, tp):
        peers.append(other)
        jobs.append((out.at[other[1]], out_all.at[tp], other))
    peers.append(device(at_x, at_y, 1 - core))
    jobs.append((x_first.at[at_x, 1 - core], x_in.at[at_x, core], peers[-1]))
    jobs.append((y_first.at[at_y, 1 - core], y_in.at[at_y, core], peers[-1]))
    run_exchange(
        peers,
        jobs,
        [
            (x_first.at[at_x, core], x_bounce, x_in.at[at_x, core], sem),
            (y_first.at[at_y, core], y_bounce, y_in.at[at_y, core], sem),
            (grads.at[at_x], grads_bounce, grads_x.at[at_x], sem),
            (out.at[tp], out_bounce, out_all.at[tp], sem),
        ],
        send_sems,
        recv_sems,
    )


def exchange_first(x_first, y_first, grads, out):
    arrays = (x_first, y_first, grads, out)
    tails = (x_first.shape[2:], y_first.shape[2:], grads.shape[1:], out.shape[1:])
    return exchange(
        first_kernel,
        "exchange_first",
        7,
        arrays,
        [jax.ShapeDtypeStruct(array.shape, BF16) for array in arrays],
        20,
        [(tail, BF16) for tail in tails],
    )


def second_kernel(
    x_sum, y_sum, grads, x_in, y_in, grads_in, send_sems, recv_sems, sem, y_bounce, grads_bounce
):
    seq, chip, core, tp = place()
    at_x, at_y = chip // 2, chip % 2
    row, depth_at = tp // 4, tp % 4
    peers = []
    jobs = []
    for hop in (2, 1, 3):
        x = lax.rem(at_x + hop, 4)
        peers.append((x * 4 + at_y * 2 + core, tp))
        jobs.append((y_sum.at[x], y_in.at[at_x], peers[-1]))
    peers.append((at_x * 4 + (1 - at_y) * 2 + core, tp))
    jobs.append((x_sum.at[1 - at_y], x_in, peers[-1]))
    jobs.append((grads.at[1 - at_y, row], grads_in.at[at_y, row], peers[-1]))
    for y in (at_y, 1 - at_y):
        peers.append((at_x * 4 + y * 2 + core, (1 - row) * 4 + depth_at))
        jobs.append((grads.at[y, 1 - row], grads_in.at[at_y, row], peers[-1]))
    run_exchange(
        peers,
        jobs,
        [
            (y_sum.at[at_x], y_bounce, y_in.at[at_x], sem),
            (grads.at[at_y, row], grads_bounce, grads_in.at[at_y, row], sem),
        ],
        send_sems,
        recv_sems,
    )


def exchange_second(x_sum, y_sum, grads):
    return exchange(
        second_kernel,
        "exchange_second",
        8,
        (x_sum, y_sum, grads),
        [
            jax.ShapeDtypeStruct(x_sum.shape[1:], BF16),
            jax.ShapeDtypeStruct(y_sum.shape, BF16),
            jax.ShapeDtypeStruct(grads.shape, BF16),
        ],
        7,
        [(y_sum.shape[1:], BF16), (grads.shape[2:], BF16)],
    )


def compute(kernel, name, ins, outs, scratch=(), limit=48, hbm=0):
    return pl.pallas_call(
        kernel,
        name=name,
        out_shape=outs,
        in_specs=[VMEM] * (len(ins) - hbm) + [HBM] * hbm,
        out_specs=[VMEM] * len(outs),
        scratch_shapes=list(scratch),
        compiler_params=pltpu.CompilerParams(vmem_limit_bytes=limit * MIB),
    )(*ins)


START_STEPS = 8


def start_kernel(
    hidden_ref, cos_ref, sin_ref, w_hbm, normed_ref, kv_ref, query_ref, out_w_ref, total_ref, w_ref, sems
):
    depth_rows = w_ref.shape[1]
    copies = [
        fetch(w_hbm.at[pl.ds(step * depth_rows, depth_rows)], w_ref.at[step], sems.at[step])
        for step in range(START_STEPS)
    ]
    hidden = hidden_ref[...].astype(F32)
    normed_ref[...] = (hidden * rms_scale(hidden)).astype(BF16)
    pieces = depth_rows // (TP * 32)
    for step in range(START_STEPS):
        copies[step].wait()
        weights = w_ref[step].reshape(depth_rows, 8 * HD)
        normed = normed_ref[:, step * depth_rows : (step + 1) * depth_rows]
        term = dot_nn(normed, weights[:, : 6 * HD])
        if step:
            total_ref[...] += term
        else:
            total_ref[...] = term
        out_w = weights[:, 6 * HD :].reshape(pieces, TP, 32, 2 * HD)
        for at in range(TP):
            for piece in range(pieces):
                low = (step * pieces + piece) * 32
                out_w_ref[at, low : low + 32] = out_w[piece, at]
    own = pl.ds(pl.multiple_of(lax.axis_index("seq") % 2 * FR, FR), FR)
    cosine, sine = cos_ref[own], sin_ref[own]

    def turned(at):
        lower = total_ref[:, at : at + HD // 2]
        upper = total_ref[:, at + HD // 2 : at + HD]
        return jnp.concatenate(
            [lower * cosine - upper * sine, upper * cosine + lower * sine], axis=1
        ).astype(BF16)

    for head in range(2):
        query_ref[head] = turned(head * HD)
        kv_ref[head, :, :HD] = turned((2 + head) * HD)
        at = (4 + head) * HD
        kv_ref[head, :, HD:] = total_ref[:, at : at + HD].astype(BF16)


def start(hidden, weights, cosine, sine):
    depth_rows = weights.shape[0] // START_STEPS
    return compute(
        start_kernel,
        "start",
        (hidden, cosine, sine, weights),
        [
            jax.ShapeDtypeStruct(hidden.shape, BF16),
            jax.ShapeDtypeStruct((2, FR, 2 * HD), BF16),
            jax.ShapeDtypeStruct((2, FR, HD), BF16),
            jax.ShapeDtypeStruct((TP, NS, 2 * HD), BF16),
        ],
        [
            pltpu.VMEM((FR, 6 * HD), F32),
            pltpu.VMEM((START_STEPS, depth_rows) + weights.shape[1:], BF16),
            pltpu.SemaphoreType.DMA((START_STEPS,)),
        ],
        hbm=1,
        limit=32,
    )


def attend_kernel(kv_ref, query_ref, out_ref, out_t_ref, level_ref, score_ref):
    chip = lax.axis_index("seq") // 2
    query = query_ref[...]
    key_at = lax.broadcasted_iota(jnp.int32, (FR2, FR2), 0)
    query_at = lax.broadcasted_iota(jnp.int32, (FR2, FR2), 1)

    def scores(block, top):
        score = dot_nt(kv_ref[block, :, :HD], query) * LOG_SCALE
        score_ref[block] = score
        return jnp.maximum(top, jnp.max(score, axis=0, keepdims=True))

    score = dot_nt(kv_ref[chip, :, :HD], query) * LOG_SCALE
    score = jnp.where(key_at <= query_at, score, MASKED)
    score_ref[chip] = score
    top = lax.fori_loop(0, chip, scores, jnp.max(score, axis=0, keepdims=True))

    def weigh(block, carry):
        total, mixed = carry
        prob = jnp.exp2(score_ref[block] - top)
        total = total + jnp.sum(prob, axis=0, keepdims=True)
        return total, mixed + dot_tn(kv_ref[block, :, HD:], prob.astype(BF16))

    total, mixed = lax.fori_loop(
        0, chip + 1, weigh, (jnp.zeros((1, FR2), F32), jnp.zeros((HD, FR2), F32))
    )
    mixed = mixed * (1.0 / total)
    out_t_ref[...] = mixed
    level_ref[...] = top + jnp.log2(total)
    out_ref[...] = mixed.T.astype(BF16)


def attend(kv_all, query):
    return compute(
        attend_kernel,
        "attend",
        (kv_all, query),
        [
            jax.ShapeDtypeStruct((FR2, HD), BF16),
            jax.ShapeDtypeStruct((HD, FR2), F32),
            jax.ShapeDtypeStruct((1, FR2), F32),
        ],
        [pltpu.VMEM((CHIPS, FR2, FR2), F32)],
        limit=20,
    )


def fetch(source, target, sem):
    copy = pltpu.make_async_copy(source, target, sem)
    copy.start()
    return copy


def order_halves(core, mine, other):
    return jnp.where(core == 0, mine, other), jnp.where(core == 0, other, mine)


def merge_kernel(
    att_ref, half_ref, other_ref, hidden_ref, depth_in_hbm, stack_hbm,
    merged_ref, round_ref, part_ref, stack_ref, depth_in_ref, sem, stack_sem,
):
    seq, chip, core, tp = place()
    copy = fetch(depth_in_hbm.at[:, tp], depth_in_ref, sem)
    stack_copy = fetch(stack_hbm, stack_ref, stack_sem)
    width = hidden_ref.shape[1]
    group = width // 2
    row_at = lax.broadcasted_iota(jnp.int32, (group, FR), 0)
    col_at = lax.broadcasted_iota(jnp.int32, (group, FR), 1)
    wanted = (col_at // 32) * 256 + tp * 32 + col_at % 32
    pick = jnp.where(row_at == wanted, 1.0, 0.0).astype(BF16)
    merged = jnp.concatenate(
        [dot_nn(hidden_ref[:, :group], pick), dot_nn(hidden_ref[:, group:], pick)], axis=1
    )
    mine = jnp.zeros((FR, FR), F32)
    other = jnp.zeros((FR, FR), F32)
    for at in range(TP):
        pair = jnp.concatenate([att_ref[2 * at], att_ref[2 * at + 1]], axis=1)
        mine = mine + dot_nt(pair, half_ref[at])
        other = other + dot_nt(pair, other_ref[at])
    merged = merged + jnp.concatenate(order_halves(core, mine, other), axis=1)
    rounded = merged.astype(BF16)
    merged_ref[...] = merged
    round_ref[...] = rounded
    squares = jnp.sum(merged * merged, axis=-1, keepdims=True)
    copy.wait()
    latent = dot_nn(rounded, depth_in_ref[...].reshape(NS, DD))
    coarse = squares.astype(BF16)
    fine = (squares - coarse.astype(F32)).astype(BF16)
    part_ref[:, :, :DD] = latent.astype(BF16).reshape(TP, FR // TP, DD)
    part_ref[:, :, DD : DD + HD] = jnp.broadcast_to(coarse, (FR, HD)).reshape(TP, FR // TP, HD)
    part_ref[:, :, DD + HD :] = jnp.broadcast_to(fine, (FR, HD)).reshape(TP, FR // TP, HD)
    stack_copy.wait()


def merge(att_all, w_half, w_other, hidden, depth_in, stack):
    return compute(
        merge_kernel,
        "merge",
        (att_all, w_half, w_other, hidden, depth_in, stack),
        [
            jax.ShapeDtypeStruct((FR, NS), F32),
            jax.ShapeDtypeStruct((FR, NS), BF16),
            jax.ShapeDtypeStruct((TP, FR // TP, DD + 2 * HD), BF16),
            jax.ShapeDtypeStruct(stack.shape, BF16),
        ],
        [
            pltpu.VMEM((2 * CHIPS, 32, DD), BF16),
            pltpu.SemaphoreType.DMA,
            pltpu.SemaphoreType.DMA,
        ],
        hbm=2,
        limit=24,
    )


def depth_kernel(
    width, loss_scale, part_ref, code_ref, stack_ref, message_ref, grad_ref, prob_ref
):
    books, frames = code_ref.shape
    grid = (frames, books, books)
    row_at = lax.broadcasted_iota(jnp.int32, grid, 1)
    col_at = lax.broadcasted_iota(jnp.int32, grid, 2)
    spread = jnp.broadcast_to(code_ref[...].astype(F32).T[:, None, :], grid)

    def column(wanted):
        picked = jnp.where(wanted, spread + 1.0, 0.0)
        picked = jnp.sum(picked, axis=-1, keepdims=True).reshape(frames * books, 1)
        return picked - 1.0

    codes = column(col_at == row_at)
    before = column(col_at == row_at - 1)
    tokens = frames * books
    total = jnp.sum(part_ref[...].astype(F32), axis=0)
    raw = total[:, :DD]
    squares = total[:, DD : DD + 1] + total[:, DD + HD : DD + HD + 1]
    scale_in = lax.rsqrt(squares * (1.0 / width) + EPSILON)
    latent = raw * scale_in
    latent = jnp.broadcast_to(latent[:, None, :], (frames, books, DD)).reshape(tokens, DD)
    vocab_at = lax.broadcasted_iota(jnp.int32, (tokens, VOCAB), 1).astype(F32)
    hot = jnp.where(before == vocab_at, 1.0, 0.0).astype(BF16)
    stream = latent + dot_nn(hot, stack_ref[4 * DD + VOCAB :])
    stream_scale = rms_scale(stream)
    stream_norm = (stream * stream_scale).astype(BF16)
    qkv_rows = stack_ref[: 3 * DD]
    proj = dot_nt(stream_norm, qkv_rows).astype(BF16)
    row_at = lax.broadcasted_iota(jnp.int32, (tokens, tokens), 0)
    col_at = lax.broadcasted_iota(jnp.int32, (tokens, tokens), 1)
    allowed = (row_at // books == col_at // books) & (col_at <= row_at)
    depth_scale = 1.0 / math.sqrt(DHD)
    mixed = []
    for head in range(DD // DHD):
        low = head * DHD
        queries = proj[:, low : low + DHD]
        keys = proj[:, DD + low : DD + low + DHD]
        values = proj[:, 2 * DD + low : 2 * DD + low + DHD]
        scores = jnp.where(allowed, dot_nt(queries, keys) * depth_scale, MASKED)
        weights = jnp.exp(scores - jnp.max(scores, axis=-1, keepdims=True))
        probs = weights * (1.0 / jnp.sum(weights, axis=-1, keepdims=True))
        prob_ref[head] = probs
        mixed.append(dot_nn(probs.astype(BF16), values))
    mixed = jnp.concatenate(mixed, axis=1).astype(BF16)
    out_rows = stack_ref[3 * DD : 4 * DD]
    resid = stream + dot_nt(mixed, out_rows)
    resid_scale = rms_scale(resid)
    resid_norm = (resid * resid_scale).astype(BF16)
    head_rows = stack_ref[4 * DD : 4 * DD + VOCAB]
    logits = dot_nt(resid_norm, head_rows)
    weights = jnp.exp(logits - jnp.max(logits, axis=-1, keepdims=True))
    logit_probs = weights * (1.0 / jnp.sum(weights, axis=-1, keepdims=True))
    target = jnp.where(codes == vocab_at, 1.0, 0.0)
    logit_grad = ((logit_probs - target) * loss_scale).astype(BF16)
    grad_ref[4 * DD : 4 * DD + VOCAB] = dot_tn(logit_grad, resid_norm).astype(BF16)
    resid_grad = norm_back(resid, resid_scale, dot_nn(logit_grad, head_rows))
    resid_round = resid_grad.astype(BF16)
    grad_ref[3 * DD : 4 * DD] = dot_tn(resid_round, mixed).astype(BF16)
    mixed_grad = dot_nn(resid_round, out_rows).astype(BF16)
    query_grad, key_grad, value_grad = [], [], []
    for head in range(DD // DHD):
        low = head * DHD
        queries = proj[:, low : low + DHD]
        keys = proj[:, DD + low : DD + low + DHD]
        values = proj[:, 2 * DD + low : 2 * DD + low + DHD]
        probs = prob_ref[head]
        mix_grad = mixed_grad[:, low : low + DHD]
        value_grad.append(dot_tn(probs.astype(BF16), mix_grad))
        prob_grad = dot_nt(mix_grad, values)
        inner = jnp.sum(probs * prob_grad, axis=-1, keepdims=True)
        score_grad = (probs * (prob_grad - inner) * depth_scale).astype(BF16)
        query_grad.append(dot_nn(score_grad, keys))
        key_grad.append(dot_tn(score_grad, queries))
    proj_grad = jnp.concatenate(query_grad + key_grad + value_grad, axis=1).astype(BF16)
    grad_ref[: 3 * DD] = dot_tn(proj_grad, stream_norm).astype(BF16)
    stream_grad = resid_grad + norm_back(stream, stream_scale, dot_nn(proj_grad, qkv_rows))
    grad_ref[4 * DD + VOCAB :] = dot_tn(hot, stream_grad.astype(BF16)).astype(BF16)
    latent_grad = jnp.sum(stream_grad.reshape(frames, books, DD), axis=1)
    latent_grad = latent_grad.astype(BF16).astype(F32)
    inner = jnp.sum(latent_grad * raw, axis=-1, keepdims=True) * (1.0 / width)
    pull = scale_in * scale_in * scale_in * inner
    coarse = pull.astype(BF16)
    fine = (pull - coarse.astype(F32)).astype(BF16)
    message_ref[:, :DD] = (latent_grad * scale_in).astype(BF16)
    message_ref[:, DD : DD + HD] = jnp.broadcast_to(coarse, (frames, HD))
    message_ref[:, DD + HD :] = jnp.broadcast_to(fine, (frames, HD))


def depth(parts, codes, stack, width, loss_scale):
    tokens = codes.shape[0] * codes.shape[1]
    return compute(
        functools.partial(depth_kernel, width, loss_scale),
        "depth",
        (parts, codes, stack),
        [
            jax.ShapeDtypeStruct((parts.shape[1], DD + 2 * HD), BF16),
            jax.ShapeDtypeStruct(stack.shape, BF16),
        ],
        [
            pltpu.VMEM((DD // DHD, tokens, tokens), F32),
        ],
        limit=32,
    )


def merged_gradient(message, merged, depth_in):
    pull = message[:, DD : DD + 1].astype(F32) + message[:, DD + HD : DD + HD + 1].astype(F32)
    return dot_nt(message[:, :DD], depth_in) - merged * pull


def unmerge_kernel(
    message_ref,
    merged_ref,
    round_ref,
    round_other_ref,
    att_ref,
    att_other_ref,
    half_ref,
    other_ref,
    grads_other_ref,
    grads_hbm,
    depth_in_hbm,
    part_ref,
    side_ref,
    grads_ref,
    depth_in_ref,
    grads_own_ref,
    sems,
):
    seq, chip, core, tp = place()
    copy = fetch(depth_in_hbm.at[:, tp], depth_in_ref, sems.at[0])
    grads_copy = fetch(grads_hbm.at[:, core], grads_own_ref, sems.at[1])
    copy.wait()
    depth_in = depth_in_ref[...].reshape(NS, DD)
    message = message_ref[core].reshape(FR, DD + 2 * HD)
    message_other = message_ref[1 - core].reshape(FR, DD + 2 * HD)
    gradient = merged_gradient(message, merged_ref[...], depth_in)
    lower, upper = gradient[:, :FR], gradient[:, FR:]
    mine, other = order_halves(core, lower, upper)
    mine, other = mine.astype(BF16), other.astype(BF16)
    for at in range(TP):
        pair = (dot_nn(mine, half_ref[at]) + dot_nn(other, other_ref[at])).astype(BF16)
        part_ref[2 * at] = pair[:, :HD]
        part_ref[2 * at + 1] = pair[:, HD:]
    gradient_other = merged_gradient(
        message_other, round_other_ref[...].astype(F32), depth_in
    )

    def pick_rows(own, others):
        both = jnp.concatenate([own.T, others.T], axis=1).reshape(CHIPS, 2, 32, FR2)
        both = jnp.where(core == 0, both[:, 0], both[:, 1])
        return both.reshape(FR, FR2).astype(BF16)

    rows = pick_rows(gradient, gradient_other)
    for at in range(TP):
        pair = jnp.concatenate([att_ref[2 * at], att_ref[2 * at + 1]], axis=1)
        pair_other = jnp.concatenate([att_other_ref[2 * at], att_other_ref[2 * at + 1]], axis=1)
        term = dot_nn(rows, jnp.concatenate([pair, pair_other], axis=0)).astype(BF16)
        side_ref[:, :, at * FR : (at + 1) * FR] = term.reshape(CHIPS, 32, FR)
    rows = pick_rows(round_ref[...].astype(F32), round_other_ref[...].astype(F32))
    both = jnp.concatenate([message[:, :DD], message_other[:, :DD]], axis=0)
    side_ref[:, :, TP * FR :] = dot_nn(rows, both).astype(BF16).reshape(CHIPS, 32, DD)
    grads_copy.wait()
    for at in range(CHIPS):
        grads_ref[at] = (
            grads_own_ref[at].astype(F32) + grads_other_ref[at].astype(F32)
        ).astype(BF16)


def unmerge(
    messages, merged, rounded, rounded_other, att_all, att_other, w_half, w_other, grads_other, grads, depth_in
):
    return compute(
        unmerge_kernel,
        "unmerge",
        (
            messages,
            merged,
            rounded,
            rounded_other,
            att_all,
            att_other,
            w_half,
            w_other,
            grads_other,
            grads,
            depth_in,
        ),
        [
            jax.ShapeDtypeStruct((2 * TP, FR, HD), BF16),
            jax.ShapeDtypeStruct((CHIPS, 32, TP * FR + DD), BF16),
            jax.ShapeDtypeStruct(grads_other.shape, BF16),
        ],
        [
            pltpu.VMEM((2 * CHIPS, 32, DD), BF16),
            pltpu.VMEM(grads_other.shape, BF16),
            pltpu.SemaphoreType.DMA((2,)),
        ],
        hbm=2,
        limit=28,
    )


def prepare_kernel(
    part_ref, query_ref, out_t_ref, level_ref, side_x_ref, pair_ref, stats_ref, side_ref
):
    gradient = jnp.sum(part_ref[...].astype(F32), axis=1).reshape(FR2, HD).astype(BF16)
    pair_ref[:, :HD] = query_ref[...]
    pair_ref[:, HD:] = gradient
    inner = jnp.sum(gradient.astype(F32).T * out_t_ref[...], axis=0, keepdims=True)
    stats_ref[...] = jnp.concatenate(
        [level_ref[...], inner, jnp.zeros((6, FR2), F32)], axis=0
    )
    side_ref[...] = jnp.sum(side_x_ref[...].astype(F32), axis=0).astype(BF16)


def prepare(parts, query, out_t, level, side_x):
    return compute(
        prepare_kernel,
        "prepare",
        (parts, query, out_t, level, side_x),
        [
            jax.ShapeDtypeStruct((FR2, 2 * HD), BF16),
            jax.ShapeDtypeStruct((8, FR2), F32),
            jax.ShapeDtypeStruct(side_x.shape[1:], BF16),
        ],
        limit=16,
    )


def attend_back_kernel(
    stats_ref, cos_ref, sin_ref, side_ref, side_in_ref, kv_hbm, pair_hbm, early_hbm, late_hbm,
    normed_hbm, other_hbm, x_ref, y_ref, grads_ref, win_ref, out_w_ref,
    kv_ref, pair_ref, early_ref, late_ref, normed_ref, other_ref, sems,
):
    chip = lax.axis_index("seq") // 2
    core = lax.axis_index("seq") % 2
    places = (
        (kv_hbm, kv_ref),
        (pair_hbm, pair_ref),
        (normed_hbm, normed_ref),
        (other_hbm, other_ref),
        (early_hbm, early_ref),
        (late_hbm, late_ref),
    )
    copies = [fetch(source, target, sems.at[at]) for at, (source, target) in enumerate(places)]
    copies[0].wait()
    copies[1].wait()
    scale = 1.0 / math.sqrt(HD)

    def pair(queries, keys, diagonal):
        query = pair_ref[queries, :, :HD]
        gradient = pair_ref[queries, :, HD:]
        score = dot_nt(kv_ref[keys, :, :HD], query) * LOG_SCALE
        if diagonal:
            key_at = lax.broadcasted_iota(jnp.int32, (FR2, FR2), 0)
            query_at = lax.broadcasted_iota(jnp.int32, (FR2, FR2), 1)
            score = jnp.where(key_at <= query_at, score, MASKED)
        prob = jnp.exp2(score - stats_ref[queries, 0:1])
        prob_grad = dot_nt(kv_ref[keys, :, HD:], gradient)
        score_grad = (prob * (prob_grad - stats_ref[queries, 1:2])).astype(BF16)
        return query, gradient, prob.astype(BF16), score_grad

    def own_queries(block, total):
        score_grad = pair(chip, block, False)[3]
        return total + dot_tn(kv_ref[block, :, :HD], score_grad)

    def own_keys(block, totals):
        query, gradient, prob, score_grad = pair(block, chip, False)
        return totals[0] + dot_nn(score_grad, query), totals[1] + dot_nn(prob, gradient)

    query, gradient, prob, score_grad = pair(chip, chip, True)
    query_grad = dot_tn(kv_ref[chip, :, :HD], score_grad)
    key_grad = dot_nn(score_grad, query)
    value_grad = dot_nn(prob, gradient)
    query_grad = lax.fori_loop(0, chip, own_queries, query_grad)
    key_grad, value_grad = lax.fori_loop(chip + 1, CHIPS, own_keys, (key_grad, value_grad))
    query_grad = query_grad.T
    cosine, sine = cos_ref[...] * scale, sin_ref[...] * scale

    def turned(total):
        lower, upper = total[:, : HD // 2], total[:, HD // 2 :]
        return [lower * cosine + upper * sine, upper * cosine - lower * sine]

    proj = jnp.concatenate(turned(query_grad) + turned(key_grad) + [value_grad], axis=1)
    proj_t = proj.T
    own, other = order_halves(core, proj_t[:, :FR], proj_t[:, FR:])
    own, other = own.astype(BF16), other.astype(BF16)
    copies[2].wait()
    copies[3].wait()
    for piece in range(2 * CHIPS):
        low = piece * FR
        term = dot_nn(own, normed_ref[:, low : low + FR])
        term = (term + dot_nn(other, other_ref[:, low : low + FR])).astype(BF16)
        x, y, c = piece // 4, piece // 2 % 2, piece % 2
        x_ref[x, c, y] = term[:X_ROWS]
        y_ref[y, c, x] = term[X_ROWS:]
    copies[4].wait()
    copies[5].wait()
    for at in range(CHIPS):
        term = early_ref[:, at] if at < Z_EARLY else late_ref[:, at - Z_EARLY]
        grads_ref[at] = jnp.sum(term.astype(F32), axis=0).astype(BF16)
    side = side_ref[chip % 2].astype(F32) + side_in_ref[...].astype(F32)
    win_ref[...] = side[:, TP * FR :]
    for at in range(TP):
        out_w_ref[at] = side[:, at * FR : (at + 1) * FR].astype(BF16)


def attend_back(
    stats_all, cosine, sine, side, side_in, kv_all, pair_all, early, late, normed, normed_other
):
    streamed = (kv_all, pair_all, early, late, normed, normed_other)
    return compute(
        attend_back_kernel,
        "attend_back",
        (stats_all, cosine, sine, side, side_in) + streamed,
        [
            jax.ShapeDtypeStruct((4, 2, 2, X_ROWS, FR), BF16),
            jax.ShapeDtypeStruct((2, 2, 4, Y_ROWS, FR), BF16),
            jax.ShapeDtypeStruct((CHIPS,) + late.shape[2:], BF16),
            jax.ShapeDtypeStruct((32, DD), F32),
            jax.ShapeDtypeStruct((TP, 32, FR), BF16),
        ],
        [pltpu.VMEM(array.shape, BF16) for array in streamed] + [pltpu.SemaphoreType.DMA((6,))],
        hbm=6,
        limit=36,
    )


def middle_kernel(x_ref, y_ref, grads_x_ref, x_sum_ref, y_sum_ref, grads_ref):
    for y in range(2):
        for c in range(2):
            terms = [x_ref[x, c, y].astype(F32) for x in range(4)]
            x_sum_ref[y, c] = (terms[0] + terms[1] + terms[2] + terms[3]).astype(BF16)
    for x in range(4):
        for c in range(2):
            term = y_ref[0, c, x].astype(F32) + y_ref[1, c, x].astype(F32)
            y_sum_ref[x, c] = term.astype(BF16)
    grads_ref[...] = jnp.sum(grads_x_ref[...].astype(F32), axis=0).astype(BF16)


def middle_sum(x_in, y_in, grads_x):
    return compute(
        middle_kernel,
        "middle_sum",
        (x_in, y_in, grads_x),
        [
            jax.ShapeDtypeStruct((2, 2, X_ROWS, FR), BF16),
            jax.ShapeDtypeStruct((4, 2, Y_ROWS, FR), BF16),
            jax.ShapeDtypeStruct(grads_x.shape[1:], BF16),
        ],
        limit=16,
    )


def last_kernel(x_own_ref, x_in_ref, y_in_ref, grads_ref, out_w_ref, out_ref, depth_ref):
    at_y = lax.axis_index("seq") // 2 % 2
    totals = []
    for head in range(2):
        x_part = x_own_ref[at_y, head].astype(F32) + x_in_ref[head].astype(F32)
        terms = [y_in_ref[x, head].astype(F32) for x in range(4)]
        y_part = terms[0] + terms[1] + terms[2] + terms[3]
        totals.append(jnp.concatenate([x_part, y_part], axis=0).T)
    pieces = [totals[head][:, kind * HD : (kind + 1) * HD] for kind in range(3) for head in range(2)]
    pieces.append(out_w_ref[...].astype(F32).reshape(FR, 2 * HD))
    out_ref[...] = jnp.concatenate(pieces, axis=1).reshape(FR, 4, 2 * HD)
    depth_ref[...] = jnp.sum(jnp.sum(grads_ref[...].astype(F32), axis=0), axis=0)


def last_sum(x_own, x_in, y_in, grads, out_all):
    return compute(
        last_kernel,
        "last_sum",
        (x_own, x_in, y_in, grads, out_all),
        [
            jax.ShapeDtypeStruct((FR, 4, 2 * HD), F32),
            jax.ShapeDtypeStruct(grads.shape[2:], F32),
        ],
        limit=16,
    )


def per_device(hidden_in, temporal_weight_stack, depth_in, depth_stack, audio_codes):
    seq_index = lax.axis_index("seq")
    tp_index = lax.axis_index("tp")
    chip = seq_index // 2
    width = hidden_in.shape[1]
    depth_frames, book_count = audio_codes.shape
    seq_count = 2 * CHIPS
    total_frames = FR * seq_count
    loss_scale = 1.0 / math.sqrt(total_frames * book_count)

    cosine, sine = angle_tables(chip * FR2, FR2)
    normed, kv, query, out_w = start(hidden_in, temporal_weight_stack, cosine, sine)
    kv_all, query, w_half = exchange_keys(kv, query, out_w)
    query = query.reshape(FR2, HD)

    depth_in = depth_in.reshape(seq_count, TP, -1, DD)
    attended, out_t, level = attend(kv_all, query)
    att_all, w_other = exchange_attended(attended, w_half)
    merged, rounded, latent_parts, depth_stack = merge(
        att_all, w_half, w_other, hidden_in, depth_in, depth_stack
    )
    latent_parts, att_other, rounded_other = exchange_latent(latent_parts, att_all, rounded)
    message, grads = depth(latent_parts, audio_codes.T, depth_stack, width, loss_scale)
    grads = grads.reshape(CHIPS, 2, TP, -1, DD)
    messages, grads_other = exchange_message(message, grads)
    cotangent_parts, side, grads = unmerge(
        messages,
        merged,
        rounded,
        rounded_other,
        att_all,
        att_other,
        w_half,
        w_other,
        grads_other,
        grads,
        depth_in,
    )
    grads = grads.reshape(CHIPS, 2, 4, -1, DD)
    cotangent_parts, side, early = exchange_cotangent(
        cotangent_parts, side.reshape(4, 2, 32, -1), grads
    )
    pair, stats, side = prepare(cotangent_parts, query, out_t, level, side)
    pair_all, stats_all, late, side_in, normed_other = exchange_grads(
        pair, stats, grads, side, normed
    )
    x_first, y_first, grads, grad_win, out_parts = attend_back(
        stats_all,
        cosine,
        sine,
        side,
        side_in,
        kv_all,
        pair_all,
        early,
        late,
        normed,
        normed_other,
    )
    x_in, y_in, grads, out_all = exchange_first(
        x_first, y_first, grads.reshape(4, 2, 2, -1, DD), out_parts
    )
    x_own, y_sum, grads = middle_sum(x_in, y_in, grads)
    x_in, y_in, grads = exchange_second(x_own, y_sum, grads)
    grad_temporal, grad_depth = last_sum(x_own, x_in, y_in, grads, out_all)
    return grad_temporal, grad_win, grad_depth


def solution(mesh):
    in_specs = (P("seq", None), P(None, None, "tp"), P(), P(), P(("seq", "tp"), None))
    out_specs = (P("seq", None, "tp"), P(("seq", "tp"), None), P(("seq", "tp"), None))
    return jax.shard_map(
        per_device, mesh=mesh, in_specs=in_specs, out_specs=out_specs, check_vma=False
    )
```
